128 devices in a mesh: dp: 16 (over z, x_hi, core), tensor: 8 (over y, x_lo).
Axes of the slice: x: 4 (x_hi: 2, x_lo: 2; x = x_hi * 2 + x_lo), y: 4, z: 4, core: 2. Of those that a mesh axis runs over, the one named last changes fastest.
Arguments:
- tokens: bfloat16 [16384, 1024], P(('dp', 'tensor')), may hold values from -6 to 6
- segment_ids: int32 [16, 1024], P('dp'), may hold values from 0 to 3, never falling along the last dimension, each value on 1 to 512 neighbouring positions
- first_gain: float32 [1024], replicated, may hold values from 0.5 to 1.5
- query_gain: float32 [128], replicated, may hold values from 0.5 to 1.5
- key_gain: float32 [128], replicated, may hold values from 0.5 to 1.5
- query_weight: bfloat16 [1024, 2048], P('dp', 'tensor'), may hold values from -0.1875 to 0.1875
- key_weight: bfloat16 [1024, 1024], P('dp', 'tensor'), may hold values from -0.1875 to 0.1875
- value_weight: bfloat16 [1024, 1024], P('dp', 'tensor'), may hold values from -0.1875 to 0.1875
- out_weight: bfloat16 [2048, 1024], P('tensor', 'dp'), may hold values from -0.5 to 0.5
- second_gain: float32 [1024], replicated, may hold values from 0.5 to 1.5
- gate_weight: bfloat16 [1024, 3072], P('dp', 'tensor'), may hold values from -0.1875 to 0.1875
- up_weight: bfloat16 [1024, 3072], P('dp', 'tensor'), may hold values from -0.1875 to 0.1875
- down_weight: bfloat16 [3072, 1024], P('tensor', 'dp'), may hold values from -0.109375 to 0.109375
- cotangent: bfloat16 [16384, 1024], P(('dp', 'tensor')), may hold values from -6 to 6
Outputs:
- layer_out: bfloat16 [16384, 1024], P(('dp', 'tensor'))
- grad_tokens: bfloat16 [16384, 1024], P(('dp', 'tensor'))
- grad_first_gain: float32 [1024], replicated
- grad_query_gain: float32 [128], replicated
- grad_key_gain: float32 [128], replicated
- grad_query: float32 [1024, 2048], P('dp', 'tensor')
- grad_key: float32 [1024, 1024], P('dp', 'tensor')
- grad_value: float32 [1024, 1024], P('dp', 'tensor')
- grad_out: float32 [2048, 1024], P('tensor', 'dp')
- grad_second_gain: float32 [1024], replicated
- grad_gate: float32 [1024, 3072], P('dp', 'tensor')
- grad_up: float32 [1024, 3072], P('dp', 'tensor')
- grad_down: float32 [3072, 1024], P('tensor', 'dp')
The draws below stay inside these ranges and needn't reach their ends.
Inputs may be any that keep to these rules, and one draw needn't show every extreme that they name: `segment_ids`: in each row, sequence numbers never fall and each sequence has 1 to 512 tokens; some sequence has exactly 512.
All inputs are finite; a program needn't handle non-finite values.
Results may differ from the reference program's by a relative error of at most 0.023.
Values may be sent and summed in bfloat16 or wider, within the bound.
No kernel may reach another device: no remote copies, remote signals or barrier semaphores. Data moves between devices by JAX's collectives and lax.ppermute only.
A program may use at most 128 MiB of HBM per device.

```python
import math
import jax
import jax.numpy as jnp
import numpy as np
from jax import lax

D = 1024
HEADS = 16
KV_HEADS = 8
HEAD_DIM = 128
FF = 3072
MAXLEN = 512
QBLOCK = 512
GROUP_TOK = 1024
GROUPS = 16
TOKENS = 16384
SEQS = 4


def level_of(rng, shape, pieces, least, top_value):
    def one(axis_at, blocks):
        heights = jax.random.uniform(jax.random.fold_in(jax.random.fold_in(rng, 6), axis_at), (blocks,), jnp.float32, least / len(pieces), top_value / len(pieces))
        return jnp.repeat(jnp.exp(heights), shape[axis_at] // blocks).reshape((-1,) + (1,) * (len(shape) - axis_at - 1))

    factor_of = one(*pieces[0])
    for cut in pieces[1:]:
        factor_of = factor_of * one(*cut)
    return factor_of


def profile(number_of, total, bound, skew):
    portions = [(1 << 20) // math.isqrt(rank ** skew) + 1 for rank in range(2, number_of + 1)]
    rest, given = total - bound - (number_of - 1), [1] * (number_of - 1)
    while rest > 0:
        movable = [i for i in range(number_of - 1) if given[i] < bound]
        whole, remaining = sum([portions[i] for i in movable]), rest
        for i in movable:
            addition = min(bound - given[i], max(1, remaining * portions[i] // whole), rest)
            given[i] = given[i] + addition
            rest = rest - addition
    return np.array([bound] + given)


def uneven_parts(own_key, number_of, total, bound, lean):
    if number_of == 2:
        one = jax.random.randint(own_key, (), max(1, total - bound), min(bound, total - 1) + 1)
        return jnp.stack([one, total - one])
    tallies = jnp.asarray(profile(number_of, total, bound, lean), jnp.int32)
    pairs = (number_of - 1) // 2
    donor, taker = tallies[1:1 + 2 * pairs:2], tallies[2:2 + 2 * pairs:2]
    margin = jnp.minimum(donor - 1, bound - taker)
    passed = jax.random.randint(jax.random.fold_in(own_key, 1), (pairs,), 0, 1 << 20) % (margin + 1)
    tallies = tallies.at[1:1 + 2 * pairs:2].set(donor - passed).at[2:2 + 2 * pairs:2].set(taker + passed)
    return tallies[jax.random.permutation(jax.random.fold_in(own_key, 2), number_of)]


def centred(stream_key, shape, scale, reach, shards=(), kind=jnp.bfloat16):
    values = scale * jax.random.normal(stream_key, shape, jnp.float32)
    if shards:
        values = values * level_of(stream_key, shape, shards, -0.22, 0.18)
    return jnp.clip(values, -reach, reach).astype(kind)


def setup_inputs(seed: int = 0) -> dict:
    arg_keys = jax.random.split(jax.random.key(seed), 15)
    tokens = centred(arg_keys[0], (TOKENS, D), 1.0, 6.0, ((0, 128),))
    segment_ids = jax.vmap(lambda own: jnp.searchsorted(jnp.cumsum(uneven_parts(own, SEQS, GROUP_TOK, MAXLEN, 2)), jnp.arange(GROUP_TOK), side="right"))(jax.random.split(arg_keys[1], GROUPS)).reshape((GROUPS, GROUP_TOK)).astype(jnp.int32)
    first_gain = jnp.clip(1.0 + 0.1 * jax.random.normal(arg_keys[2], (D,), jnp.float32), 0.5, 1.5)
    query_gain = jnp.clip(1.0 + 0.1 * jax.random.normal(arg_keys[3], (HEAD_DIM,), jnp.float32), 0.5, 1.5)
    key_gain = jnp.clip(1.0 + 0.1 * jax.random.normal(arg_keys[4], (HEAD_DIM,), jnp.float32), 0.5, 1.5)
    query_weight = centred(arg_keys[5], (D, HEADS * HEAD_DIM), D ** -0.5, 0.1875, ((0, 16), (1, 8)))
    key_weight = centred(arg_keys[6], (D, KV_HEADS * HEAD_DIM), D ** -0.5, 0.1875, ((0, 16), (1, 8)))
    value_weight = centred(arg_keys[7], (D, KV_HEADS * HEAD_DIM), D ** -0.5, 0.1875, ((0, 16), (1, 8)))
    out_weight = centred(arg_keys[8], (HEADS * HEAD_DIM, D), (HEADS * HEAD_DIM // 16) ** -0.5, 0.5, ((0, 8), (1, 16)))
    second_gain = jnp.clip(1.0 + 0.1 * jax.random.normal(arg_keys[9], (D,), jnp.float32), 0.5, 1.5)
    gate_weight = centred(arg_keys[10], (D, FF), D ** -0.5, 0.1875, ((0, 16), (1, 8)))
    up_weight = centred(arg_keys[11], (D, FF), D ** -0.5, 0.1875, ((0, 16), (1, 8)))
    down_weight = centred(arg_keys[12], (FF, D), FF ** -0.5, 0.109375, ((0, 8), (1, 16)))
    cotangent = centred(arg_keys[13], (TOKENS, D), 1.0, 6.0, ((0, 128),))
    return dict(tokens=tokens, segment_ids=segment_ids, first_gain=first_gain, query_gain=query_gain, key_gain=key_gain, query_weight=query_weight, key_weight=key_weight, value_weight=value_weight, out_weight=out_weight, second_gain=second_gain, gate_weight=gate_weight, up_weight=up_weight, down_weight=down_weight, cotangent=cotangent)


EPSILON = 1e-06
ROPE_BASE = 1000000.0
NEG_LARGE = -1e+30

@jax.custom_vjp
def low(v):
    return lax.optimization_barrier(v.astype(jnp.bfloat16)).astype(jnp.float32)

@jax.custom_vjp
def low_back(v):
    return v

def low_keep(v):
    return (low(v), None)

def low_pass(kept, grad):
    return (grad,)

def back_keep(v):
    return (v, None)

def back_low(kept, grad):
    return (low(grad),)
low.defvjp(low_keep, low_pass)
low_back.defvjp(back_keep, back_low)

def norm_scale(values, weight_gain):
    return values * lax.rsqrt(lax.optimization_barrier(jnp.mean(values * values, -1, keepdims=True)) + EPSILON) * weight_gain

def rotate(values, cosine, sine):
    half_dim = values.shape[-1] // 2
    turned = jnp.concatenate([-values[..., half_dim:], values[..., :half_dim]], -1)
    return values * cosine + turned * sine

def positions_of(seg_row):
    length = seg_row.shape[0]
    indices = jnp.arange(length, dtype=jnp.int32)
    change = jnp.concatenate([jnp.ones((1,), jnp.bool_), seg_row[1:] != seg_row[:-1]])
    starts = lax.cummax(jnp.where(change, indices, 0), axis=0)
    return indices - starts

def angles_of(seg_row, head_size):
    places = positions_of(seg_row).astype(jnp.float32)
    inverse = ROPE_BASE ** (-jnp.arange(0, head_size, 2, dtype=jnp.float32) / head_size)
    phases = places[:, None] * inverse[None, :]
    phases = jnp.concatenate([phases, phases], -1)[:, None, :]
    return (jnp.cos(phases), jnp.sin(phases))

def head_prep(projected, head_gain, cosine, sine, head_count):
    shaped = projected.reshape(projected.shape[0], head_count, -1)
    return rotate(norm_scale(shaped, head_gain), cosine, sine)

def mask_of(seg_row, seg_padded, start_row, block_rows):
    seg_query = lax.dynamic_slice_in_dim(seg_row, start_row, block_rows, 0)
    seg_key = lax.dynamic_slice_in_dim(seg_padded, start_row, 2 * block_rows, 0)
    query_index = start_row + jnp.arange(block_rows, dtype=jnp.int32)
    key_index = start_row - block_rows + jnp.arange(2 * block_rows, dtype=jnp.int32)
    return (seg_query[:, None] == seg_key[None, :]) & (key_index[None, :] <= query_index[:, None])

def dense(left_side, right_side):
    return jnp.dot(left_side, right_side, precision=lax.Precision.HIGHEST)

def reference(tokens, segment_ids, first_gain, query_gain, key_gain, query_weight, key_weight, value_weight, out_weight, second_gain, gate_weight, up_weight, down_weight, cotangent):
    token_count = TOKENS
    seg_offset = (jnp.arange(GROUPS, dtype=jnp.int32) * SEQS)[:, None]
    seg_row = (segment_ids + seg_offset).reshape(token_count)
    cosine, sine = angles_of(seg_row, HEAD_DIM)
    group_size = HEADS // KV_HEADS
    score_scale = HEAD_DIM ** (-0.5)
    block_count = token_count // QBLOCK
    seg_padded = jnp.concatenate([jnp.full((QBLOCK,), -1, jnp.int32), seg_row])

    def forward(input_float, gain_one, gain_query, gain_key, query_mat, key_mat, value_mat, out_mat, gain_two, gate_mat, up_mat, down_mat):
        normed_one = low(norm_scale(input_float, gain_one))
        query_raw = low_back(dense(normed_one, query_mat))
        key_raw = low_back(dense(normed_one, key_mat))
        value_raw = low_back(dense(normed_one, value_mat))
        queries = low(head_prep(query_raw, gain_query, cosine, sine, HEADS)).reshape(token_count, KV_HEADS, group_size, HEAD_DIM)
        keys_all = low(head_prep(key_raw, gain_key, cosine, sine, KV_HEADS))
        values_all = low(value_raw).reshape(token_count, KV_HEADS, HEAD_DIM)
        zero_rows = jnp.zeros((QBLOCK, KV_HEADS, HEAD_DIM), jnp.float32)
        key_padded = jnp.concatenate([zero_rows, keys_all], 0)
        value_padded = jnp.concatenate([zero_rows, values_all], 0)

        def attend_block(block_index):
            start_row = block_index * QBLOCK
            query_block = lax.dynamic_slice_in_dim(queries, start_row, QBLOCK, 0)
            key_block = lax.dynamic_slice_in_dim(key_padded, start_row, 2 * QBLOCK, 0)
            value_block = lax.dynamic_slice_in_dim(value_padded, start_row, 2 * QBLOCK, 0)
            allowed = mask_of(seg_row, seg_padded, start_row, QBLOCK)
            scores = low_back(jnp.einsum('qhgd,khd->hgqk', query_block, key_block, precision=lax.Precision.HIGHEST) * score_scale)
            masked = jnp.where(allowed, scores, NEG_LARGE)
            row_max = lax.optimization_barrier(jnp.max(masked, -1, keepdims=True))
            exponent = jnp.exp(masked - row_max)
            attn_prob = low(exponent / lax.optimization_barrier(jnp.sum(exponent, -1, keepdims=True)))
            return jnp.einsum('hgqk,khd->qhgd', attn_prob, value_block, precision=lax.Precision.HIGHEST)
        head_blocks = lax.map(jax.checkpoint(attend_block), jnp.arange(block_count, dtype=jnp.int32))
        attended = low(low_back(head_blocks.reshape(token_count, HEADS * HEAD_DIM)))
        hidden_state = input_float + low_back(dense(attended, out_mat))
        normed_two = low(norm_scale(hidden_state, gain_two))
        gate_value = low_back(dense(normed_two, gate_mat))
        up_value = low_back(dense(normed_two, up_mat))
        activated = low(jax.nn.silu(gate_value) * up_value)
        return hidden_state + low_back(dense(activated, down_mat))
    result, back_fn = jax.vjp(forward, tokens.astype(jnp.float32), first_gain, query_gain, key_gain, query_weight.astype(jnp.float32), key_weight.astype(jnp.float32), value_weight.astype(jnp.float32), out_weight.astype(jnp.float32), second_gain, gate_weight.astype(jnp.float32), up_weight.astype(jnp.float32), down_weight.astype(jnp.float32))
    grads = back_fn(cotangent.astype(jnp.float32))
    return (result.astype(jnp.bfloat16), grads[0].astype(jnp.bfloat16), grads[1], grads[2], grads[3], grads[4], grads[5], grads[6], grads[7], grads[8], grads[9], grads[10], grads[11])
```

```python
import jax
import jax.numpy as jnp
import numpy as np
from jax import lax
from jax.sharding import Mesh
from jax.sharding import PartitionSpec as P

EPSILON = 1e-06
ROPE_BASE = 1000000.0
NEG_LARGE = -1e30
BF16 = jnp.bfloat16
F32 = jnp.float32

SIZES = {"z": 4, "h": 2, "c": 2, "y": 4, "l": 2}
DP_RINGS = (("h", "l"), ("z",))


def ring_size(axes):
    return int(np.prod([SIZES[a] for a in axes]))


def fetch(value, axes, step):
    n = ring_size(axes)
    return lax.ppermute(value, axes, [(i, (i - step) % n) for i in range(n)])


def send(value, axes, step):
    n = ring_size(axes)
    return lax.ppermute(value, axes, [(i, (i + step) % n) for i in range(n)])


def core_swap(value):
    return lax.ppermute(value, ("c",), [(0, 1), (1, 0)])


def remap(value):
    pairs = []
    for c in range(2):
        for y in range(4):
            for l in range(2):
                pairs.append(((c * 4 + y) * 2 + l, (l * 4 + y) * 2 + c))
    return lax.ppermute(value, ("c", "y", "l"), pairs)


def dot_nn(a, b):
    return lax.dot_general(a, b, (((1,), (0,)), ((), ())), preferred_element_type=F32)


def dot_nt(a, b):
    return lax.dot_general(a, b, (((1,), (1,)), ((), ())), preferred_element_type=F32)


def dot_tn(a, b):
    return lax.dot_general(a, b, (((0,), (0,)), ((), ())), preferred_element_type=F32)


def gather_tokens(block):
    parts = []
    for s in range(4):
        piece = block if s == 0 else fetch(block, ("y",), s)
        parts += [piece, core_swap(piece)]
    return jnp.concatenate(parts, 0)


def scatter_tokens(partial):
    width = partial.shape[-1]
    blocks = partial.reshape(4, 2, 128, width)
    other = core_swap(blocks[:, 1].astype(BF16))
    mine = blocks[:, 0] + other.astype(F32)
    low = mine.astype(BF16)
    total = mine[0]
    for s in range(1, 4):
        total = total + send(low[s], ("y",), s).astype(F32)
    return total


def rolled(values, axis, amount):
    n = values.shape[axis]
    twice = jnp.concatenate([values, values], axis)
    return lax.dynamic_slice_in_dim(twice, amount, n, axis)


def gather_weights(shard, z, x):
    stage = jnp.stack([shard] + [fetch(shard, ("h", "l"), s) for s in range(1, 4)])
    full = jnp.stack([stage] + [fetch(stage, ("z",), s) for s in range(1, 4)])
    full = rolled(rolled(full, 0, (4 - z) % 4), 1, (4 - x) % 4)
    return full.reshape(1024, shard.shape[1])


def scatter_weights(grad, z, x):
    width = grad.shape[1]
    low = grad.astype(BF16).reshape(4, 4, 64, width)
    low = rolled(rolled(low, 0, z), 1, x)
    total = low[:, 0].astype(F32)
    for s in range(1, 4):
        total = total + send(low[:, s], ("h", "l"), s).astype(F32)
    low = total.astype(BF16)
    result = total[0]
    for s in range(1, 4):
        result = result + send(low[s], ("z",), s).astype(F32)
    return remap(result.astype(BF16)).astype(F32)


def all_sum(values):
    values = values + core_swap(values)
    for axes in (("y",), ("h", "l"), ("z",)):
        got = [send(values, axes, s) for s in range(1, 4)]
        values = (values + got[1]) + (got[0] + got[2])
    return values


def turned(values):
    half = values.shape[-1] // 2
    return jnp.concatenate([-values[..., half:], values[..., :half]], -1)


def norm_forward(values):
    scale = lax.rsqrt(jnp.mean(values * values, -1, keepdims=True) + EPSILON)
    return values * scale, scale


def norm_backward(unit, scale, gain, grad):
    weighted = grad * gain
    return scale * (weighted - unit * jnp.mean(unit * weighted, -1, keepdims=True))


def per_device(
    tokens,
    segment_ids,
    first_gain,
    query_gain,
    key_gain,
    query_weight,
    key_weight,
    value_weight,
    out_weight,
    second_gain,
    gate_weight,
    up_weight,
    down_weight,
    cotangent,
):
    z = lax.axis_index("z")
    x = lax.axis_index("h") * 2 + lax.axis_index("l")
    y = lax.axis_index("y")
    c = lax.axis_index("c")
    tokens = remap(tokens)
    attn_shard = remap(jnp.concatenate([query_weight, key_weight, value_weight], 1))
    seg_row = remap(segment_ids)[0]
    mlp_shard = remap(jnp.concatenate([out_weight.T, gate_weight, up_weight, down_weight.T], 1))
    cotangent = remap(cotangent)

    slot = jnp.arange(8, dtype=jnp.int32)
    block_of = ((y + slot // 2) % 4) * 2 + (slot % 2 + c) % 2
    index = (block_of[:, None] * 128 + jnp.arange(128, dtype=jnp.int32)[None, :]).reshape(1024)
    seg4 = rolled(seg_row.reshape(4, 2, 128), 0, y)
    seg4 = rolled(seg4, 1, c)
    seg = seg4.reshape(1024)
    start = jnp.zeros((1024,), jnp.int32)
    for v in range(1, 4):
        start = start + jnp.where(seg == v, jnp.sum((seg_row < v).astype(jnp.int32)), 0)
    places = (index - start).astype(F32)
    inverse = ROPE_BASE ** (-jnp.arange(0, 128, 2, dtype=F32) / 128)
    phases = places[:, None] * inverse[None, :]
    phases = jnp.concatenate([phases, phases], -1)
    cosine, sine = jnp.cos(phases), jnp.sin(phases)
    allowed = (seg[:, None] == seg[None, :]) & (index[None, :] <= index[:, None])

    input_float = tokens.astype(F32)
    unit_one, scale_one = norm_forward(input_float)
    normed_one = gather_tokens((unit_one * first_gain).astype(BF16))
    attn_full = gather_weights(attn_shard, z, x)
    mlp_full = gather_weights(mlp_shard, z, x)
    cot_all = gather_tokens(cotangent)
    raw = dot_nn(normed_one, attn_full)
    heads = [raw[:, i * 128 : (i + 1) * 128] for i in range(4)]
    gains = [query_gain, query_gain, key_gain]
    units, scales, rots = [], [], []
    for i in range(3):
        unit, scale = norm_forward(heads[i])
        scaled = unit * gains[i]
        units.append(unit)
        scales.append(scale)
        rots.append((scaled * cosine + turned(scaled) * sine).astype(BF16))
    key, value = rots[2], heads[3].astype(BF16)
    score_scale = 128 ** (-0.5)
    outs, logs = [], []
    for i in range(2):
        scores = jnp.where(allowed, dot_nt(rots[i], key) * score_scale, NEG_LARGE)
        top = jnp.max(scores, -1, keepdims=True)
        exponent = jnp.exp(scores - top)
        total = jnp.sum(exponent, -1, keepdims=True)
        prob = (exponent / total).astype(BF16)
        outs.append(dot_nn(prob, value).astype(BF16))
        logs.append(top + jnp.log(total))
    attended = jnp.concatenate(outs, 1)
    out_t = mlp_full[:, :256]
    gate_up = mlp_full[:, 256:1024]
    down_t = mlp_full[:, 1024:]
    hidden = input_float + scatter_tokens(dot_nt(attended, out_t))

    unit_two, scale_two = norm_forward(hidden)
    normed_two = gather_tokens((unit_two * second_gain).astype(BF16))
    gate_up_value = dot_nn(normed_two, gate_up)
    gate, up = gate_up_value[:, :384], gate_up_value[:, 384:]
    sig = jax.nn.sigmoid(gate)
    silu = gate * sig
    act = (silu * up).astype(BF16)
    grad_act = dot_nn(cot_all, down_t)
    grad_gate = (grad_act * up * (sig + silu * (1.0 - sig))).astype(BF16)
    grad_up = (grad_act * silu).astype(BF16)
    grad_gu = jnp.concatenate([grad_gate, grad_up], 1)
    partial_two = dot_nt(grad_gu, gate_up)
    grad_normed_two = scatter_tokens(partial_two)
    layer_out = remap((hidden + scatter_tokens(dot_nt(act, down_t))).astype(BF16))
    second_part = jnp.sum(partial_two * normed_two.astype(F32), 0) / second_gain
    mlp_grad = jnp.concatenate([dot_tn(normed_two, grad_gu), dot_tn(cot_all, act)], 1)
    mlp_owned = scatter_weights(mlp_grad, z, x)

    grad_hidden = cotangent.astype(F32) + norm_backward(
        unit_two, scale_two, second_gain, grad_normed_two
    )
    hidden_grad = gather_tokens(grad_hidden.astype(BF16))
    grad_attended = dot_nn(hidden_grad, out_t).astype(BF16)
    out_owned = scatter_weights(dot_tn(hidden_grad, attended), z, x)
    grad_key = jnp.zeros((1024, 128), F32)
    grad_value = jnp.zeros((1024, 128), F32)
    grad_rot = []
    for i in range(2):
        scores = dot_nt(rots[i], key) * score_scale
        prob = jnp.where(allowed, jnp.exp(scores - logs[i]), 0.0)
        grad_out = grad_attended[:, i * 128 : (i + 1) * 128]
        grad_prob = dot_nt(grad_out, value)
        inner = jnp.sum(prob * grad_prob, -1, keepdims=True)
        grad_scores = (prob * (grad_prob - inner)).astype(BF16)
        grad_rot.append(dot_nn(grad_scores, key) * score_scale)
        grad_key = grad_key + dot_tn(grad_scores, rots[i]) * score_scale
        grad_value = grad_value + dot_tn(prob.astype(BF16), grad_out)
    grad_rot.append(grad_key)
    grad_raw, gain_parts = [], []
    for i in range(3):
        grad = grad_rot[i] * cosine - turned(grad_rot[i]) * sine
        gain_parts.append(jnp.sum(grad * units[i], 0))
        grad_raw.append(norm_backward(units[i], scales[i], gains[i], grad).astype(BF16))
    grad_raw = jnp.concatenate(grad_raw + [grad_value.astype(BF16)], 1)
    partial_one = dot_nt(grad_raw, attn_full)
    grad_normed_one = scatter_tokens(partial_one)
    first_part = jnp.sum(partial_one * normed_one.astype(F32), 0) / first_gain
    attn_owned = scatter_weights(dot_tn(normed_one, grad_raw), z, x)
    sums = all_sum(
        jnp.concatenate([first_part, second_part, gain_parts[0] + gain_parts[1], gain_parts[2]])
    )
    grad_tokens = grad_hidden + norm_backward(unit_one, scale_one, first_gain, grad_normed_one)
    grad_tokens = remap(grad_tokens.astype(BF16))
    return (
        layer_out,
        grad_tokens,
        sums[:1024],
        sums[2048:2176],
        sums[2176:],
        attn_owned[:, :256],
        attn_owned[:, 256:384],
        attn_owned[:, 384:],
        out_owned.T,
        sums[1024:2048],
        mlp_owned[:, :384],
        mlp_owned[:, 384:768],
        mlp_owned[:, 768:].T,
    )


def solution(mesh):
    fine = Mesh(mesh.devices.reshape(4, 2, 2, 4, 2), ("z", "h", "c", "y", "l"))
    dp, tensor = ("z", "h", "c"), ("y", "l")
    rows, cols, trans = P(dp + tensor, None), P(dp, tensor), P(tensor, dp)
    in_specs = (
        rows, P(dp, None), P(), P(), P(), cols, cols, cols, trans, P(), cols, cols, trans, rows,
    )
    out_specs = (rows, rows, P(), P(), P(), cols, cols, cols, trans, P(), cols, cols, trans)
    return jax.shard_map(
        per_device, mesh=fine, in_specs=in_specs, out_specs=out_specs, check_vma=False
    )
```

```python
import jax
import jax.numpy as jnp
from jax import lax
from jax.experimental import pallas as pl
from jax.experimental.pallas import tpu as pltpu
from jax.sharding import Mesh
from jax.sharding import PartitionSpec as P

EPSILON = 1e-06
ROPE_BASE = 1000000.0
NEG_LARGE = -1e30
BF16 = jnp.bfloat16
F32 = jnp.float32
SQUARE = ((0, 0), (0, 1), (1, 0), (1, 1))


def place_of(y, pair):
    return y if y // 2 == pair else 3 - y


def remap_pairs():
    pairs = []
    for c in range(2):
        for y in range(4):
            for l in range(2):
                pairs.append(((c * 4 + y) * 2 + l, ((y % 2) * 4 + place_of(y, c)) * 2 + l))
    return pairs


def remap(value):
    return lax.ppermute(value, ("c", "y", "l"), remap_pairs())


def remap_back(value):
    return lax.ppermute(value, ("c", "y", "l"), [(b, a) for a, b in remap_pairs()])


def shard_pairs(a, b):
    pairs = []
    for h in range(2):
        for c in range(2):
            for y in range(4):
                for l in range(2):
                    source = ((h * 2 + c) * 4 + y) * 2 + l
                    pairs.append((source, (((h ^ a) * 2 + y % 2) * 4 + place_of(y, c ^ b)) * 2 + l))
    return pairs


def shard_out(value, a, b):
    return lax.ppermute(value, ("h", "c", "y", "l"), shard_pairs(a, b))


def shard_home(value, a, b):
    return lax.ppermute(value, ("h", "c", "y", "l"), [(t, s) for s, t in shard_pairs(a, b)])


def ring(value, axis, step):
    return lax.ppermute(value, (axis,), [(i, (i + step) % 4) for i in range(4)])


def core_swap(value):
    return lax.ppermute(value, ("c",), [(0, 1), (1, 0)])


def across(value, i, j):
    if (i, j) == (0, 0):
        return value
    pairs = [(y * 2 + l, (y ^ i) * 2 + (l ^ j)) for y in range(4) for l in range(2)]
    return lax.ppermute(value, ("y", "l"), pairs)


def dot_nn(a, b):
    return lax.dot_general(a, b, (((1,), (0,)), ((), ())), preferred_element_type=F32)


def dot_nt(a, b):
    return lax.dot_general(a, b, (((1,), (1,)), ((), ())), preferred_element_type=F32)


def dot_tn(a, b):
    return lax.dot_general(a, b, (((0,), (0,)), ((), ())), preferred_element_type=F32)


def gather_tokens(block):
    return jnp.concatenate([across(block, i, j) for i, j in SQUARE], 0)


def scatter_tokens(partial):
    total = partial[:128]
    for s in (1, 2, 3):
        total = total + across(partial[s * 128 : (s + 1) * 128].astype(BF16), *SQUARE[s]).astype(F32)
    return total


def place_kernel(where, *refs):
    out = refs[-1]
    for s in range(4):
        for k in range(4):
            at = ((where[0] + s) % 4) * 4 + (where[1] ^ k)
            out[pl.ds(pl.multiple_of(at * 64, 64), 64), :] = refs[s][k]


def pick_kernel(where, grad, *outs):
    for s in range(4):
        for k in range(4):
            at = ((where[0] + s) % 4) * 4 + (where[1] ^ k)
            outs[s][k] = grad[pl.ds(pl.multiple_of(at * 64, 64), 64), :].astype(outs[s].dtype)


def vmem(n):
    return [pl.BlockSpec(memory_space=pltpu.VMEM)] * n


SMEM = pl.BlockSpec(memory_space=pltpu.SMEM)
PARAMS = pltpu.CompilerParams(vmem_limit_bytes=48 * 1024 * 1024)


def gather_weights(shard, where):
    width = shard.shape[1]
    stage = jnp.stack([shard_out(shard, a, b) for a, b in SQUARE])
    parts = [stage] + [ring(stage, "z", -s) for s in (1, 2, 3)]
    return pl.pallas_call(
        place_kernel,
        out_shape=jax.ShapeDtypeStruct((1024, width), BF16),
        in_specs=[SMEM] + vmem(4),
        out_specs=vmem(1)[0],
        compiler_params=PARAMS,
    )(where, *parts)


def scatter_weights(own, other, where):
    width = own.shape[1]
    total = own + core_swap(other.astype(BF16)).astype(F32)
    parts = pl.pallas_call(
        pick_kernel,
        out_shape=[jax.ShapeDtypeStruct((4, 64, width), BF16)] * 4,
        in_specs=[SMEM] + vmem(1),
        out_specs=vmem(4),
        compiler_params=PARAMS,
    )(where, total.astype(BF16))
    total = parts[0].astype(F32)
    for s in (1, 2, 3):
        total = total + ring(parts[s], "z", s).astype(F32)
    low = total.astype(BF16)
    result = 0.0
    for k in range(4):
        result = result + shard_home(low[k], *SQUARE[k]).astype(F32)
    return result


def all_sum(values):
    values = values + core_swap(values)
    got = [across(values, i, j) for i, j in SQUARE]
    values = (got[0] + got[1]) + (got[2] + got[3])
    pairs = [(y, 3 - y) for y in range(4)]
    values = values + lax.ppermute(values, ("y",), pairs)
    values = values + lax.ppermute(values, ("h",), [(0, 1), (1, 0)])
    got = [ring(values, "z", s) for s in (1, 2, 3)]
    return (values + got[1]) + (got[0] + got[2])


def turned(values):
    half = values.shape[-1] // 2
    return jnp.concatenate([-values[..., half:], values[..., :half]], -1)


def norm_forward(values):
    scale = lax.rsqrt(jnp.mean(values * values, -1, keepdims=True) + EPSILON)
    return values * scale, scale


def norm_backward(unit, scale, gain, grad):
    weighted = grad * gain
    return scale * (weighted - unit * jnp.mean(unit * weighted, -1, keepdims=True))


def per_device(
    tokens,
    segment_ids,
    first_gain,
    query_gain,
    key_gain,
    query_weight,
    key_weight,
    value_weight,
    out_weight,
    second_gain,
    gate_weight,
    up_weight,
    down_weight,
    cotangent,
):
    z, h, c = lax.axis_index("z"), lax.axis_index("h"), lax.axis_index("c")
    y, l = lax.axis_index("y"), lax.axis_index("l")
    where = jnp.stack([z, h * 2 + y // 2]).astype(jnp.int32)
    y_own = jnp.where(y % 2 == c, y, 3 - y)
    tokens = remap(tokens)
    attn_shard = jnp.concatenate([query_weight, key_weight, value_weight], 1)
    attn_own = gather_weights(attn_shard, where)
    attn_w = [attn_own, core_swap(attn_own)]
    seg_row = remap(segment_ids)[0]
    cotangent = remap(cotangent)

    def index_of(y_here):
        blocks = [((y_here ^ (2 * i)) * 2 + (l ^ j)) for i, j in SQUARE]
        return blocks

    blocks = index_of(y_own) + index_of(3 - y_own)
    index = jnp.concatenate([b * 128 + jnp.arange(128, dtype=jnp.int32) for b in blocks])
    seg = jnp.concatenate([lax.dynamic_slice_in_dim(seg_row, b * 128, 128, 0) for b in blocks])
    start = jnp.zeros((1024,), jnp.int32)
    for v in range(1, 4):
        start = start + jnp.where(seg == v, jnp.sum((seg_row < v).astype(jnp.int32)), 0)
    places = (index - start).astype(F32)[:512]
    inverse = ROPE_BASE ** (-jnp.arange(0, 128, 2, dtype=F32) / 128)
    phases = places[:, None] * inverse[None, :]
    phases = jnp.concatenate([phases, phases], -1)
    cosine, sine = jnp.cos(phases), jnp.sin(phases)
    allowed = (seg[:512, None] == seg[None, :]) & (index[None, :] <= index[:512, None])

    input_float = tokens.astype(F32)
    unit_one, scale_one = norm_forward(input_float)
    normed_one = gather_tokens((unit_one * first_gain).astype(BF16))
    out_own = gather_weights(out_weight.T, where)
    out_w = [out_own, core_swap(out_own)]
    mlp_shard = jnp.concatenate([gate_weight, up_weight, down_weight.T], 1)
    mlp_own = gather_weights(mlp_shard, where)
    mlp_w = [mlp_own, core_swap(mlp_own)]
    gu_w = [w[:, :768] for w in mlp_w]
    down_w = [w[:, 768:] for w in mlp_w]
    cot_all = gather_tokens(cotangent)
    gains = [query_gain, query_gain, key_gain]
    units, scales, rots, values = [], [], [], []
    for j in range(2):
        raw = dot_nn(normed_one, attn_w[j])
        heads = [raw[:, i * 128 : (i + 1) * 128] for i in range(4)]
        for i in range(3):
            unit, scale = norm_forward(heads[i])
            scaled = unit * gains[i]
            units.append(unit)
            scales.append(scale)
            rots.append((scaled * cosine + turned(scaled) * sine).astype(BF16))
        values.append(heads[3].astype(BF16))
    swapped = core_swap(jnp.concatenate([rots[2], rots[5], values[0], values[1]], 1))
    keys = [
        jnp.concatenate([rots[2], swapped[:, 128:256]], 0),
        jnp.concatenate([rots[5], swapped[:, :128]], 0),
    ]
    vals = [
        jnp.concatenate([values[0], swapped[:, 384:]], 0),
        jnp.concatenate([values[1], swapped[:, 256:384]], 0),
    ]
    score_scale = 128 ** (-0.5)
    attended, logs = [], []
    for j in range(2):
        outs = []
        for i in range(2):
            scores = jnp.where(allowed, dot_nt(rots[j * 3 + i], keys[j]) * score_scale, NEG_LARGE)
            top = jnp.max(scores, -1, keepdims=True)
            exponent = jnp.exp(scores - top)
            total = jnp.sum(exponent, -1, keepdims=True)
            outs.append(dot_nn((exponent / total).astype(BF16), vals[j]).astype(BF16))
            logs.append(top + jnp.log(total))
        attended.append(jnp.concatenate(outs, 1))
    hidden = input_float + scatter_tokens(
        dot_nt(attended[0], out_w[0]) + dot_nt(attended[1], out_w[1])
    )

    unit_two, scale_two = norm_forward(hidden)
    normed_two = gather_tokens((unit_two * second_gain).astype(BF16))
    partial_two, branch, gu_grads, down_grads = 0.0, 0.0, [], []
    for j in range(2):
        gate_up = dot_nn(normed_two, gu_w[j])
        gate, up = gate_up[:, :384], gate_up[:, 384:]
        sig = jax.nn.sigmoid(gate)
        silu = gate * sig
        act = (silu * up).astype(BF16)
        grad_act = dot_nn(cot_all, down_w[j])
        grad_gate = (grad_act * up * (sig + silu * (1.0 - sig))).astype(BF16)
        grad_up = (grad_act * silu).astype(BF16)
        grad_gu = jnp.concatenate([grad_gate, grad_up], 1)
        partial_two = partial_two + dot_nt(grad_gu, gu_w[j])
        branch = branch + dot_nt(act, down_w[j])
        gu_grads.append(dot_tn(normed_two, grad_gu))
        down_grads.append(dot_tn(cot_all, act))
    grad_normed_two = scatter_tokens(partial_two)
    second_part = jnp.sum(partial_two * normed_two.astype(F32), 0) / second_gain

    grad_hidden = cotangent.astype(F32) + norm_backward(
        unit_two, scale_two, second_gain, grad_normed_two
    )
    hidden_grad = gather_tokens(grad_hidden.astype(BF16))
    layer_out = remap_back((hidden + scatter_tokens(branch)).astype(BF16))
    mlp_owned = scatter_weights(
        jnp.concatenate([gu_grads[0], down_grads[0]], 1),
        jnp.concatenate([gu_grads[1], down_grads[1]], 1),
        where,
    )
    out_owned = scatter_weights(
        dot_tn(hidden_grad, attended[0]), dot_tn(hidden_grad, attended[1]), where
    )
    grad_rot, grad_keys, grad_values = [], [], []
    for j in range(2):
        grad_attended = dot_nn(hidden_grad, out_w[j]).astype(BF16)
        grad_key, grad_value = 0.0, 0.0
        for i in range(2):
            query = rots[j * 3 + i]
            scores = dot_nt(query, keys[j]) * score_scale
            prob = jnp.where(allowed, jnp.exp(scores - logs[j * 2 + i]), 0.0)
            grad_out = grad_attended[:, i * 128 : (i + 1) * 128]
            grad_prob = dot_nt(grad_out, vals[j])
            inner = jnp.sum(prob * grad_prob, -1, keepdims=True)
            grad_scores = (prob * (grad_prob - inner)).astype(BF16)
            grad_rot.append(dot_nn(grad_scores, keys[j]) * score_scale)
            grad_key = grad_key + dot_tn(grad_scores, query) * score_scale
            grad_value = grad_value + dot_tn(prob.astype(BF16), grad_out)
        grad_rot.append(grad_key[:512])
        grad_keys.append(grad_key)
        grad_values.append(grad_value)
    swapped = core_swap(
        jnp.concatenate([g[512:].astype(BF16) for g in grad_keys + grad_values], 1)
    ).astype(F32)
    grad_rot[2] = grad_rot[2] + swapped[:, 128:256]
    grad_rot[5] = grad_rot[5] + swapped[:, :128]
    grad_values = [
        grad_values[0][:512] + swapped[:, 384:],
        grad_values[1][:512] + swapped[:, 256:384],
    ]
    gain_parts, grad_raws, partial_one = [], [], 0.0
    for j in range(2):
        grad_raw = []
        for i in range(3):
            g = grad_rot[j * 3 + i]
            grad = g * cosine - turned(g) * sine
            gain_parts.append(jnp.sum(grad * units[j * 3 + i], 0))
            grad_raw.append(
                norm_backward(units[j * 3 + i], scales[j * 3 + i], gains[i], grad).astype(BF16)
            )
        grad_raw = jnp.concatenate(grad_raw + [grad_values[j].astype(BF16)], 1)
        grad_raws.append(grad_raw)
        partial_one = partial_one + dot_nt(grad_raw, attn_w[j])
    grad_normed_one = scatter_tokens(partial_one)
    first_part = jnp.sum(partial_one * normed_one.astype(F32), 0) / first_gain
    attn_owned = scatter_weights(
        dot_tn(normed_one, grad_raws[0]), dot_tn(normed_one, grad_raws[1]), where
    )
    query_part = gain_parts[0] + gain_parts[1] + gain_parts[3] + gain_parts[4]
    sums = all_sum(
        jnp.concatenate([first_part, second_part, query_part, gain_parts[2] + gain_parts[5]])
    )
    grad_tokens = grad_hidden + norm_backward(unit_one, scale_one, first_gain, grad_normed_one)
    grad_tokens = remap_back(grad_tokens.astype(BF16))
    return (
        layer_out,
        grad_tokens,
        sums[:1024],
        sums[2048:2176],
        sums[2176:],
        attn_owned[:, :256],
        attn_owned[:, 256:384],
        attn_owned[:, 384:],
        out_owned.T,
        sums[1024:2048],
        mlp_owned[:, :384],
        mlp_owned[:, 384:768],
        mlp_owned[:, 768:].T,
    )


def solution(mesh):
    fine = Mesh(mesh.devices.reshape(4, 2, 2, 4, 2), ("z", "h", "c", "y", "l"))
    dp, tensor = ("z", "h", "c"), ("y", "l")
    rows, cols, trans = P(dp + tensor, None), P(dp, tensor), P(tensor, dp)
    in_specs = (
        rows, P(dp, None), P(), P(), P(), cols, cols, cols, trans, P(), cols, cols, trans, rows,
    )
    out_specs = (rows, rows, P(), P(), P(), cols, cols, cols, trans, P(), cols, cols, trans)
    return jax.shard_map(
        per_device, mesh=fine, in_specs=in_specs, out_specs=out_specs, check_vma=False
    )
```

```python
import jax
import jax.numpy as jnp
from jax import lax
from jax.experimental import pallas as pl
from jax.experimental.pallas import tpu as pltpu
from jax.sharding import Mesh
from jax.sharding import PartitionSpec as P

EPSILON = 1e-06
ROPE_BASE = 1000000.0
NEG_LARGE = -1e30
BF16 = jnp.bfloat16
F32 = jnp.float32
SQUARE = ((0, 0), (0, 1), (1, 0), (1, 1))


def place_of(y, pair):
    return y if y // 2 == pair else 3 - y


def remap_pairs():
    pairs = []
    for c in range(2):
        for y in range(4):
            for l in range(2):
                pairs.append(((c * 4 + y) * 2 + l, ((y % 2) * 4 + place_of(y, c)) * 2 + l))
    return pairs


def remap(value):
    return lax.ppermute(value, ("c", "y", "l"), remap_pairs())


def remap_back(value):
    return lax.ppermute(value, ("c", "y", "l"), [(b, a) for a, b in remap_pairs()])


def shard_pairs(a, b):
    pairs = []
    for h in range(2):
        for c in range(2):
            for y in range(4):
                for l in range(2):
                    source = ((h * 2 + c) * 4 + y) * 2 + l
                    pairs.append((source, (((h ^ a) * 2 + y % 2) * 4 + place_of(y, c ^ b)) * 2 + l))
    return pairs


def shard_out(value, a, b):
    return lax.ppermute(value, ("h", "c", "y", "l"), shard_pairs(a, b))


def shard_home(value, a, b):
    return lax.ppermute(value, ("h", "c", "y", "l"), [(t, s) for s, t in shard_pairs(a, b)])


def ring(value, axis, step):
    return lax.ppermute(value, (axis,), [(i, (i + step) % 4) for i in range(4)])


def core_swap(value):
    return lax.ppermute(value, ("c",), [(0, 1), (1, 0)])


def across(value, i, j):
    if (i, j) == (0, 0):
        return value
    pairs = [(y * 2 + l, (y ^ i) * 2 + (l ^ j)) for y in range(4) for l in range(2)]
    return lax.ppermute(value, ("y", "l"), pairs)


def dot_nn(a, b):
    return lax.dot_general(a, b, (((1,), (0,)), ((), ())), preferred_element_type=F32)


def dot_nt(a, b):
    return lax.dot_general(a, b, (((1,), (1,)), ((), ())), preferred_element_type=F32)


def dot_tn(a, b):
    return lax.dot_general(a, b, (((0,), (0,)), ((), ())), preferred_element_type=F32)


def gather_tokens(block):
    return jnp.concatenate([across(block, i, j) for i, j in SQUARE], 0)


def scatter_tokens(partial):
    total = partial[:128]
    for s in (1, 2, 3):
        total = total + across(partial[s * 128 : (s + 1) * 128].astype(BF16), *SQUARE[s]).astype(F32)
    return total


def place_kernel(where, *refs):
    *parts, out = refs
    if len(parts) == 5:
        parts[2:4] = [(parts[2], parts[3])]
    for s in range(4):
        for k in range(4):
            at = ((where[0] + s) % 4) * 4 + (where[1] ^ k)
            block = parts[s][k // 2][k % 2] if isinstance(parts[s], tuple) else parts[s][k]
            out[pl.ds(pl.multiple_of(at * 64, 64), 64), :] = block


def pick_kernel(where, own, swapped, *outs):
    for s in range(4):
        for k in range(4):
            at = ((where[0] + s) % 4) * 4 + (where[1] ^ k)
            rows = pl.ds(pl.multiple_of(at * 64, 64), 64)
            total = own[rows, :].astype(F32) + swapped[rows, :].astype(F32)
            outs[s][k] = total.astype(BF16)


def vmem(n):
    return [pl.BlockSpec(memory_space=pltpu.VMEM)] * n


SMEM = pl.BlockSpec(memory_space=pltpu.SMEM)
PARAMS = pltpu.CompilerParams(vmem_limit_bytes=48 * 1024 * 1024)


def after(value, *others):
    return lax.optimization_barrier((value, *others))[0]


def gather_stage(shard):
    return jnp.stack([shard_out(shard, a, b) for a, b in SQUARE])


def gather_rings(stage):
    return [stage] + [ring(stage, "z", -s) for s in (1, 2, 3)]


def gather_chain(stage):
    behind, ahead = ring(stage, "z", 1), ring(stage, "z", -1)
    return [stage, ahead, (ring(ahead[:2], "z", -1), ring(behind[2:], "z", 1)), behind]


def place(parts, where):
    width = parts[0].shape[2]
    parts = jax.tree.leaves(parts)
    return pl.pallas_call(
        place_kernel,
        out_shape=jax.ShapeDtypeStruct((1024, width), BF16),
        in_specs=[SMEM] + vmem(len(parts)),
        out_specs=vmem(1)[0],
        compiler_params=PARAMS,
    )(where, *parts)


def pick(own, swapped, where):
    width = own.shape[1]
    return pl.pallas_call(
        pick_kernel,
        out_shape=[jax.ShapeDtypeStruct((4, 64, width), BF16)] * 4,
        in_specs=[SMEM] + vmem(2),
        out_specs=vmem(4),
        compiler_params=PARAMS,
    )(where, own, swapped)


def scatter_rings(parts, first=False):
    got = [ring(parts[s], "z", s) for s in (1, 2, 3)]
    total = parts[0].astype(F32)
    for value in got:
        total = total + value.astype(F32)
    return (total.astype(BF16), got[0]) if first else total.astype(BF16)


def scatter_chain(parts):
    add = lambda a, b: (a.astype(F32) + b.astype(F32)).astype(BF16)
    up, down = ring(parts[2][:2], "z", 1), ring(parts[2][2:], "z", -1)
    ahead = ring(jnp.concatenate([add(parts[1][:2], up), parts[1][2:]]), "z", 1)
    behind = ring(jnp.concatenate([parts[3][:2], add(parts[3][2:], down)]), "z", -1)
    return (parts[0].astype(F32) + ahead.astype(F32) + behind.astype(F32)).astype(BF16)


def scatter_home(low):
    result = 0.0
    for k in range(4):
        result = result + shard_home(low[k], *SQUARE[k]).astype(F32)
    return result


def square_sum(values):
    values = values + core_swap(values)
    got = [across(values, i, j) for i, j in SQUARE]
    return (got[0] + got[1]) + (got[2] + got[3])


def squares_sum(values):
    got = [values]
    for a, b in SQUARE[1:]:
        pairs = [(h * 4 + y, (h ^ a) * 4 + (3 - y if b else y)) for h in range(2) for y in range(4)]
        got.append(lax.ppermute(values, ("h", "y"), pairs))
    values = (got[0] + got[1]) + (got[2] + got[3])
    got = [ring(values, "z", s) for s in (1, 2, 3)]
    return (values + got[1]) + (got[0] + got[2])


def turned(values):
    half = values.shape[-1] // 2
    return jnp.concatenate([-values[..., half:], values[..., :half]], -1)


def norm_forward(values):
    scale = lax.rsqrt(jnp.mean(values * values, -1, keepdims=True) + EPSILON)
    return values * scale, scale


def norm_backward(unit, scale, gain, grad):
    weighted = grad * gain
    return scale * (weighted - unit * jnp.mean(unit * weighted, -1, keepdims=True))


def per_device(
    tokens,
    segment_ids,
    first_gain,
    query_gain,
    key_gain,
    query_weight,
    key_weight,
    value_weight,
    out_weight,
    second_gain,
    gate_weight,
    up_weight,
    down_weight,
    cotangent,
):
    z, h, c = lax.axis_index("z"), lax.axis_index("h"), lax.axis_index("c")
    y, l = lax.axis_index("y"), lax.axis_index("l")
    where = jnp.stack([z, h * 2 + y // 2]).astype(jnp.int32)
    y_own = jnp.where(y % 2 == c, y, 3 - y)
    tokens = remap(tokens)
    attn_shard = jnp.concatenate([query_weight, key_weight, value_weight], 1)
    attn_stage = gather_stage(attn_shard)
    attn_own = place(gather_rings(attn_stage), where)
    attn_w = [attn_own, core_swap(attn_own)]
    seg_row = jnp.where(y // 2 == c, segment_ids, core_swap(segment_ids))[0]

    def index_of(y_here):
        blocks = [((y_here ^ (2 * i)) * 2 + (l ^ j)) for i, j in SQUARE]
        return blocks

    blocks = index_of(y_own) + index_of(3 - y_own)
    index = jnp.concatenate([b * 128 + jnp.arange(128, dtype=jnp.int32) for b in blocks])
    seg = jnp.concatenate([lax.dynamic_slice_in_dim(seg_row, b * 128, 128, 0) for b in blocks])
    start = jnp.zeros((1024,), jnp.int32)
    for v in range(1, 4):
        start = start + jnp.where(seg == v, jnp.sum((seg_row < v).astype(jnp.int32)), 0)
    places = (index - start).astype(F32)[:512]
    inverse = ROPE_BASE ** (-jnp.arange(0, 128, 2, dtype=F32) / 128)
    phases = places[:, None] * inverse[None, :]
    phases = jnp.concatenate([phases, phases], -1)
    cosine, sine = jnp.cos(phases), jnp.sin(phases)
    allowed = (seg[:512, None] == seg[None, :]) & (index[None, :] <= index[:512, None])

    input_float = tokens.astype(F32)
    unit_one, scale_one = norm_forward(input_float)
    normed_one = gather_tokens((unit_one * first_gain).astype(BF16))
    out_stage = gather_stage(after(out_weight.T, attn_stage))
    out_own = place(gather_rings(after(out_stage, attn_own)), where)
    out_w = [out_own, core_swap(out_own)]
    mlp_shard = jnp.concatenate([gate_weight, up_weight, down_weight.T], 1)
    cotangent = remap(after(cotangent, normed_one))
    mlp_stage = gather_stage(after(mlp_shard, normed_one))
    mlp_parts = gather_chain(after(mlp_stage, out_own))
    cot_all = gather_tokens(cotangent)
    cosine, sine, out_stage, mlp_stage = lax.optimization_barrier(
        (cosine, sine, out_stage, mlp_stage)
    )
    gains = [query_gain, query_gain, key_gain]
    units, scales, rots, values = [], [], [], []
    for j in range(2):
        raw = dot_nn(normed_one, attn_w[j])
        heads = [raw[:, i * 128 : (i + 1) * 128] for i in range(4)]
        for i in range(3):
            unit, scale = norm_forward(heads[i])
            scaled = unit * gains[i]
            units.append(unit)
            scales.append(scale)
            rots.append((scaled * cosine + turned(scaled) * sine).astype(BF16))
        values.append(heads[3].astype(BF16))
    swapped = core_swap(jnp.concatenate([rots[2], rots[5], values[0], values[1]], 1))
    keys = [
        jnp.concatenate([rots[2], swapped[:, 128:256]], 0),
        jnp.concatenate([rots[5], swapped[:, :128]], 0),
    ]
    vals = [
        jnp.concatenate([values[0], swapped[:, 384:]], 0),
        jnp.concatenate([values[1], swapped[:, 256:384]], 0),
    ]
    score_scale = 128 ** (-0.5)
    attended, logs = [], []
    for j in range(2):
        outs = []
        for i in range(2):
            scores = jnp.where(allowed, dot_nt(rots[j * 3 + i], keys[j]) * score_scale, NEG_LARGE)
            top = jnp.max(scores, -1, keepdims=True)
            exponent = jnp.exp(scores - top)
            total = jnp.sum(exponent, -1, keepdims=True)
            outs.append(dot_nn((exponent / total).astype(BF16), vals[j]).astype(BF16))
            logs.append(top + jnp.log(total))
        attended.append(jnp.concatenate(outs, 1))
    mlp_parts, attended = lax.optimization_barrier((mlp_parts, attended))
    mlp_own = place(mlp_parts, where)
    mlp_w = [mlp_own, core_swap(mlp_own)]
    gu_w = [w[:, :768] for w in mlp_w]
    down_w = [w[:, 768:] for w in mlp_w]
    hidden = input_float + scatter_tokens(
        dot_nt(attended[0], out_w[0]) + dot_nt(attended[1], out_w[1])
    )

    unit_two, scale_two = norm_forward(hidden)
    normed_two = gather_tokens((unit_two * second_gain).astype(BF16))
    partial_two, branch, gu_grads, down_grads = 0.0, 0.0, [], []
    for j in range(2):
        gate_up = dot_nn(normed_two, gu_w[j])
        gate, up = gate_up[:, :384], gate_up[:, 384:]
        sig = jax.nn.sigmoid(gate)
        silu = gate * sig
        act = (silu * up).astype(BF16)
        grad_act = dot_nn(cot_all, down_w[j])
        grad_gate = (grad_act * up * (sig + silu * (1.0 - sig))).astype(BF16)
        grad_up = (grad_act * silu).astype(BF16)
        grad_gu = jnp.concatenate([grad_gate, grad_up], 1)
        partial_two = partial_two + dot_nt(grad_gu, gu_w[j])
        branch = branch + dot_nt(act, down_w[j])
        gu_grads.append(dot_tn(normed_two, grad_gu))
        down_grads.append(dot_tn(cot_all, act))
    grad_normed_two = scatter_tokens(partial_two)
    second_part = jnp.sum(partial_two * normed_two.astype(F32), 0) / second_gain

    grad_hidden = cotangent.astype(F32) + norm_backward(
        unit_two, scale_two, second_gain, grad_normed_two
    )
    hidden_grad = gather_tokens(grad_hidden.astype(BF16))
    mlp_low_own = jnp.concatenate([gu_grads[0], down_grads[0]], 1).astype(BF16)
    mlp_low_other = jnp.concatenate([gu_grads[1], down_grads[1]], 1).astype(BF16)
    mlp_picked = pick(mlp_low_own, core_swap(mlp_low_other), where)
    hidden_grad, mlp_picked = lax.optimization_barrier((hidden_grad, mlp_picked))
    layer_out = (hidden + scatter_tokens(after(branch, hidden_grad))).astype(BF16)
    mlp_low = scatter_chain(mlp_picked)
    out_grads = [dot_tn(hidden_grad, attended[j]).astype(BF16) for j in range(2)]
    out_picked = pick(out_grads[0], core_swap(out_grads[1]), where)
    grad_rot, grad_keys, grad_values = [], [], []
    for j in range(2):
        grad_attended = dot_nn(hidden_grad, out_w[j]).astype(BF16)
        grad_key, grad_value = 0.0, 0.0
        for i in range(2):
            query = rots[j * 3 + i]
            scores = dot_nt(query, keys[j]) * score_scale
            prob = jnp.where(allowed, jnp.exp(scores - logs[j * 2 + i]), 0.0)
            grad_out = grad_attended[:, i * 128 : (i + 1) * 128]
            grad_prob = dot_nt(grad_out, vals[j])
            inner = jnp.sum(prob * grad_prob, -1, keepdims=True)
            grad_scores = (prob * (grad_prob - inner)).astype(BF16)
            grad_rot.append(dot_nn(grad_scores, keys[j]) * score_scale)
            grad_key = grad_key + dot_tn(grad_scores, query) * score_scale
            grad_value = grad_value + dot_tn(prob.astype(BF16), grad_out)
        grad_rot.append(grad_key[:512])
        grad_keys.append(grad_key)
        grad_values.append(grad_value)
    swapped = core_swap(
        jnp.concatenate([g[512:].astype(BF16) for g in grad_keys + grad_values], 1)
    ).astype(F32)
    grad_rot[2] = grad_rot[2] + swapped[:, 128:256]
    grad_rot[5] = grad_rot[5] + swapped[:, :128]
    grad_values = [
        grad_values[0][:512] + swapped[:, 384:],
        grad_values[1][:512] + swapped[:, 256:384],
    ]
    grad_rot, layer_out, out_picked = lax.optimization_barrier((grad_rot, layer_out, out_picked))
    gain_parts, grad_raws, partial_one = [], [], 0.0
    for j in range(2):
        grad_raw = []
        for i in range(3):
            g = grad_rot[j * 3 + i]
            grad = g * cosine - turned(g) * sine
            gain_parts.append(jnp.sum(grad * units[j * 3 + i], 0))
            grad_raw.append(
                norm_backward(units[j * 3 + i], scales[j * 3 + i], gains[i], grad).astype(BF16)
            )
        grad_raw = jnp.concatenate(grad_raw + [grad_values[j].astype(BF16)], 1)
        grad_raws.append(grad_raw)
        partial_one = partial_one + dot_nt(grad_raw, attn_w[j])
    attn_grads = [
        dot_tn(normed_one, after(grad_raws[j], partial_one)).astype(BF16) for j in range(2)
    ]
    first_part = jnp.sum(partial_one * normed_one.astype(F32), 0) / first_gain
    grad_normed_one = scatter_tokens(partial_one)
    attn_swapped = core_swap(attn_grads[1])
    query_part = gain_parts[0] + gain_parts[1] + gain_parts[3] + gain_parts[4]
    sums = jnp.concatenate([first_part, second_part, query_part, gain_parts[2] + gain_parts[5]])
    sums = square_sum(after(sums, attn_swapped))
    attn_picked = pick(attn_grads[0], attn_swapped, where)
    out_low = scatter_rings(after(out_picked, mlp_low))
    attn_low, attn_near = scatter_rings(attn_picked, True)
    sums = squares_sum(after(sums, attn_near))
    rest_low = jnp.concatenate([mlp_low, after(out_low, attn_near)], 2)
    grad_tokens = grad_hidden + norm_backward(unit_one, scale_one, first_gain, grad_normed_one)
    grad_tokens = remap_back(after(grad_tokens.astype(BF16), attn_near))
    layer_out = remap_back(after(layer_out, attn_near))
    rest_owned = scatter_home(rest_low)
    mlp_owned, out_owned = rest_owned[:, :1152], rest_owned[:, 1152:]
    attn_owned = scatter_home(attn_low)
    return (
        layer_out,
        grad_tokens,
        sums[:1024],
        sums[2048:2176],
        sums[2176:],
        attn_owned[:, :256],
        attn_owned[:, 256:384],
        attn_owned[:, 384:],
        out_owned.T,
        sums[1024:2048],
        mlp_owned[:, :384],
        mlp_owned[:, 384:768],
        mlp_owned[:, 768:].T,
    )


def solution(mesh):
    fine = Mesh(mesh.devices.reshape(4, 2, 2, 4, 2), ("z", "h", "c", "y", "l"))
    dp, tensor = ("z", "h", "c"), ("y", "l")
    rows, cols, trans = P(dp + tensor, None), P(dp, tensor), P(tensor, dp)
    in_specs = (
        rows, P(dp, None), P(), P(), P(), cols, cols, cols, trans, P(), cols, cols, trans, rows,
    )
    out_specs = (rows, rows, P(), P(), P(), cols, cols, cols, trans, P(), cols, cols, trans)
    return jax.shard_map(
        per_device, mesh=fine, in_specs=in_specs, out_specs=out_specs, check_vma=False
    )
```

```python
import jax
import jax.numpy as jnp
from jax import lax
from jax.experimental import pallas as pl
from jax.experimental.pallas import tpu as pltpu
from jax.sharding import Mesh
from jax.sharding import PartitionSpec as P

EPSILON = 1e-06
ROPE_BASE = 1000000.0
NEG_LARGE = -1e30
BF16 = jnp.bfloat16
F32 = jnp.float32
SQUARE = ((0, 0), (0, 1), (1, 0), (1, 1))


def place_of(y, pair):
    return y if y // 2 == pair else 3 - y


def remap_pairs():
    pairs = []
    for c in range(2):
        for y in range(4):
            for l in range(2):
                pairs.append(((c * 4 + y) * 2 + l, ((y % 2) * 4 + place_of(y, c)) * 2 + l))
    return pairs


def remap(value):
    return lax.ppermute(value, ("c", "y", "l"), remap_pairs())


def remap_back(value):
    return lax.ppermute(value, ("c", "y", "l"), [(b, a) for a, b in remap_pairs()])


def shard_pairs(a, b):
    pairs = []
    for h in range(2):
        for c in range(2):
            for y in range(4):
                for l in range(2):
                    source = ((h * 2 + c) * 4 + y) * 2 + l
                    pairs.append((source, (((h ^ a) * 2 + y % 2) * 4 + place_of(y, c ^ b)) * 2 + l))
    return pairs


def shard_out(value, a, b):
    return lax.ppermute(value, ("h", "c", "y", "l"), shard_pairs(a, b))


def shard_home(value, a, b):
    return lax.ppermute(value, ("h", "c", "y", "l"), [(t, s) for s, t in shard_pairs(a, b)])


def ring(value, axis, step):
    return lax.ppermute(value, (axis,), [(i, (i + step) % 4) for i in range(4)])


def core_swap(value):
    return lax.ppermute(value, ("c",), [(0, 1), (1, 0)])


def across(value, i, j):
    if (i, j) == (0, 0):
        return value
    pairs = [(y * 2 + l, (y ^ i) * 2 + (l ^ j)) for y in range(4) for l in range(2)]
    return lax.ppermute(value, ("y", "l"), pairs)


def dot_nn(a, b):
    return lax.dot_general(a, b, (((1,), (0,)), ((), ())), preferred_element_type=F32)


def dot_nt(a, b):
    return lax.dot_general(a, b, (((1,), (1,)), ((), ())), preferred_element_type=F32)


def dot_tn(a, b):
    return lax.dot_general(a, b, (((0,), (0,)), ((), ())), preferred_element_type=F32)


def gather_tokens(block):
    return jnp.concatenate([across(block, i, j) for i, j in SQUARE], 0)


def scatter_tokens(partial):
    total = partial[:128]
    for s in (1, 2, 3):
        total = total + across(partial[s * 128 : (s + 1) * 128].astype(BF16), *SQUARE[s]).astype(F32)
    return total


def place_kernel(where, *refs):
    *parts, out = refs
    if len(parts) == 5:
        parts[2:4] = [(parts[2], parts[3])]
    for s in range(4):
        for k in range(4):
            at = ((where[0] + s) % 4) * 4 + (where[1] ^ k)
            block = parts[s][k // 2][k % 2] if isinstance(parts[s], tuple) else parts[s][k]
            out[pl.ds(pl.multiple_of(at * 64, 64), 64), :] = block


def pick_kernel(where, own, swapped, *outs):
    for s in range(4):
        for k in range(4):
            at = ((where[0] + s) % 4) * 4 + (where[1] ^ k)
            rows = pl.ds(pl.multiple_of(at * 64, 64), 64)
            total = own[rows, :].astype(F32) + swapped[rows, :].astype(F32)
            outs[s][k] = total.astype(BF16)


def attend_kernel(meta, query, kv_own, kv_other, begin, index, out_own, out_other, *refs):
    keys, values, probs_low, probs_high, attended = refs[:5]
    pieces = refs[5:]
    for t in range(8):
        source, at = (kv_own, t) if t < 4 else (kv_other, t - 4)
        rows = pl.ds(pl.multiple_of(meta[3 + t] * 128, 128), 128)
        part = source[at * 128 : (at + 1) * 128, :]
        for j in range(2):
            jj = j if t < 4 else 1 - j
            keys[j, rows, :] = part[:, jj * 128 : jj * 128 + 128]
            values[j, rows, :] = part[:, 256 + jj * 128 : 384 + jj * 128]
    for half, (count, probs) in enumerate(((512, probs_low), (768, probs_high))):
        rows = pl.ds(pl.multiple_of(meta[half], 256), 256)
        first = 0 if half == 0 else pl.multiple_of(meta[2], 256)
        place = first + lax.broadcasted_iota(jnp.int32, (256, count), 1)
        allowed = (place >= begin[rows, :]) & (place <= index[rows, :])
        for j in range(2):
            key = keys[j, pl.ds(first, count), :]
            value = values[j, pl.ds(first, count), :]
            for i in range(2):
                n = j * 2 + i
                scores = dot_nt(query[rows, n * 128 : (n + 1) * 128], key) * 128 ** (-0.5)
                scores = jnp.where(allowed, scores, NEG_LARGE)
                exponent = jnp.exp(scores - jnp.max(scores, -1, keepdims=True))
                prob = exponent * (1.0 / jnp.sum(exponent, -1, keepdims=True))
                prob = prob.astype(BF16)
                probs[n] = prob
                attended[rows, n * 128 : (n + 1) * 128] = dot_nn(prob, value).astype(BF16)
    for s in range(4):
        rows = attended[s * 128 : (s + 1) * 128, :]
        total = dot_nt(rows[:, :256], out_own[...]) + dot_nt(rows[:, 256:], out_other[...])
        pieces[s][...] = total.astype(pieces[s].dtype)


def attend_back_kernel(meta, *refs):
    grads = refs[:4]
    out_own, out_other, query, keys, values, probs_low, probs_high = refs[4:11]
    grad_query, back_own, back_other = refs[11:14]
    grad_out, grad_keys, grad_values = refs[14:]
    for s in range(4):
        grad = grads[s][...]
        rows = pl.ds(s * 128, 128)
        grad_out[rows, :256] = dot_nn(grad, out_own[...]).astype(BF16)
        grad_out[rows, 256:] = dot_nn(grad, out_other[...]).astype(BF16)
    grad_keys[...] = jnp.zeros_like(grad_keys)
    grad_values[...] = jnp.zeros_like(grad_values)
    for half, (count, probs) in enumerate(((512, probs_low), (768, probs_high))):
        rows = pl.ds(pl.multiple_of(meta[half], 256), 256)
        first = 0 if half == 0 else pl.multiple_of(meta[2], 256)
        span = pl.ds(first, count)
        for j in range(2):
            key = keys[j, span, :]
            value = values[j, span, :]
            for i in range(2):
                n = j * 2 + i
                cols = slice(n * 128, (n + 1) * 128)
                grad = grad_out[rows, cols]
                prob = probs[n]
                wide = prob.astype(F32)
                grad_prob = dot_nt(grad, value)
                inner = jnp.sum(wide * grad_prob, -1, keepdims=True)
                grad_scores = (wide * (grad_prob - inner)).astype(BF16)
                grad_query[rows, cols] = dot_nn(grad_scores, key) * 128 ** (-0.5)
                grad_keys[j, span, :] += dot_tn(grad_scores, query[rows, cols]) * 128 ** (-0.5)
                grad_values[j, span, :] += dot_tn(prob, grad)
    for t in range(8):
        rows = pl.ds(pl.multiple_of(meta[3 + t] * 128, 128), 128)
        target = back_own if t < 4 else back_other
        at = slice((t % 4) * 128, (t % 4 + 1) * 128)
        for j in range(2):
            jj = j if t < 4 else 1 - j
            target[at, jj * 128 : jj * 128 + 128] = grad_keys[j, rows, :].astype(target.dtype)
            target[at, 256 + jj * 128 : 384 + jj * 128] = grad_values[j, rows, :].astype(target.dtype)


def rolled(values, sine):
    return pltpu.roll(values, 64, 1) * sine


def tail_kernel(*refs):
    (grad_query, back_own, swapped, raw_own, raw_other, cosine, sine, gains, weight_own, weight_other) = refs[:10]
    normed, branch, small, first_gain = refs[10:14], refs[14], refs[15], refs[16]
    (low_own, low_other, mine, *pieces) = refs[17:23]
    partial = refs[23]
    sums = [0.0, 0.0]
    for j, (raw, low) in enumerate(((raw_own, low_own), (raw_other, low_other))):
        cols = slice(j * 128, (j + 1) * 128)
        grad_key = back_own[:, cols] + swapped[:, cols].astype(F32)
        cols = slice(256 + j * 128, 384 + j * 128)
        grad_value = back_own[:, cols] + swapped[:, cols].astype(F32)
        for i in range(3):
            cols = slice(i * 128, (i + 1) * 128)
            grad = grad_key if i == 2 else grad_query[:, (j * 2 + i) * 128 : (j * 2 + i + 1) * 128]
            grad = grad * cosine[...] - rolled(grad, sine[...])
            value = raw[:, cols]
            scale = lax.rsqrt(jnp.mean(value * value, -1, keepdims=True) + EPSILON)
            unit = value * scale
            sums[i // 2] = sums[i // 2] + jnp.sum(grad * unit, 0, keepdims=True)
            weighted = grad * gains[i // 2 : i // 2 + 1, :]
            back = scale * (weighted - unit * jnp.mean(unit * weighted, -1, keepdims=True))
            low[:, cols] = back.astype(BF16)
        low[:, 384:] = grad_value.astype(BF16)
    first = 0.0
    for s in range(4):
        rows = slice(s * 128, (s + 1) * 128)
        partial[...] = dot_nt(low_own[rows, :], weight_own[:, :512]) + dot_nt(
            low_other[rows, :], weight_other[:, :512]
        )
        first = first + jnp.sum(partial[...] * normed[s][:128, :].astype(F32), 0, keepdims=True)
        out = mine if s == 0 else pieces[s - 1]
        out[:128, :] = partial[...].astype(out.dtype)
        out[128:256, :] = branch[rows, :].astype(out.dtype)
    gains_row = jnp.concatenate([sums[0], sums[1], jnp.zeros((1, 768), F32)], 1)
    block = jnp.concatenate(
        [first / first_gain[...], small[...], gains_row, jnp.zeros((13, 1024), F32)], 0
    ).astype(BF16)
    mine[256:, :] = block.astype(F32)
    for piece in pieces:
        piece[256:, :] = block


def pack_kernel(*refs):
    at = 0
    for ref in refs[:-1]:
        refs[-1][:, at : at + ref.shape[1]] = ref[...]
        at += ref.shape[1]


def vmem(n):
    return [pl.BlockSpec(memory_space=pltpu.VMEM)] * n


SMEM = pl.BlockSpec(memory_space=pltpu.SMEM)
PARAMS = pltpu.CompilerParams(vmem_limit_bytes=48 * 1024 * 1024)


def after(value, *others):
    return lax.optimization_barrier((value, *others))[0]


def gather_stage(shard):
    return jnp.stack([shard_out(shard, a, b) for a, b in SQUARE])


def gather_rings(stage):
    return [stage] + [ring(stage, "z", -s) for s in (1, 2, 3)]


def gather_chain(stage):
    behind, ahead = ring(stage, "z", 1), ring(stage, "z", -1)
    return [stage, ahead, (ring(ahead[:2], "z", -1), ring(behind[2:], "z", 1)), behind]


def place(parts, where):
    width = parts[0].shape[2]
    parts = jax.tree.leaves(parts)
    return pl.pallas_call(
        place_kernel,
        out_shape=jax.ShapeDtypeStruct((1024, width), BF16),
        in_specs=[SMEM] + vmem(len(parts)),
        out_specs=vmem(1)[0],
        compiler_params=PARAMS,
    )(where, *parts)


def pick(own, swapped, where):
    width = own.shape[1]
    return pl.pallas_call(
        pick_kernel,
        out_shape=[jax.ShapeDtypeStruct((4, 64, width), BF16)] * 4,
        in_specs=[SMEM] + vmem(2),
        out_specs=vmem(4),
        compiler_params=PARAMS,
    )(where, own, swapped)


def chain_first(parts):
    add = lambda a, b: (a.astype(F32) + b.astype(F32)).astype(BF16)
    up, down = ring(parts[2][:2], "z", 1), ring(parts[2][2:], "z", -1)
    ahead = jnp.concatenate([add(parts[1][:2], up), parts[1][2:]])
    behind = jnp.concatenate([parts[3][:2], add(parts[3][2:], down)])
    return parts[0], ahead, behind


def chain_second(own, ahead, behind):
    total = own.astype(F32) + ring(ahead, "z", 1).astype(F32) + ring(behind, "z", -1).astype(F32)
    return total.astype(BF16)


def scatter_home(low):
    result = 0.0
    for k in range(4):
        result = result + shard_home(low[k], *SQUARE[k]).astype(F32)
    return result


def call(kernel, shapes, *args, smem=0, scratch=()):
    return pl.pallas_call(
        kernel,
        out_shape=[jax.ShapeDtypeStruct(shape, kind) for shape, kind in shapes],
        in_specs=[SMEM] * smem + vmem(len(args) - smem),
        out_specs=vmem(len(shapes)),
        scratch_shapes=[pltpu.VMEM(shape, kind) for shape, kind in scratch],
        compiler_params=PARAMS,
    )(*args)


def pack(*shards):
    return call(pack_kernel, [((64, sum(v.shape[1] for v in shards)), BF16)], *shards)[0]


def norm_forward(values):
    scale = lax.rsqrt(jnp.mean(values * values, -1, keepdims=True) + EPSILON)
    return values * scale, scale


def norm_backward(unit, scale, gain, grad):
    weighted = grad * gain
    return scale * (weighted - unit * jnp.mean(unit * weighted, -1, keepdims=True))


def per_device(
    tokens,
    segment_ids,
    first_gain,
    query_gain,
    key_gain,
    query_weight,
    key_weight,
    value_weight,
    out_weight,
    second_gain,
    gate_weight,
    up_weight,
    down_weight,
    cotangent,
):
    z, h, c = lax.axis_index("z"), lax.axis_index("h"), lax.axis_index("c")
    y, l = lax.axis_index("y"), lax.axis_index("l")
    where = jnp.stack([z, h * 2 + y // 2]).astype(jnp.int32)
    y_own = jnp.where(y % 2 == c, y, 3 - y)
    both = remap(jnp.concatenate([tokens, cotangent], 0))
    attn_stage = gather_stage(pack(query_weight, key_weight, value_weight, out_weight.T))
    attn_own = place(gather_rings(attn_stage), where)
    attn_w = [attn_own, core_swap(attn_own)]
    tokens, cotangent = both[:128], both[128:]
    seg_row = jnp.where(y // 2 == c, segment_ids, core_swap(segment_ids))[0]

    blocks = [(y_own ^ (2 * i)) * 2 + (l ^ j) for i, j in SQUARE]
    other_blocks = [((3 - y_own) ^ (2 * i)) * 2 + (l ^ j) for i, j in SQUARE]
    index = jnp.concatenate([b * 128 + jnp.arange(128, dtype=jnp.int32) for b in blocks])
    seg = jnp.concatenate([lax.dynamic_slice_in_dim(seg_row, b * 128, 128, 0) for b in blocks])
    begin = jnp.zeros((512,), jnp.int32)
    for v in range(1, 4):
        begin = begin + jnp.where(seg == v, jnp.sum((seg_row < v).astype(jnp.int32)), 0)
    places = (index - begin).astype(F32)
    inverse = ROPE_BASE ** (-jnp.arange(0, 128, 2, dtype=F32) / 128)
    phases = places[:, None] * inverse[None, :]
    cosine, sine = jnp.cos(phases), jnp.sin(phases)
    cosine = jnp.concatenate([cosine, cosine], -1)
    sine = jnp.concatenate([-sine, sine], -1)
    upper = y_own // 2
    meta = jnp.stack([upper * 256, (1 - upper) * 256, (y_own % 2) * 256] + blocks + other_blocks)
    meta = meta.astype(jnp.int32)

    input_float = tokens.astype(F32)
    unit_one, scale_one = norm_forward(input_float)
    pieces = jnp.concatenate([(unit_one * first_gain).astype(BF16), cotangent], 0)
    pieces = [across(pieces, i, j) for i, j in SQUARE]
    normed_one = jnp.concatenate([p[:128] for p in pieces], 0)
    cot_all = jnp.concatenate([p[128:] for p in pieces], 0)
    mlp_shard = pack(gate_weight, up_weight, down_weight.T)
    mlp_stage = gather_stage(after(mlp_shard, *pieces[1:]))
    mlp_parts = gather_chain(after(mlp_stage, attn_own))
    gains = [query_gain, query_gain, key_gain]
    raws, rots, values = [], [], []
    for j in range(2):
        raw = dot_nn(normed_one, attn_w[j][:, :512])
        raws.append(raw)
        for i in range(3):
            scaled = norm_forward(raw[:, i * 128 : (i + 1) * 128])[0] * gains[i]
            flipped = jnp.concatenate([scaled[:, 64:], scaled[:, :64]], 1)
            rots.append((scaled * cosine + flipped * sine).astype(BF16))
        values.append(raw[:, 384:].astype(BF16))
    query = jnp.concatenate([rots[0], rots[1], rots[3], rots[4]], 1)
    kv_own = jnp.concatenate([rots[2], rots[5], values[0], values[1]], 1)
    out_w = [w[:, 512:] for w in attn_w]
    block = (128, 1024)
    keys, vals, probs_low, probs_high, attended, *parts = call(
        attend_kernel,
        [((2, 1024, 128), BF16)] * 2
        + [((4, 256, 512), BF16), ((4, 256, 768), BF16), ((512, 512), BF16), (block, F32)]
        + [(block, BF16)] * 3,
        meta,
        query,
        kv_own,
        core_swap(kv_own),
        begin[:, None],
        index[:, None],
        *out_w,
        smem=1,
    )
    mlp_parts = lax.optimization_barrier((mlp_parts, attended))[0]
    mlp_own = place(mlp_parts, where)
    mlp_w = [mlp_own, core_swap(mlp_own)]
    gu_w = [w[:, :768] for w in mlp_w]
    down_w = [w[:, 768:] for w in mlp_w]
    hidden = input_float + parts[0]
    for s in (1, 2, 3):
        hidden = hidden + across(parts[s], *SQUARE[s]).astype(F32)

    unit_two, scale_two = norm_forward(hidden)
    normed_two = gather_tokens((unit_two * second_gain).astype(BF16))
    partial_two, branch, gu_grads, down_grads = 0.0, 0.0, [], []
    for j in range(2):
        gate_up = dot_nn(normed_two, gu_w[j])
        gate, up = gate_up[:, :384], gate_up[:, 384:]
        sig = jax.nn.sigmoid(gate)
        silu = gate * sig
        act = (silu * up).astype(BF16)
        grad_act = dot_nn(cot_all, down_w[j])
        grad_gate = (grad_act * up * (sig + silu * (1.0 - sig))).astype(BF16)
        grad_up = (grad_act * silu).astype(BF16)
        grad_gu = jnp.concatenate([grad_gate, grad_up], 1)
        partial_two = partial_two + dot_nt(grad_gu, gu_w[j])
        branch = branch + dot_nt(act, down_w[j])
        gu_grads.append(dot_tn(normed_two, grad_gu))
        down_grads.append(dot_tn(cot_all, act))
    grad_normed_two = scatter_tokens(partial_two)
    second_part = jnp.sum(partial_two * normed_two.astype(F32), 0) / second_gain

    grad_hidden = cotangent.astype(F32) + norm_backward(
        unit_two, scale_two, second_gain, grad_normed_two
    )
    grad_low = grad_hidden.astype(BF16)
    hidden_grads = [across(grad_low, i, j) for i, j in SQUARE]
    mlp_low_own = jnp.concatenate([gu_grads[0], down_grads[0]], 1).astype(BF16)
    mlp_low_other = jnp.concatenate([gu_grads[1], down_grads[1]], 1).astype(BF16)
    mlp_picked = pick(mlp_low_own, core_swap(mlp_low_other), where)
    mlp_chain = chain_first(mlp_picked)
    hidden_grads = lax.optimization_barrier((hidden_grads, mlp_picked))[0]
    grad_query, back_own, back_other = call(
        attend_back_kernel,
        [((512, 512), F32), ((512, 512), F32), ((512, 512), BF16)],
        meta,
        *hidden_grads,
        *out_w,
        query,
        keys,
        vals,
        probs_low,
        probs_high,
        smem=1,
        scratch=[((512, 512), BF16), ((2, 1024, 128), F32), ((2, 1024, 128), F32)],
    )
    hidden_grad = jnp.concatenate(after(hidden_grads, grad_query), 0)
    out_grads = [dot_tn(hidden_grad, attended[:, j * 256 : (j + 1) * 256]).astype(BF16) for j in range(2)]
    mlp_low = chain_second(*mlp_chain)
    back_own = after(back_own, *mlp_chain)
    *grad_raws, mine, piece_1, piece_2, piece_3 = call(
        tail_kernel,
        [((512, 512), BF16)] * 2 + [((272, 1024), F32)] + [((272, 1024), BF16)] * 3,
        grad_query,
        back_own,
        core_swap(back_other),
        *raws,
        cosine,
        sine,
        jnp.stack([query_gain, key_gain]),
        *attn_w,
        *pieces,
        branch,
        second_part[None, :],
        first_gain[None, :],
        scratch=[(block, F32)],
    )
    attn_grads = [dot_tn(normed_one, after(grad_raws[j], piece_1)).astype(BF16) for j in range(2)]
    attn_grads = [jnp.concatenate([a, b], 1) for a, b in zip(attn_grads, out_grads)]
    got = [across(p, *SQUARE[s + 1]) for s, p in enumerate((piece_1, piece_2, piece_3))]
    got = [p.astype(F32) for p in got]
    total = (mine + got[0]) + (got[1] + got[2])
    attn_swapped = core_swap(attn_grads[1])
    attn_picked = pick(attn_grads[0], attn_swapped, where)
    attn_chain = chain_first([after(p, mlp_low) for p in attn_picked])
    attn_low = chain_second(*attn_chain)
    sums = total[256:264]
    sums = (sums + core_swap(sums)).astype(BF16)
    sums = jnp.pad(sums, ((0, 8), (0, 128)))
    grad_tokens = grad_hidden + norm_backward(unit_one, scale_one, first_gain, total[:128])
    layer_out = hidden + total[128:256]
    results = jnp.concatenate([grad_tokens.astype(BF16), layer_out.astype(BF16)], 0)
    results = remap_back(after(results, *attn_chain[1:]))
    mlp_low = after(mlp_low, *attn_chain[1:])
    rest = [
        shard_home(jnp.concatenate([mlp_low[k], sums], 0), *SQUARE[k]).astype(F32) for k in range(4)
    ]
    rest = (rest[0] + rest[1]) + (rest[2] + rest[3])
    mlp_owned = rest[:64]
    sums = rest[64:67, :1024]
    got = [ring(sums, "z", s) for s in (1, 2, 3)]
    sums = (sums + got[1]) + (got[0] + got[2])
    attn_owned = scatter_home(attn_low)
    attn_owned, out_owned = attn_owned[:, :512], attn_owned[:, 512:]
    layer_out, grad_tokens = results[128:], results[:128]
    return (
        layer_out,
        grad_tokens,
        sums[0],
        sums[2, :128],
        sums[2, 128:256],
        attn_owned[:, :256],
        attn_owned[:, 256:384],
        attn_owned[:, 384:],
        out_owned.T,
        sums[1],
        mlp_owned[:, :384],
        mlp_owned[:, 384:768],
        mlp_owned[:, 768:].T,
    )


def solution(mesh):
    fine = Mesh(mesh.devices.reshape(4, 2, 2, 4, 2), ("z", "h", "c", "y", "l"))
    dp, tensor = ("z", "h", "c"), ("y", "l")
    rows, cols, trans = P(dp + tensor, None), P(dp, tensor), P(tensor, dp)
    in_specs = (
        rows, P(dp, None), P(), P(), P(), cols, cols, cols, trans, P(), cols, cols, trans, rows,
    )
    out_specs = (rows, rows, P(), P(), P(), cols, cols, cols, trans, P(), cols, cols, trans)
    return jax.shard_map(
        per_device, mesh=fine, in_specs=in_specs, out_specs=out_specs, check_vma=False
    )
```

```python
import jax
import jax.numpy as jnp
from jax import lax
from jax.experimental import pallas as pl
from jax.experimental.pallas import tpu as pltpu
from jax.sharding import Mesh
from jax.sharding import PartitionSpec as P

EPSILON = 1e-06
ROPE_BASE = 1000000.0
NEG_LARGE = -1e30
BF16 = jnp.bfloat16
F32 = jnp.float32
SQUARE = ((0, 0), (0, 1), (1, 0), (1, 1))


def place_of(y, pair):
    return y if y // 2 == pair else 3 - y


def remap_pairs():
    pairs = []
    for c in range(2):
        for y in range(4):
            for l in range(2):
                pairs.append(((c * 4 + y) * 2 + l, ((y % 2) * 4 + place_of(y, c)) * 2 + l))
    return pairs


def remap(value):
    return lax.ppermute(value, ("c", "y", "l"), remap_pairs())


def remap_back(value):
    return lax.ppermute(value, ("c", "y", "l"), [(b, a) for a, b in remap_pairs()])


def shard_pairs(a, b):
    pairs = []
    for h in range(2):
        for c in range(2):
            for y in range(4):
                for l in range(2):
                    source = ((h * 2 + c) * 4 + y) * 2 + l
                    pairs.append((source, (((h ^ a) * 2 + y % 2) * 4 + place_of(y, c ^ b)) * 2 + l))
    return pairs


def shard_out(value, a, b):
    return lax.ppermute(value, ("h", "c", "y", "l"), shard_pairs(a, b))


def shard_home(value, a, b):
    return lax.ppermute(value, ("h", "c", "y", "l"), [(t, s) for s, t in shard_pairs(a, b)])


def ring(value, axis, step):
    return lax.ppermute(value, (axis,), [(i, (i + step) % 4) for i in range(4)])


def core_swap(value):
    return lax.ppermute(value, ("c",), [(0, 1), (1, 0)])


def across(value, i, j):
    if (i, j) == (0, 0):
        return value
    pairs = [(y * 2 + l, (y ^ i) * 2 + (l ^ j)) for y in range(4) for l in range(2)]
    return lax.ppermute(value, ("y", "l"), pairs)


def dot_nn(a, b):
    return lax.dot_general(a, b, (((1,), (0,)), ((), ())), preferred_element_type=F32)


def dot_nt(a, b):
    return lax.dot_general(a, b, (((1,), (1,)), ((), ())), preferred_element_type=F32)


def dot_tn(a, b):
    return lax.dot_general(a, b, (((0,), (0,)), ((), ())), preferred_element_type=F32)


def gather_tokens(block):
    return jnp.concatenate([across(block, i, j) for i, j in SQUARE], 0)


def scatter_tokens(partial):
    total = partial[:128]
    for s in (1, 2, 3):
        total = total + across(partial[s * 128 : (s + 1) * 128].astype(BF16), *SQUARE[s]).astype(F32)
    return total


def place_kernel(where, *refs):
    *parts, out = refs
    if len(parts) == 5:
        parts[2:4] = [(parts[2], parts[3])]
    for s in range(4):
        for k in range(4):
            at = ((where[0] + s) % 4) * 4 + (where[1] ^ k)
            block = parts[s][k // 2][k % 2] if isinstance(parts[s], tuple) else parts[s][k]
            out[pl.ds(pl.multiple_of(at * 64, 64), 64), :] = block


def pick_kernel(where, *refs):
    outs, pairs = refs[-4:], len(refs) // 2 - 2
    for s in range(4):
        for k in range(4):
            place = ((where[0] + s) % 4) * 4 + (where[1] ^ k)
            rows = pl.ds(pl.multiple_of(place * 64, 64), 64)
            at = 0
            for own, swapped in zip(refs[:pairs], refs[pairs : 2 * pairs]):
                total = own[rows, :].astype(F32) + swapped[rows, :].astype(F32)
                outs[s][k, :, at : at + own.shape[1]] = total.astype(BF16)
                at += own.shape[1]


def prep_kernel(*refs):
    if len(refs) == 12:
        weight, cosine, sine, gains = refs[4:8]
        query, kv, raw, joined = refs[8:]
        for s in range(4):
            joined[s * 128 : (s + 1) * 128, :] = refs[s][:128, :]
    else:
        joined, weight, cosine, sine, gains, query, kv, raw = refs
    value = dot_nn(joined[...], weight[:, :512])
    kv[:, 128:] = value[:, 384:].astype(BF16)
    raw[...] = value[:, :384]
    for i in range(3):
        cols = slice(i * 128, (i + 1) * 128)
        head = raw[:, cols]
        scale = lax.rsqrt(jnp.mean(head * head, -1, keepdims=True) + EPSILON)
        head = head * scale * gains[i // 2 : i // 2 + 1, :]
        head = (head * cosine[...] + rolled(head, sine[...])).astype(BF16)
        if i == 2:
            kv[:, :128] = head
        else:
            query[:, cols] = head


def attend_kernel(meta, *refs):
    queries, kv_own, kv_other, begin, index, out_w = refs[:2], refs[2:4], refs[4:6], refs[6], refs[7], refs[8:10]
    keys, values, probs_low, probs_high, attended = refs[10:15]
    pieces, total = refs[15:19], refs[19]
    for t in range(8):
        rows = pl.ds(pl.multiple_of(meta[3 + t] * 128, 128), 128)
        at = slice((t % 4) * 128, (t % 4 + 1) * 128)
        for j in range(2):
            source = kv_own[j] if t < 4 else kv_other[1 - j]
            keys[j, rows, :] = source[at, :128]
            values[j, rows, :] = source[at, 128:]
    for half, (count, probs) in enumerate(((512, probs_low), (768, probs_high))):
        rows = pl.ds(pl.multiple_of(meta[half], 256), 256)
        first = 0 if half == 0 else pl.multiple_of(meta[2], 256)
        place = first + lax.broadcasted_iota(jnp.int32, (256, count), 1)
        allowed = (place >= begin[rows, :]) & (place <= index[rows, :])
        for j in range(2):
            key = keys[j, pl.ds(first, count), :]
            value = values[j, pl.ds(first, count), :]
            for i in range(2):
                n = j * 2 + i
                scores = dot_nt(queries[j][rows, i * 128 : (i + 1) * 128], key) * 128 ** (-0.5)
                scores = jnp.where(allowed, scores, NEG_LARGE)
                exponent = jnp.exp(scores - jnp.max(scores, -1, keepdims=True))
                prob = exponent * (1.0 / jnp.sum(exponent, -1, keepdims=True))
                prob = prob.astype(BF16)
                probs[n] = prob
                attended[rows, n * 128 : (n + 1) * 128] = dot_nn(prob, value).astype(BF16)
    total[...] = dot_nt(attended[:, :256], out_w[0][:, 512:])
    total[...] += dot_nt(attended[:, 256:], out_w[1][:, 512:])
    for s in range(4):
        pieces[s][...] = total[s * 128 : (s + 1) * 128, :].astype(pieces[s].dtype)


def attend_back_kernel(meta, *refs):
    grads, out_w, queries = refs[:4], refs[4:6], refs[6:8]
    keys, values, probs_low, probs_high = refs[8:12]
    grad_query, back_own, back_other = refs[12:15]
    grad_out, grad_keys, grad_values, joined = refs[15:]
    for s in range(4):
        joined[s * 128 : (s + 1) * 128, :] = grads[s][...]
    for j in range(2):
        grad_out[:, j * 256 : j * 256 + 256] = dot_nn(joined[...], out_w[j][:, 512:]).astype(BF16)
    grad_keys[...] = jnp.zeros_like(grad_keys)
    grad_values[...] = jnp.zeros_like(grad_values)
    for half, (count, probs) in enumerate(((512, probs_low), (768, probs_high))):
        rows = pl.ds(pl.multiple_of(meta[half], 256), 256)
        first = 0 if half == 0 else pl.multiple_of(meta[2], 256)
        span = pl.ds(first, count)
        for j in range(2):
            key = keys[j, span, :]
            value = values[j, span, :]
            for i in range(2):
                n = j * 2 + i
                cols = slice(n * 128, (n + 1) * 128)
                grad = grad_out[rows, cols]
                prob = probs[n]
                wide = prob.astype(F32)
                grad_prob = dot_nt(grad, value)
                inner = jnp.sum(wide * grad_prob, -1, keepdims=True)
                grad_scores = (wide * (grad_prob - inner)).astype(BF16)
                grad_query[rows, cols] = dot_nn(grad_scores, key) * 128 ** (-0.5)
                grad_keys[j, span, :] += dot_tn(
                    grad_scores, queries[j][rows, i * 128 : (i + 1) * 128]
                ) * 128 ** (-0.5)
                grad_values[j, span, :] += dot_tn(prob, grad)
    for t in range(8):
        rows = pl.ds(pl.multiple_of(meta[3 + t] * 128, 128), 128)
        target = back_own if t < 4 else back_other
        at = slice((t % 4) * 128, (t % 4 + 1) * 128)
        for j in range(2):
            jj = j if t < 4 else 1 - j
            target[at, jj * 128 : jj * 128 + 128] = grad_keys[j, rows, :].astype(target.dtype)
            target[at, 256 + jj * 128 : 384 + jj * 128] = grad_values[j, rows, :].astype(target.dtype)


def rolled(values, sine):
    return pltpu.roll(values, 64, 1) * sine


def tail_kernel(*refs):
    (grad_query, back_own, swapped, raw_own, raw_other, cosine, sine, gains, weight_own, weight_other) = refs[:10]
    normed, branch, small, first_gain = refs[10:14]
    (low_own, low_other, mine, *pieces) = refs[14:20]
    partial = refs[20]
    sums = [0.0, 0.0]
    for j, (raw, low) in enumerate(((raw_own, low_own), (raw_other, low_other))):
        cols = slice(j * 128, (j + 1) * 128)
        grad_key = back_own[:, cols] + swapped[:, cols].astype(F32)
        cols = slice(256 + j * 128, 384 + j * 128)
        grad_value = back_own[:, cols] + swapped[:, cols].astype(F32)
        for i in range(3):
            cols = slice(i * 128, (i + 1) * 128)
            grad = grad_key if i == 2 else grad_query[:, (j * 2 + i) * 128 : (j * 2 + i + 1) * 128]
            grad = grad * cosine[...] - rolled(grad, sine[...])
            value = raw[:, cols]
            scale = lax.rsqrt(jnp.mean(value * value, -1, keepdims=True) + EPSILON)
            unit = value * scale
            sums[i // 2] = sums[i // 2] + jnp.sum(grad * unit, 0, keepdims=True)
            weighted = grad * gains[i // 2 : i // 2 + 1, :]
            back = scale * (weighted - unit * jnp.mean(unit * weighted, -1, keepdims=True))
            low[:, cols] = back.astype(BF16)
        low[:, 384:] = grad_value.astype(BF16)
    partial[...] = dot_nt(low_own[...], weight_own[:, :512])
    partial[...] += dot_nt(low_other[...], weight_other[:, :512])
    first = jnp.sum(partial[...] * normed[...].astype(F32), 0, keepdims=True)
    for s in range(4):
        rows = slice(s * 128, (s + 1) * 128)
        out = mine if s == 0 else pieces[s - 1]
        out[:128, :] = partial[rows, :].astype(out.dtype)
        out[128:256, :] = branch[rows, :].astype(out.dtype)
    gains_row = jnp.concatenate([sums[0], sums[1], jnp.zeros((1, 768), F32)], 1)
    block = jnp.concatenate(
        [first / first_gain[...], small[...], gains_row, jnp.zeros((13, 1024), F32)], 0
    ).astype(BF16)
    mine[256:, :] = block.astype(F32)
    for piece in pieces:
        piece[256:, :] = block


def pack_kernel(*refs):
    *shards, packed, done = refs
    copies, at = [], 0
    for n, ref in enumerate(shards):
        width = ref.shape[1]
        copies.append(pltpu.make_async_copy(ref, packed.at[:, at : at + width], done.at[n]))
        at += width
    for copy in copies:
        copy.start()
    for copy in copies:
        copy.wait()


def vmem(n):
    return [pl.BlockSpec(memory_space=pltpu.VMEM)] * n


SMEM = pl.BlockSpec(memory_space=pltpu.SMEM)
PARAMS = pltpu.CompilerParams(vmem_limit_bytes=48 * 1024 * 1024)


def after(value, *others):
    return lax.optimization_barrier((value, *others))[0]


def gather_stage(shard):
    return jnp.stack([shard_out(shard, a, b) for a, b in SQUARE])


def gather_near(stage):
    return stage, ring(stage, "z", -1), ring(stage, "z", 1)


def gather_far(stage, ahead, behind):
    return [stage, ahead, (ring(ahead[:2], "z", -1), ring(behind[2:], "z", 1)), behind]


def place(parts, where):
    width = parts[0].shape[2]
    parts = jax.tree.leaves(parts)
    return pl.pallas_call(
        place_kernel,
        out_shape=jax.ShapeDtypeStruct((1024, width), BF16),
        in_specs=[SMEM] + vmem(len(parts)),
        out_specs=vmem(1)[0],
        compiler_params=PARAMS,
    )(where, *parts)


def pick(owns, swaps, where):
    width = sum(v.shape[1] for v in owns)
    return call(pick_kernel, [((4, 64, width), BF16)] * 4, where, *owns, *swaps, smem=1)


def chain_first(parts):
    add = lambda a, b: (a.astype(F32) + b.astype(F32)).astype(BF16)
    up, down = ring(parts[2][:2], "z", 1), ring(parts[2][2:], "z", -1)
    ahead = jnp.concatenate([add(parts[1][:2], up), parts[1][2:]])
    behind = jnp.concatenate([parts[3][:2], add(parts[3][2:], down)])
    return parts[0], ahead, behind


def chain_second(own, ahead, behind):
    total = own.astype(F32) + ring(ahead, "z", 1).astype(F32) + ring(behind, "z", -1).astype(F32)
    return total.astype(BF16)


def scatter_home(low):
    result = 0.0
    for k in range(4):
        result = result + shard_home(low[k], *SQUARE[k]).astype(F32)
    return result


def call(kernel, shapes, *args, smem=0, scratch=()):
    return pl.pallas_call(
        kernel,
        out_shape=[jax.ShapeDtypeStruct(shape, kind) for shape, kind in shapes],
        in_specs=[SMEM] * smem + vmem(len(args) - smem),
        out_specs=vmem(len(shapes)),
        scratch_shapes=[pltpu.VMEM(shape, kind) for shape, kind in scratch],
        compiler_params=PARAMS,
    )(*args)


def pack(*shards):
    return pl.pallas_call(
        pack_kernel,
        out_shape=jax.ShapeDtypeStruct((64, sum(v.shape[1] for v in shards)), BF16),
        in_specs=[pl.BlockSpec(memory_space=pl.ANY)] * len(shards),
        out_specs=vmem(1)[0],
        scratch_shapes=[pltpu.SemaphoreType.DMA((len(shards),))],
    )(*shards)


def norm_forward(values):
    scale = lax.rsqrt(jnp.mean(values * values, -1, keepdims=True) + EPSILON)
    return values * scale, scale


def norm_backward(unit, scale, gain, grad):
    weighted = grad * gain
    return scale * (weighted - unit * jnp.mean(unit * weighted, -1, keepdims=True))


def per_device(
    tokens,
    segment_ids,
    first_gain,
    query_gain,
    key_gain,
    query_weight,
    key_weight,
    value_weight,
    out_weight,
    second_gain,
    gate_weight,
    up_weight,
    down_weight,
    cotangent,
):
    z, h, c = lax.axis_index("z"), lax.axis_index("h"), lax.axis_index("c")
    y, l = lax.axis_index("y"), lax.axis_index("l")
    where = jnp.stack([z, h * 2 + y // 2]).astype(jnp.int32)
    y_own = jnp.where(y % 2 == c, y, 3 - y)
    both = remap(jnp.concatenate([tokens, cotangent], 0))
    attn_stage = gather_stage(pack(query_weight, key_weight, value_weight, out_weight.T))
    attn_parts = gather_far(*gather_near(attn_stage))
    tokens, cotangent = both[:128], both[128:]
    seg_row = jnp.where(y // 2 == c, segment_ids, core_swap(segment_ids))[0]

    blocks = [(y_own ^ (2 * i)) * 2 + (l ^ j) for i, j in SQUARE]
    other_blocks = [((3 - y_own) ^ (2 * i)) * 2 + (l ^ j) for i, j in SQUARE]
    index = jnp.concatenate([b * 128 + jnp.arange(128, dtype=jnp.int32) for b in blocks])
    seg = jnp.concatenate([lax.dynamic_slice_in_dim(seg_row, b * 128, 128, 0) for b in blocks])
    begin = jnp.zeros((512,), jnp.int32)
    for v in range(1, 4):
        begin = begin + jnp.where(seg == v, jnp.sum((seg_row < v).astype(jnp.int32)), 0)
    places = (index - begin).astype(F32)
    inverse = ROPE_BASE ** (-jnp.arange(0, 128, 2, dtype=F32) / 128)
    phases = places[:, None] * inverse[None, :]
    cosine, sine = jnp.cos(phases), jnp.sin(phases)
    cosine = jnp.concatenate([cosine, cosine], -1)
    sine = jnp.concatenate([-sine, sine], -1)
    upper = y_own // 2
    meta = jnp.stack([upper * 256, (1 - upper) * 256, (y_own % 2) * 256] + blocks + other_blocks)
    meta = meta.astype(jnp.int32)

    input_float = tokens.astype(F32)
    unit_one, scale_one = norm_forward(input_float)
    pieces = jnp.concatenate([(unit_one * first_gain).astype(BF16), cotangent], 0)
    pieces = [across(pieces, i, j) for i, j in SQUARE]
    begin, index = begin[:, None], index[:, None]
    attn_parts = lax.optimization_barrier((attn_parts, pieces, cosine, sine, begin, index))[0]
    attn_own = place(attn_parts, where)
    attn_other = core_swap(attn_own)
    attn_w = [attn_own, attn_other]
    pair_gains = jnp.stack([query_gain, key_gain])
    shapes = [((512, 256), BF16)] * 2 + [((512, 384), F32)]
    query_0, kv_0, raw_0, normed_one = call(
        prep_kernel, shapes + [((512, 1024), BF16)], *pieces, attn_own, cosine, sine, pair_gains
    )
    mlp_shard = pack(gate_weight, up_weight, down_weight.T)
    mlp_stage = gather_stage(after(mlp_shard, query_0))
    query_1, kv_1, raw_1 = call(
        prep_kernel, shapes, normed_one, attn_other, cosine, sine, pair_gains
    )
    block = (128, 1024)
    keys, vals, probs_low, probs_high, attended, *parts = call(
        attend_kernel,
        [((2, 1024, 128), BF16)] * 2
        + [((4, 256, 512), BF16), ((4, 256, 768), BF16), ((512, 512), BF16), (block, F32)]
        + [(block, BF16)] * 3,
        meta,
        query_0,
        query_1,
        kv_0,
        kv_1,
        core_swap(kv_0),
        core_swap(kv_1),
        begin,
        index,
        *attn_w,
        smem=1,
        scratch=[((512, 1024), F32)],
    )
    cot_all = jnp.concatenate([p[128:] for p in lax.optimization_barrier((pieces, attended))[0]], 0)
    mlp_parts = gather_far(*gather_near(after(mlp_stage, attended)))
    got = [across(parts[s], *SQUARE[s]) for s in (1, 2, 3)]
    mlp_parts = lax.optimization_barrier((mlp_parts, got))[0]
    mlp_own = place(mlp_parts, where)
    mlp_w = [mlp_own, core_swap(mlp_own)]
    gu_w = [w[:, :768] for w in mlp_w]
    down_w = [w[:, 768:] for w in mlp_w]
    hidden = input_float + parts[0]
    for value in got:
        hidden = hidden + value.astype(F32)

    unit_two, scale_two = norm_forward(hidden)
    normed_two = gather_tokens((unit_two * second_gain).astype(BF16))
    partial_two, acts, grad_gus = 0.0, [], []
    for j in range(2):
        gate_up = dot_nn(normed_two, gu_w[j])
        gate, up = gate_up[:, :384], gate_up[:, 384:]
        sig = jax.nn.sigmoid(gate)
        silu = gate * sig
        act = (silu * up).astype(BF16)
        grad_act = dot_nn(cot_all, down_w[j])
        grad_gate = (grad_act * up * (sig + silu * (1.0 - sig))).astype(BF16)
        grad_up = (grad_act * silu).astype(BF16)
        grad_gu = jnp.concatenate([grad_gate, grad_up], 1)
        partial_two = partial_two + dot_nt(grad_gu, gu_w[j])
        acts.append(act)
        grad_gus.append(grad_gu)
    grad_normed_two = scatter_tokens(partial_two)
    acts, grad_gus = lax.optimization_barrier((acts, grad_gus, partial_two))[:2]
    mlp_grads = [
        jnp.concatenate([dot_tn(normed_two, grad_gus[j]), dot_tn(cot_all, acts[j])], 1).astype(BF16)
        for j in range(2)
    ]
    branch = dot_nt(acts[0], down_w[0]) + dot_nt(acts[1], down_w[1])
    second_part = jnp.sum(partial_two * normed_two.astype(F32), 0) / second_gain

    grad_hidden = cotangent.astype(F32) + norm_backward(
        unit_two, scale_two, second_gain, grad_normed_two
    )
    grad_low = grad_hidden.astype(BF16)
    hidden_grads = [across(grad_low, i, j) for i, j in SQUARE]
    mlp_picked = pick(mlp_grads[:1], [core_swap(mlp_grads[1])], where)
    mlp_chain = chain_first(mlp_picked)
    mlp_low = chain_second(*mlp_chain)
    hidden_grads = lax.optimization_barrier((hidden_grads, mlp_picked))[0]
    grad_query, back_own, back_other = call(
        attend_back_kernel,
        [((512, 512), F32), ((512, 512), F32), ((512, 512), BF16)],
        meta,
        *hidden_grads,
        *attn_w,
        query_0,
        query_1,
        keys,
        vals,
        probs_low,
        probs_high,
        smem=1,
        scratch=[
            ((512, 512), BF16),
            ((2, 1024, 128), F32),
            ((2, 1024, 128), F32),
            ((512, 1024), BF16),
        ],
    )
    *grad_raws, mine, piece_1, piece_2, piece_3 = call(
        tail_kernel,
        [((512, 512), BF16)] * 2 + [((272, 1024), F32)] + [((272, 1024), BF16)] * 3,
        grad_query,
        back_own,
        core_swap(back_other),
        raw_0,
        raw_1,
        cosine,
        sine,
        pair_gains,
        *attn_w,
        normed_one,
        branch,
        second_part[None, :],
        first_gain[None, :],
        scratch=[((512, 1024), F32)],
    )
    hidden_grad = jnp.concatenate(lax.optimization_barrier((hidden_grads, piece_1))[0], 0)
    attn_grads = [
        jnp.concatenate(
            [
                dot_tn(normed_one, after(grad_raws[j], piece_1)).astype(BF16),
                dot_tn(hidden_grad, attended[:, j * 256 : (j + 1) * 256]).astype(BF16),
            ],
            1,
        )
        for j in range(2)
    ]
    got = [across(p, *SQUARE[s + 1]) for s, p in enumerate((piece_1, piece_2, piece_3))]
    attn_swapped = core_swap(attn_grads[1])
    attn_picked = pick(attn_grads[:1], [attn_swapped], where)
    got = [p.astype(F32) for p in lax.optimization_barrier((got, attn_picked))[0]]
    total = (mine + got[0]) + (got[1] + got[2])
    attn_chain = chain_first(lax.optimization_barrier((attn_picked, mlp_chain[1:]))[0])
    attn_low = chain_second(*attn_chain)
    sums = total[256:264]
    sums = (sums + core_swap(sums)).astype(BF16)
    sums = jnp.pad(sums, ((0, 8), (0, 128)))
    grad_tokens = grad_hidden + norm_backward(unit_one, scale_one, first_gain, total[:128])
    layer_out = hidden + total[128:256]
    results = jnp.concatenate([grad_tokens.astype(BF16), layer_out.astype(BF16)], 0)
    results = remap_back(after(results, *attn_chain[1:]))
    mlp_low = after(mlp_low, *attn_chain[1:])
    rest = [
        shard_home(jnp.concatenate([mlp_low[k], sums], 0), *SQUARE[k]).astype(F32) for k in range(4)
    ]
    rest = (rest[0] + rest[1]) + (rest[2] + rest[3])
    mlp_owned = rest[:64]
    sums = rest[64:67, :1024]
    got = [ring(sums, "z", s) for s in (1, 2, 3)]
    sums = (sums + got[1]) + (got[0] + got[2])
    attn_owned = scatter_home(attn_low)
    attn_owned, out_owned = attn_owned[:, :512], attn_owned[:, 512:]
    layer_out, grad_tokens = results[128:], results[:128]
    return (
        layer_out,
        grad_tokens,
        sums[0],
        sums[2, :128],
        sums[2, 128:256],
        attn_owned[:, :256],
        attn_owned[:, 256:384],
        attn_owned[:, 384:],
        out_owned.T,
        sums[1],
        mlp_owned[:, :384],
        mlp_owned[:, 384:768],
        mlp_owned[:, 768:].T,
    )


def solution(mesh):
    fine = Mesh(mesh.devices.reshape(4, 2, 2, 4, 2), ("z", "h", "c", "y", "l"))
    dp, tensor = ("z", "h", "c"), ("y", "l")
    rows, cols, trans = P(dp + tensor, None), P(dp, tensor), P(tensor, dp)
    in_specs = (
        rows, P(dp, None), P(), P(), P(), cols, cols, cols, trans, P(), cols, cols, trans, rows,
    )
    out_specs = (rows, rows, P(), P(), P(), cols, cols, cols, trans, P(), cols, cols, trans)
    return jax.shard_map(
        per_device, mesh=fine, in_specs=in_specs, out_specs=out_specs, check_vma=False
    )
```

```python
import jax
import jax.numpy as jnp
from jax import lax
from jax.experimental import pallas as pl
from jax.experimental.pallas import tpu as pltpu
from jax.sharding import Mesh
from jax.sharding import PartitionSpec as P

EPSILON = 1e-06
ROPE_BASE = 1000000.0
NEG_LARGE = -1e30
BF16 = jnp.bfloat16
F32 = jnp.float32
SQUARE = ((0, 0), (0, 1), (1, 0), (1, 1))


def place_of(y, pair):
    return y if y // 2 == pair else 3 - y


def remap_pairs():
    pairs = []
    for c in range(2):
        for y in range(4):
            for l in range(2):
                pairs.append(((c * 4 + y) * 2 + l, ((y % 2) * 4 + place_of(y, c)) * 2 + l))
    return pairs


def remap(value):
    return lax.ppermute(value, ("c", "y", "l"), remap_pairs())


def remap_back(value):
    return lax.ppermute(value, ("c", "y", "l"), [(b, a) for a, b in remap_pairs()])


def shard_pairs(a, b):
    pairs = []
    for h in range(2):
        for c in range(2):
            for y in range(4):
                for l in range(2):
                    source = ((h * 2 + c) * 4 + y) * 2 + l
                    pairs.append((source, (((h ^ a) * 2 + y % 2) * 4 + place_of(y, c ^ b)) * 2 + l))
    return pairs


def shard_out(value, a, b):
    return lax.ppermute(value, ("h", "c", "y", "l"), shard_pairs(a, b))


def shard_home(value, a, b):
    return lax.ppermute(value, ("h", "c", "y", "l"), [(t, s) for s, t in shard_pairs(a, b)])


def ring(value, axis, step):
    return lax.ppermute(value, (axis,), [(i, (i + step) % 4) for i in range(4)])


def core_swap(value):
    return lax.ppermute(value, ("c",), [(0, 1), (1, 0)])


def across(value, i, j):
    if (i, j) == (0, 0):
        return value
    pairs = [(y * 2 + l, (y ^ i) * 2 + (l ^ j)) for y in range(4) for l in range(2)]
    return lax.ppermute(value, ("y", "l"), pairs)


def dot_nn(a, b):
    return lax.dot_general(a, b, (((1,), (0,)), ((), ())), preferred_element_type=F32)


def dot_nt(a, b):
    return lax.dot_general(a, b, (((1,), (1,)), ((), ())), preferred_element_type=F32)


def dot_tn(a, b):
    return lax.dot_general(a, b, (((0,), (0,)), ((), ())), preferred_element_type=F32)


def gather_tokens(block):
    return jnp.concatenate([across(block, i, j) for i, j in SQUARE], 0)


def scatter_tokens(partial):
    total = partial[:128]
    for s in (1, 2, 3):
        total = total + across(partial[s * 128 : (s + 1) * 128].astype(BF16), *SQUARE[s]).astype(F32)
    return total


def place_kernel(where, *refs):
    *parts, out = refs
    if len(parts) == 5:
        parts[2:4] = [(parts[2], parts[3])]
    for s in range(4):
        for k in range(4):
            at = ((where[0] + s) % 4) * 4 + (where[1] ^ k)
            block = parts[s][k // 2][k % 2] if isinstance(parts[s], tuple) else parts[s][k]
            out[pl.ds(pl.multiple_of(at * 64, 64), 64), :] = block


def pick_kernel(where, *refs):
    outs, pairs = refs[-4:], len(refs) // 2 - 2
    for s in range(4):
        for k in range(4):
            place = ((where[0] + s) % 4) * 4 + (where[1] ^ k)
            rows = pl.ds(pl.multiple_of(place * 64, 64), 64)
            at = 0
            for own, swapped in zip(refs[:pairs], refs[pairs : 2 * pairs]):
                total = own[rows, :].astype(F32) + swapped[rows, :].astype(F32)
                outs[s][k, :, at : at + own.shape[1]] = total.astype(BF16)
                at += own.shape[1]


def prep_kernel(*refs):
    if len(refs) == 12:
        weight, cosine, sine, gains = refs[4:8]
        query, kv, raw, joined = refs[8:]
        for s in range(4):
            joined[s * 128 : (s + 1) * 128, :] = refs[s][:128, :]
    else:
        joined, weight, cosine, sine, gains, query, kv, raw = refs
    value = dot_nn(joined[...], weight[:, :512])
    kv[:, 128:] = value[:, 384:].astype(BF16)
    raw[...] = value[:, :384]
    for i in range(3):
        cols = slice(i * 128, (i + 1) * 128)
        head = raw[:, cols]
        scale = lax.rsqrt(jnp.mean(head * head, -1, keepdims=True) + EPSILON)
        head = head * scale * gains[i // 2 : i // 2 + 1, :]
        head = (head * cosine[...] + rolled(head, sine[...])).astype(BF16)
        if i == 2:
            kv[:, :128] = head
        else:
            query[:, cols] = head


def attend_kernel(meta, *refs):
    queries, kv_own, kv_other, begin, index, out_w = refs[:2], refs[2:4], refs[4:6], refs[6], refs[7], refs[8:10]
    keys, values, probs_low, probs_high, attended = refs[10:15]
    pieces, total = refs[15:19], refs[19]
    for t in range(8):
        rows = pl.ds(pl.multiple_of(meta[3 + t] * 128, 128), 128)
        at = slice((t % 4) * 128, (t % 4 + 1) * 128)
        for j in range(2):
            source = kv_own[j] if t < 4 else kv_other[1 - j]
            keys[j, rows, :] = source[at, :128]
            values[j, rows, :] = source[at, 128:]
    for half, (count, probs) in enumerate(((512, probs_low), (768, probs_high))):
        rows = pl.ds(pl.multiple_of(meta[half], 256), 256)
        first = 0 if half == 0 else pl.multiple_of(meta[2], 256)
        place = first + lax.broadcasted_iota(jnp.int32, (256, count), 1)
        allowed = (place >= begin[rows, :]) & (place <= index[rows, :])
        for j in range(2):
            key = keys[j, pl.ds(first, count), :]
            value = values[j, pl.ds(first, count), :]
            for i in range(2):
                n = j * 2 + i
                scores = dot_nt(queries[j][rows, i * 128 : (i + 1) * 128], key) * 128 ** (-0.5)
                scores = jnp.where(allowed, scores, NEG_LARGE)
                exponent = jnp.exp(scores - jnp.max(scores, -1, keepdims=True))
                prob = exponent * (1.0 / jnp.sum(exponent, -1, keepdims=True))
                prob = prob.astype(BF16)
                probs[n] = prob
                attended[rows, n * 128 : (n + 1) * 128] = dot_nn(prob, value).astype(BF16)
    total[...] = dot_nt(attended[:, :256], out_w[0][:, 512:])
    total[...] += dot_nt(attended[:, 256:], out_w[1][:, 512:])
    for s in range(4):
        pieces[s][...] = total[s * 128 : (s + 1) * 128, :].astype(pieces[s].dtype)


def attend_back_kernel(meta, *refs):
    grads, out_w, queries = refs[:4], refs[4:6], refs[6:8]
    keys, values, probs_low, probs_high = refs[8:12]
    grad_query, back_own, back_other = refs[12:15]
    grad_out, grad_keys, grad_values, joined = refs[15:]
    for s in range(4):
        joined[s * 128 : (s + 1) * 128, :] = grads[s][...]
    for j in range(2):
        grad_out[:, j * 256 : j * 256 + 256] = dot_nn(joined[...], out_w[j][:, 512:]).astype(BF16)
    grad_keys[...] = jnp.zeros_like(grad_keys)
    grad_values[...] = jnp.zeros_like(grad_values)
    for half, (count, probs) in enumerate(((512, probs_low), (768, probs_high))):
        rows = pl.ds(pl.multiple_of(meta[half], 256), 256)
        first = 0 if half == 0 else pl.multiple_of(meta[2], 256)
        span = pl.ds(first, count)
        for j in range(2):
            key = keys[j, span, :]
            value = values[j, span, :]
            for i in range(2):
                n = j * 2 + i
                cols = slice(n * 128, (n + 1) * 128)
                grad = grad_out[rows, cols]
                prob = probs[n]
                wide = prob.astype(F32)
                grad_prob = dot_nt(grad, value)
                inner = jnp.sum(wide * grad_prob, -1, keepdims=True)
                grad_scores = (wide * (grad_prob - inner)).astype(BF16)
                grad_query[rows, cols] = dot_nn(grad_scores, key) * 128 ** (-0.5)
                grad_keys[j, span, :] += dot_tn(
                    grad_scores, queries[j][rows, i * 128 : (i + 1) * 128]
                ) * 128 ** (-0.5)
                grad_values[j, span, :] += dot_tn(prob, grad)
    for t in range(8):
        rows = pl.ds(pl.multiple_of(meta[3 + t] * 128, 128), 128)
        target = back_own if t < 4 else back_other
        at = slice((t % 4) * 128, (t % 4 + 1) * 128)
        for j in range(2):
            jj = j if t < 4 else 1 - j
            target[at, jj * 128 : jj * 128 + 128] = grad_keys[j, rows, :].astype(target.dtype)
            target[at, 256 + jj * 128 : 384 + jj * 128] = grad_values[j, rows, :].astype(target.dtype)


def rolled(values, sine):
    return pltpu.roll(values, 64, 1) * sine


def tail_kernel(*refs):
    (grad_query, back_own, swapped, raw_own, raw_other, cosine, sine, gains, weight_own, weight_other) = refs[:10]
    normed, small, first_gain = refs[10:13]
    (low_own, low_other, mine, *pieces) = refs[13:19]
    partial = refs[19]
    sums = [0.0, 0.0]
    for j, (raw, low) in enumerate(((raw_own, low_own), (raw_other, low_other))):
        cols = slice(j * 128, (j + 1) * 128)
        grad_key = back_own[:, cols] + swapped[:, cols].astype(F32)
        cols = slice(256 + j * 128, 384 + j * 128)
        grad_value = back_own[:, cols] + swapped[:, cols].astype(F32)
        for i in range(3):
            cols = slice(i * 128, (i + 1) * 128)
            grad = grad_key if i == 2 else grad_query[:, (j * 2 + i) * 128 : (j * 2 + i + 1) * 128]
            grad = grad * cosine[...] - rolled(grad, sine[...])
            value = raw[:, cols]
            scale = lax.rsqrt(jnp.mean(value * value, -1, keepdims=True) + EPSILON)
            unit = value * scale
            sums[i // 2] = sums[i // 2] + jnp.sum(grad * unit, 0, keepdims=True)
            weighted = grad * gains[i // 2 : i // 2 + 1, :]
            back = scale * (weighted - unit * jnp.mean(unit * weighted, -1, keepdims=True))
            low[:, cols] = back.astype(BF16)
        low[:, 384:] = grad_value.astype(BF16)
    partial[...] = dot_nt(low_own[...], weight_own[:, :512])
    partial[...] += dot_nt(low_other[...], weight_other[:, :512])
    first = jnp.sum(partial[...] * normed[...].astype(F32), 0, keepdims=True)
    for s in range(4):
        rows = slice(s * 128, (s + 1) * 128)
        out = mine if s == 0 else pieces[s - 1]
        out[:128, :] = partial[rows, :].astype(out.dtype)
    gains_row = jnp.concatenate([sums[0], sums[1], jnp.zeros((1, 768), F32)], 1)
    block = jnp.concatenate(
        [first / first_gain[...], small[...], gains_row, jnp.zeros((13, 1024), F32)], 0
    ).astype(BF16)
    mine[128:, :] = block.astype(F32)
    for piece in pieces:
        piece[128:, :] = block


def pack_kernel(*refs):
    *shards, packed, done = refs
    copies, at = [], 0
    for n, ref in enumerate(shards):
        width = ref.shape[1]
        copies.append(pltpu.make_async_copy(ref, packed.at[:, at : at + width], done.at[n]))
        at += width
    for copy in copies:
        copy.start()
    for copy in copies:
        copy.wait()


def vmem(n):
    return [pl.BlockSpec(memory_space=pltpu.VMEM)] * n


SMEM = pl.BlockSpec(memory_space=pltpu.SMEM)
PARAMS = pltpu.CompilerParams(vmem_limit_bytes=48 * 1024 * 1024)


def after(value, *others):
    return lax.optimization_barrier((value, *others))[0]


def gather_stage(shard):
    return jnp.stack([shard_out(shard, a, b) for a, b in SQUARE])


def gather_near(stage):
    return stage, ring(stage, "z", -1), ring(stage, "z", 1)


def gather_far(stage, ahead, behind):
    return [stage, ahead, (ring(ahead[:2], "z", -1), ring(behind[2:], "z", 1)), behind]


def place(parts, where):
    width = parts[0].shape[2]
    parts = jax.tree.leaves(parts)
    return pl.pallas_call(
        place_kernel,
        out_shape=jax.ShapeDtypeStruct((1024, width), BF16),
        in_specs=[SMEM] + vmem(len(parts)),
        out_specs=vmem(1)[0],
        compiler_params=PARAMS,
    )(where, *parts)


def pick(owns, swaps, where):
    width = sum(v.shape[1] for v in owns)
    return call(pick_kernel, [((4, 64, width), BF16)] * 4, where, *owns, *swaps, smem=1)


def chain_first(parts):
    add = lambda a, b: (a.astype(F32) + b.astype(F32)).astype(BF16)
    up, down = ring(parts[2][:2], "z", 1), ring(parts[2][2:], "z", -1)
    ahead = jnp.concatenate([add(parts[1][:2], up), parts[1][2:]])
    behind = jnp.concatenate([parts[3][:2], add(parts[3][2:], down)])
    return parts[0], ahead, behind


def chain_send(own, ahead, behind):
    return own, ring(ahead, "z", 1), ring(behind, "z", -1)


def chain_total(own, ahead, behind):
    return (own.astype(F32) + ahead.astype(F32) + behind.astype(F32)).astype(BF16)


def scatter_home(low):
    result = 0.0
    for k in range(4):
        result = result + shard_home(low[k], *SQUARE[k]).astype(F32)
    return result


def call(kernel, shapes, *args, smem=0, scratch=(), micros=1):
    return pl.pallas_call(
        kernel,
        out_shape=[jax.ShapeDtypeStruct(shape, kind) for shape, kind in shapes],
        in_specs=[SMEM] * smem + vmem(len(args) - smem),
        out_specs=vmem(len(shapes)),
        scratch_shapes=[pltpu.VMEM(shape, kind) for shape, kind in scratch],
        compiler_params=PARAMS,
        cost_estimate=pl.CostEstimate(
            flops=micros * 10**9, bytes_accessed=micros * 3 * 10**6, transcendentals=0
        ),
    )(*args)


def pack(*shards):
    return pl.pallas_call(
        pack_kernel,
        out_shape=jax.ShapeDtypeStruct((64, sum(v.shape[1] for v in shards)), BF16),
        in_specs=[pl.BlockSpec(memory_space=pl.ANY)] * len(shards),
        out_specs=vmem(1)[0],
        scratch_shapes=[pltpu.SemaphoreType.DMA((len(shards),))],
    )(*shards)


def norm_forward(values):
    scale = lax.rsqrt(jnp.mean(values * values, -1, keepdims=True) + EPSILON)
    return values * scale, scale


def norm_backward(unit, scale, gain, grad):
    weighted = grad * gain
    return scale * (weighted - unit * jnp.mean(unit * weighted, -1, keepdims=True))


def per_device(
    tokens,
    segment_ids,
    first_gain,
    query_gain,
    key_gain,
    query_weight,
    key_weight,
    value_weight,
    out_weight,
    second_gain,
    gate_weight,
    up_weight,
    down_weight,
    cotangent,
):
    z, h, c = lax.axis_index("z"), lax.axis_index("h"), lax.axis_index("c")
    y, l = lax.axis_index("y"), lax.axis_index("l")
    where = jnp.stack([z, h * 2 + y // 2]).astype(jnp.int32)
    y_own = jnp.where(y % 2 == c, y, 3 - y)
    tokens = remap(tokens)
    attn_stage = gather_stage(pack(query_weight, key_weight, value_weight, out_weight.T))
    attn_parts = gather_far(*gather_near(attn_stage))
    segment_ids = after(segment_ids, attn_stage)
    seg_row = jnp.where(y // 2 == c, segment_ids, core_swap(segment_ids))[0]

    blocks = [(y_own ^ (2 * i)) * 2 + (l ^ j) for i, j in SQUARE]
    other_blocks = [((3 - y_own) ^ (2 * i)) * 2 + (l ^ j) for i, j in SQUARE]
    index = jnp.concatenate([b * 128 + jnp.arange(128, dtype=jnp.int32) for b in blocks])
    seg = jnp.concatenate([lax.dynamic_slice_in_dim(seg_row, b * 128, 128, 0) for b in blocks])
    begin = jnp.zeros((512,), jnp.int32)
    for v in range(1, 4):
        begin = begin + jnp.where(seg == v, jnp.sum((seg_row < v).astype(jnp.int32)), 0)
    places = (index - begin).astype(F32)
    inverse = ROPE_BASE ** (-jnp.arange(0, 128, 2, dtype=F32) / 128)
    phases = places[:, None] * inverse[None, :]
    cosine, sine = jnp.cos(phases), jnp.sin(phases)
    cosine = jnp.concatenate([cosine, cosine], -1)
    sine = jnp.concatenate([-sine, sine], -1)
    upper = y_own // 2
    meta = jnp.stack([upper * 256, (1 - upper) * 256, (y_own % 2) * 256] + blocks + other_blocks)
    meta = meta.astype(jnp.int32)

    input_float = tokens.astype(F32)
    unit_one, scale_one = norm_forward(input_float)
    own_piece = (unit_one * first_gain).astype(BF16)
    pieces = [across(own_piece, i, j) for i, j in SQUARE]
    mlp_shard = pack(gate_weight, up_weight, down_weight.T)
    begin, index = begin[:, None], index[:, None]
    attn_parts, mlp_shard = lax.optimization_barrier(
        (attn_parts, mlp_shard, pieces, cosine, sine, begin, index)
    )[:2]
    attn_own = place(attn_parts, where)
    attn_other = core_swap(attn_own)
    attn_w = [attn_own, attn_other]
    pair_gains = jnp.stack([query_gain, key_gain])
    shapes = [((512, 256), BF16)] * 2 + [((512, 384), F32)]
    query_0, kv_0, raw_0, normed_one = call(
        prep_kernel, shapes + [((512, 1024), BF16)], *pieces, attn_own, cosine, sine, pair_gains, micros=4
    )
    mlp_stage = gather_stage(mlp_shard)
    query_1, kv_1, raw_1 = call(
        prep_kernel, shapes, normed_one, attn_other, cosine, sine, pair_gains, micros=3
    )
    cotangent = remap(after(cotangent, *pieces))
    cot_pieces = [across(cotangent, i, j) for i, j in SQUARE]
    block = (128, 1024)
    keys, vals, probs_low, probs_high, attended, *parts = call(
        attend_kernel,
        [((2, 1024, 128), BF16)] * 2
        + [((4, 256, 512), BF16), ((4, 256, 768), BF16), ((512, 512), BF16), (block, F32)]
        + [(block, BF16)] * 3,
        meta,
        query_0,
        query_1,
        kv_0,
        kv_1,
        core_swap(kv_0),
        core_swap(kv_1),
        begin,
        index,
        *attn_w,
        smem=1,
        scratch=[((512, 1024), F32)],
        micros=8,
    )
    mlp_near = gather_near(mlp_stage)
    got = [across(parts[s], *SQUARE[s]) for s in (1, 2, 3)]
    mlp_near, cot_pieces = lax.optimization_barrier((mlp_near, cot_pieces, got))[:2]
    cot_all = jnp.concatenate(cot_pieces, 0)
    mlp_parts = gather_far(*mlp_near)
    mlp_own = place(mlp_parts, where)
    mlp_w = [mlp_own, core_swap(mlp_own)]
    gu_w = [w[:, :768] for w in mlp_w]
    down_w = [w[:, 768:] for w in mlp_w]
    hidden = input_float + parts[0]
    for value in got:
        hidden = hidden + value.astype(F32)

    unit_two, scale_two = norm_forward(hidden)
    normed_two = gather_tokens((unit_two * second_gain).astype(BF16))
    partial_two, acts, grad_gus = 0.0, [], []
    for j in range(2):
        gate_up = dot_nn(normed_two, gu_w[j])
        gate, up = gate_up[:, :384], gate_up[:, 384:]
        sig = jax.nn.sigmoid(gate)
        silu = gate * sig
        act = (silu * up).astype(BF16)
        grad_act = dot_nn(cot_all, down_w[j])
        grad_gate = (grad_act * up * (sig + silu * (1.0 - sig))).astype(BF16)
        grad_up = (grad_act * silu).astype(BF16)
        grad_gu = jnp.concatenate([grad_gate, grad_up], 1)
        partial_two = partial_two + dot_nt(grad_gu, gu_w[j])
        acts.append(act)
        grad_gus.append(grad_gu)
    grad_normed_two = scatter_tokens(partial_two)
    acts, grad_gus = lax.optimization_barrier((acts, grad_gus, partial_two))[:2]
    mlp_grads = [
        jnp.concatenate([dot_tn(normed_two, grad_gus[j]), dot_tn(cot_all, acts[j])], 1).astype(BF16)
        for j in range(2)
    ]
    branch = dot_nt(acts[0], down_w[0]) + dot_nt(acts[1], down_w[1])
    second_part = jnp.sum(partial_two * normed_two.astype(F32), 0) / second_gain

    grad_hidden = cotangent.astype(F32) + norm_backward(
        unit_two, scale_two, second_gain, grad_normed_two
    )
    grad_low = grad_hidden.astype(BF16)
    hidden_grads = [across(grad_low, i, j) for i, j in SQUARE]
    mlp_picked = pick(mlp_grads[:1], [core_swap(mlp_grads[1])], where)
    mlp_chain = chain_first(mlp_picked)
    mlp_far = chain_send(*mlp_chain)
    hidden_grads = lax.optimization_barrier((hidden_grads, mlp_picked))[0]
    grad_query, back_own, back_other = call(
        attend_back_kernel,
        [((512, 512), F32), ((512, 512), F32), ((512, 512), BF16)],
        meta,
        *hidden_grads,
        *attn_w,
        query_0,
        query_1,
        keys,
        vals,
        probs_low,
        probs_high,
        smem=1,
        scratch=[
            ((512, 512), BF16),
            ((2, 1024, 128), F32),
            ((2, 1024, 128), F32),
            ((512, 1024), BF16),
        ],
        micros=8,
    )
    low_branch = branch.astype(BF16)
    branches = [
        across(low_branch[s * 128 : (s + 1) * 128], *SQUARE[s]) for s in (1, 2, 3)
    ]
    back_own, branches = lax.optimization_barrier((back_own, branches, mlp_chain[1:]))[:2]
    *grad_raws, mine, piece_1, piece_2, piece_3 = call(
        tail_kernel,
        [((512, 512), BF16)] * 2 + [((144, 1024), F32)] + [((144, 1024), BF16)] * 3,
        grad_query,
        back_own,
        core_swap(back_other),
        raw_0,
        raw_1,
        cosine,
        sine,
        pair_gains,
        *attn_w,
        normed_one,
        second_part[None, :],
        first_gain[None, :],
        scratch=[((512, 1024), F32)],
        micros=9,
    )
    hidden_grad = jnp.concatenate(lax.optimization_barrier((hidden_grads, piece_1))[0], 0)
    attn_grads = [
        jnp.concatenate(
            [
                dot_tn(normed_one, after(grad_raws[j], piece_1)).astype(BF16),
                dot_tn(hidden_grad, attended[:, j * 256 : (j + 1) * 256]).astype(BF16),
            ],
            1,
        )
        for j in range(2)
    ]
    got = [across(p, *SQUARE[s + 1]) for s, p in enumerate((piece_1, piece_2, piece_3))]
    attn_swapped = core_swap(attn_grads[1])
    attn_swapped, got = lax.optimization_barrier((attn_swapped, got))
    attn_picked = pick(attn_grads[:1], [attn_swapped], where)
    attn_chain = chain_first(lax.optimization_barrier((attn_picked, mlp_chain[1:]))[0])
    mlp_far = lax.optimization_barrier((mlp_far, attn_chain[1:]))[0]
    mlp_low = chain_total(*mlp_far)
    got = [p.astype(F32) for p in got]
    total = (mine + got[0]) + (got[1] + got[2])
    attn_far = chain_send(*attn_chain)
    attn_low = chain_total(*attn_far)
    sums = total[128:136]
    sums = (sums + core_swap(sums)).astype(BF16)
    sums = jnp.pad(sums, ((0, 8), (0, 128)))
    grad_tokens = grad_hidden + norm_backward(unit_one, scale_one, first_gain, total[:128])
    layer_out = hidden + branch[:128]
    for value in branches:
        layer_out = layer_out + value.astype(F32)
    results = jnp.concatenate([grad_tokens.astype(BF16), layer_out.astype(BF16)], 0)
    results = remap_back(after(results, *attn_far[1:]))
    rest = [
        shard_home(jnp.concatenate([mlp_low[k], sums], 0), *SQUARE[k]).astype(F32) for k in range(4)
    ]
    rest = (rest[0] + rest[1]) + (rest[2] + rest[3])
    mlp_owned = rest[:64]
    sums = rest[64:67, :1024]
    got = [ring(sums, "z", s) for s in (1, 2, 3)]
    sums = (sums + got[1]) + (got[0] + got[2])
    attn_owned = scatter_home(attn_low)
    attn_owned, out_owned = attn_owned[:, :512], attn_owned[:, 512:]
    layer_out, grad_tokens = results[128:], results[:128]
    return (
        layer_out,
        grad_tokens,
        sums[0],
        sums[2, :128],
        sums[2, 128:256],
        attn_owned[:, :256],
        attn_owned[:, 256:384],
        attn_owned[:, 384:],
        out_owned.T,
        sums[1],
        mlp_owned[:, :384],
        mlp_owned[:, 384:768],
        mlp_owned[:, 768:].T,
    )


def solution(mesh):
    fine = Mesh(mesh.devices.reshape(4, 2, 2, 4, 2), ("z", "h", "c", "y", "l"))
    dp, tensor = ("z", "h", "c"), ("y", "l")
    rows, cols, trans = P(dp + tensor, None), P(dp, tensor), P(tensor, dp)
    in_specs = (
        rows, P(dp, None), P(), P(), P(), cols, cols, cols, trans, P(), cols, cols, trans, rows,
    )
    out_specs = (rows, rows, P(), P(), P(), cols, cols, cols, trans, P(), cols, cols, trans)
    return jax.shard_map(
        per_device, mesh=fine, in_specs=in_specs, out_specs=out_specs, check_vma=False
    )
```

```python
import jax
import jax.numpy as jnp
from jax import lax
from jax.experimental import pallas as pl
from jax.experimental.pallas import tpu as pltpu
from jax.sharding import Mesh
from jax.sharding import PartitionSpec as P

EPSILON = 1e-06
ROPE_BASE = 1000000.0
NEG_LARGE = -1e30
BF16 = jnp.bfloat16
F32 = jnp.float32
SQUARE = ((0, 0), (0, 1), (1, 0), (1, 1))


def place_of(y, pair):
    return y if y // 2 == pair else 3 - y


def remap_pairs():
    pairs = []
    for c in range(2):
        for y in range(4):
            for l in range(2):
                pairs.append(((c * 4 + y) * 2 + l, ((y % 2) * 4 + place_of(y, c)) * 2 + l))
    return pairs


def remap(value):
    return lax.ppermute(value, ("c", "y", "l"), remap_pairs())


def remap_back(value):
    return lax.ppermute(value, ("c", "y", "l"), [(b, a) for a, b in remap_pairs()])


def shard_pairs(a, b):
    pairs = []
    for h in range(2):
        for c in range(2):
            for y in range(4):
                for l in range(2):
                    source = ((h * 2 + c) * 4 + y) * 2 + l
                    pairs.append((source, (((h ^ a) * 2 + y % 2) * 4 + place_of(y, c ^ b)) * 2 + l))
    return pairs


def shard_out(value, a, b):
    return lax.ppermute(value, ("h", "c", "y", "l"), shard_pairs(a, b))


def shard_home(value, a, b):
    return lax.ppermute(value, ("h", "c", "y", "l"), [(t, s) for s, t in shard_pairs(a, b)])


def ring(value, axis, step):
    return lax.ppermute(value, (axis,), [(i, (i + step) % 4) for i in range(4)])


def core_swap(value):
    return lax.ppermute(value, ("c",), [(0, 1), (1, 0)])


def across(value, i, j):
    if (i, j) == (0, 0):
        return value
    pairs = [(y * 2 + l, (y ^ i) * 2 + (l ^ j)) for y in range(4) for l in range(2)]
    return lax.ppermute(value, ("y", "l"), pairs)


def dot_nn(a, b):
    return lax.dot_general(a, b, (((1,), (0,)), ((), ())), preferred_element_type=F32)


def dot_nt(a, b):
    return lax.dot_general(a, b, (((1,), (1,)), ((), ())), preferred_element_type=F32)


def dot_tn(a, b):
    return lax.dot_general(a, b, (((0,), (0,)), ((), ())), preferred_element_type=F32)


def gather_tokens(block):
    return jnp.concatenate([across(block, i, j) for i, j in SQUARE], 0)


def scatter_tokens(partial):
    total = partial[:128]
    for s in (1, 2, 3):
        total = total + across(partial[s * 128 : (s + 1) * 128].astype(BF16), *SQUARE[s]).astype(F32)
    return total


def place_kernel(where, *refs):
    *parts, out = refs
    if len(parts) == 5:
        parts[2:4] = [(parts[2], parts[3])]
    for s in range(4):
        for k in range(4):
            at = ((where[0] + s) % 4) * 4 + (where[1] ^ k)
            block = parts[s][k // 2][k % 2] if isinstance(parts[s], tuple) else parts[s][k]
            out[pl.ds(pl.multiple_of(at * 64, 64), 64), :] = block


def pick_kernel(where, own, swapped, extra, *outs):
    for s in range(4):
        for k in range(4):
            at = ((where[0] + s) % 4) * 4 + (where[1] ^ k)
            rows = pl.ds(pl.multiple_of(at * 64, 64), 64)
            total = own[rows, :].astype(F32) + swapped[rows, :].astype(F32)
            outs[s][k * 64 : (k + 1) * 64, :] = total.astype(BF16)
        outs[s][256:, :] = extra[...]


def prep_kernel(*refs):
    if len(refs) == 12:
        weight, cosine, sine, gains = refs[4:8]
        query, kv, raw, joined = refs[8:]
        for s in range(4):
            joined[s * 128 : (s + 1) * 128, :] = refs[s][:128, :]
    else:
        joined, weight, cosine, sine, gains, query, kv, raw = refs
    value = dot_nn(joined[...], weight[:, :512])
    kv[:, 128:] = value[:, 384:].astype(BF16)
    raw[...] = value[:, :384]
    for i in range(3):
        cols = slice(i * 128, (i + 1) * 128)
        head = raw[:, cols]
        scale = lax.rsqrt(jnp.mean(head * head, -1, keepdims=True) + EPSILON)
        head = head * scale * gains[i // 2 : i // 2 + 1, :]
        head = (head * cosine[...] + rolled(head, sine[...])).astype(BF16)
        if i == 2:
            kv[:, :128] = head
        else:
            query[:, cols] = head


def attend_kernel(meta, *refs):
    queries, kv_own, kv_other, begin, index, out_w = refs[:2], refs[2:4], refs[4:6], refs[6], refs[7], refs[8:10]
    keys, values, probs_low, probs_high, attended = refs[10:15]
    pieces, total = refs[15:19], refs[19]
    for t in range(8):
        rows = pl.ds(pl.multiple_of(meta[3 + t] * 128, 128), 128)
        at = slice((t % 4) * 128, (t % 4 + 1) * 128)
        for j in range(2):
            source = kv_own[j] if t < 4 else kv_other[1 - j]
            keys[j, rows, :] = source[at, :128]
            values[j, rows, :] = source[at, 128:]
    for half, (count, probs) in enumerate(((512, probs_low), (768, probs_high))):
        rows = pl.ds(pl.multiple_of(meta[half], 256), 256)
        first = 0 if half == 0 else pl.multiple_of(meta[2], 256)
        place = first + lax.broadcasted_iota(jnp.int32, (256, count), 1)
        allowed = (place >= begin[rows, :]) & (place <= index[rows, :])
        for j in range(2):
            key = keys[j, pl.ds(first, count), :]
            value = values[j, pl.ds(first, count), :]
            for i in range(2):
                n = j * 2 + i
                scores = dot_nt(queries[j][rows, i * 128 : (i + 1) * 128], key) * 128 ** (-0.5)
                scores = jnp.where(allowed, scores, NEG_LARGE)
                exponent = jnp.exp(scores - jnp.max(scores, -1, keepdims=True))
                prob = exponent * (1.0 / jnp.sum(exponent, -1, keepdims=True))
                prob = prob.astype(BF16)
                probs[n] = prob
                attended[rows, n * 128 : (n + 1) * 128] = dot_nn(prob, value).astype(BF16)
    total[...] = dot_nt(attended[:, :256], out_w[0][:, 512:])
    total[...] += dot_nt(attended[:, 256:], out_w[1][:, 512:])
    for s in range(4):
        pieces[s][...] = total[s * 128 : (s + 1) * 128, :].astype(pieces[s].dtype)


def attend_back_kernel(meta, *refs):
    grads, out_w, queries = refs[:4], refs[4:6], refs[6:8]
    keys, values, probs_low, probs_high = refs[8:12]
    grad_query, back_own, back_other = refs[12:15]
    grad_out, grad_keys, grad_values, joined = refs[15:]
    for s in range(4):
        joined[s * 128 : (s + 1) * 128, :] = grads[s][...]
    for j in range(2):
        grad_out[:, j * 256 : j * 256 + 256] = dot_nn(joined[...], out_w[j][:, 512:]).astype(BF16)
    grad_keys[...] = jnp.zeros_like(grad_keys)
    grad_values[...] = jnp.zeros_like(grad_values)
    for half, (count, probs) in enumerate(((512, probs_low), (768, probs_high))):
        rows = pl.ds(pl.multiple_of(meta[half], 256), 256)
        first = 0 if half == 0 else pl.multiple_of(meta[2], 256)
        span = pl.ds(first, count)
        for j in range(2):
            key = keys[j, span, :]
            value = values[j, span, :]
            for i in range(2):
                n = j * 2 + i
                cols = slice(n * 128, (n + 1) * 128)
                grad = grad_out[rows, cols]
                prob = probs[n]
                wide = prob.astype(F32)
                grad_prob = dot_nt(grad, value)
                inner = jnp.sum(wide * grad_prob, -1, keepdims=True)
                grad_scores = (wide * (grad_prob - inner)).astype(BF16)
                grad_query[rows, cols] = dot_nn(grad_scores, key) * 128 ** (-0.5)
                grad_keys[j, span, :] += dot_tn(
                    grad_scores, queries[j][rows, i * 128 : (i + 1) * 128]
                ) * 128 ** (-0.5)
                grad_values[j, span, :] += dot_tn(prob, grad)
    for t in range(8):
        rows = pl.ds(pl.multiple_of(meta[3 + t] * 128, 128), 128)
        target = back_own if t < 4 else back_other
        at = slice((t % 4) * 128, (t % 4 + 1) * 128)
        for j in range(2):
            jj = j if t < 4 else 1 - j
            target[at, jj * 128 : jj * 128 + 128] = grad_keys[j, rows, :].astype(target.dtype)
            target[at, 256 + jj * 128 : 384 + jj * 128] = grad_values[j, rows, :].astype(target.dtype)


def rolled(values, sine):
    return pltpu.roll(values, 64, 1) * sine


def tail_kernel(*refs):
    (grad_query, back_own, swapped, raw_own, raw_other, cosine, sine, gains, weight_own, weight_other) = refs[:10]
    normed, small, first_gain = refs[10:13]
    (low_own, low_other, mine, *pieces) = refs[13:19]
    partial = refs[19]
    sums = [0.0, 0.0]
    for j, (raw, low) in enumerate(((raw_own, low_own), (raw_other, low_other))):
        cols = slice(j * 128, (j + 1) * 128)
        grad_key = back_own[:, cols] + swapped[:, cols].astype(F32)
        cols = slice(256 + j * 128, 384 + j * 128)
        grad_value = back_own[:, cols] + swapped[:, cols].astype(F32)
        for i in range(3):
            cols = slice(i * 128, (i + 1) * 128)
            grad = grad_key if i == 2 else grad_query[:, (j * 2 + i) * 128 : (j * 2 + i + 1) * 128]
            grad = grad * cosine[...] - rolled(grad, sine[...])
            value = raw[:, cols]
            scale = lax.rsqrt(jnp.mean(value * value, -1, keepdims=True) + EPSILON)
            unit = value * scale
            sums[i // 2] = sums[i // 2] + jnp.sum(grad * unit, 0, keepdims=True)
            weighted = grad * gains[i // 2 : i // 2 + 1, :]
            back = scale * (weighted - unit * jnp.mean(unit * weighted, -1, keepdims=True))
            low[:, cols] = back.astype(BF16)
        low[:, 384:] = grad_value.astype(BF16)
    partial[...] = dot_nt(low_own[...], weight_own[:, :512])
    partial[...] += dot_nt(low_other[...], weight_other[:, :512])
    first = jnp.sum(partial[...] * normed[...].astype(F32), 0, keepdims=True)
    for s in range(4):
        rows = slice(s * 128, (s + 1) * 128)
        out = mine if s == 0 else pieces[s - 1]
        out[:128, :] = partial[rows, :].astype(out.dtype)
    gains_row = jnp.concatenate([sums[0], sums[1], jnp.zeros((1, 768), F32)], 1)
    block = jnp.concatenate(
        [first / first_gain[...], small[...], gains_row, jnp.zeros((13, 1024), F32)], 0
    ).astype(BF16)
    mine[128:, :] = block.astype(F32)
    for piece in pieces:
        piece[128:, :] = block


def pack_kernel(*refs):
    *shards, packed, done = refs
    copies, at = [], 0
    for n, ref in enumerate(shards):
        width = ref.shape[1]
        copies.append(pltpu.make_async_copy(ref, packed.at[:, at : at + width], done.at[n]))
        at += width
    for copy in copies:
        copy.start()
    for copy in copies:
        copy.wait()


def vmem(n):
    return [pl.BlockSpec(memory_space=pltpu.VMEM)] * n


SMEM = pl.BlockSpec(memory_space=pltpu.SMEM)
PARAMS = pltpu.CompilerParams(vmem_limit_bytes=48 * 1024 * 1024)


def after(value, *others):
    return lax.optimization_barrier((value, *others))[0]


def gather_stage(shard):
    return jnp.stack([shard_out(shard, a, b) for a, b in SQUARE])


def column_groups():
    groups = []
    for y in range(4):
        for l in range(2):
            groups.append(
                [
                    (((z * 2 + h) * 2 + y % 2) * 4 + place_of(y, pair)) * 2 + l
                    for z in range(4)
                    for h in range(2)
                    for pair in range(2)
                ]
            )
    return groups


AXES = ("z", "h", "c", "y", "l")


def gather_near(stage):
    return stage, ring(stage, "z", -1), ring(stage, "z", 1)


def gather_far(stage, ahead, behind):
    return [stage, ahead, (ring(ahead[:2], "z", -1), ring(behind[2:], "z", 1)), behind]


def place(parts, where):
    width = parts[0].shape[2]
    parts = jax.tree.leaves(parts)
    return pl.pallas_call(
        place_kernel,
        out_shape=jax.ShapeDtypeStruct((1024, width), BF16),
        in_specs=[SMEM] + vmem(len(parts)),
        out_specs=vmem(1)[0],
        compiler_params=PARAMS,
    )(where, *parts)


def pick(own, swapped, extra, where):
    shape = (272, own.shape[1])
    return call(pick_kernel, [(shape, BF16)] * 4, where, own, swapped, extra, smem=1)


def call(kernel, shapes, *args, smem=0, scratch=(), micros=1):
    return pl.pallas_call(
        kernel,
        out_shape=[jax.ShapeDtypeStruct(shape, kind) for shape, kind in shapes],
        in_specs=[SMEM] * smem + vmem(len(args) - smem),
        out_specs=vmem(len(shapes)),
        scratch_shapes=[pltpu.VMEM(shape, kind) for shape, kind in scratch],
        compiler_params=PARAMS,
        cost_estimate=pl.CostEstimate(
            flops=micros * 10**9, bytes_accessed=micros * 3 * 10**6, transcendentals=0
        ),
    )(*args)


def pack(*shards):
    return pl.pallas_call(
        pack_kernel,
        out_shape=jax.ShapeDtypeStruct((64, sum(v.shape[1] for v in shards)), BF16),
        in_specs=[pl.BlockSpec(memory_space=pl.ANY)] * len(shards),
        out_specs=vmem(1)[0],
        scratch_shapes=[pltpu.SemaphoreType.DMA((len(shards),))],
    )(*shards)


def norm_forward(values):
    scale = lax.rsqrt(jnp.mean(values * values, -1, keepdims=True) + EPSILON)
    return values * scale, scale


def norm_backward(unit, scale, gain, grad):
    weighted = grad * gain
    return scale * (weighted - unit * jnp.mean(unit * weighted, -1, keepdims=True))


def per_device(
    tokens,
    segment_ids,
    first_gain,
    query_gain,
    key_gain,
    query_weight,
    key_weight,
    value_weight,
    out_weight,
    second_gain,
    gate_weight,
    up_weight,
    down_weight,
    cotangent,
):
    z, h, c = lax.axis_index("z"), lax.axis_index("h"), lax.axis_index("c")
    y, l = lax.axis_index("y"), lax.axis_index("l")
    where = jnp.stack([z, h * 2 + y // 2]).astype(jnp.int32)
    y_own = jnp.where(y % 2 == c, y, 3 - y)
    tokens = remap(tokens)
    attn_stage = gather_stage(pack(query_weight, key_weight, value_weight, out_weight.T))
    attn_parts = gather_far(*gather_near(attn_stage))
    segment_ids = after(segment_ids, attn_stage)
    seg_row = jnp.where(y // 2 == c, segment_ids, core_swap(segment_ids))[0]

    blocks = [(y_own ^ (2 * i)) * 2 + (l ^ j) for i, j in SQUARE]
    other_blocks = [((3 - y_own) ^ (2 * i)) * 2 + (l ^ j) for i, j in SQUARE]
    index = jnp.concatenate([b * 128 + jnp.arange(128, dtype=jnp.int32) for b in blocks])
    seg = jnp.concatenate([lax.dynamic_slice_in_dim(seg_row, b * 128, 128, 0) for b in blocks])
    begin = jnp.zeros((512,), jnp.int32)
    for v in range(1, 4):
        begin = begin + jnp.where(seg == v, jnp.sum((seg_row < v).astype(jnp.int32)), 0)
    places = (index - begin).astype(F32)
    inverse = ROPE_BASE ** (-jnp.arange(0, 128, 2, dtype=F32) / 128)
    phases = places[:, None] * inverse[None, :]
    cosine, sine = jnp.cos(phases), jnp.sin(phases)
    cosine = jnp.concatenate([cosine, cosine], -1)
    sine = jnp.concatenate([-sine, sine], -1)
    upper = y_own // 2
    meta = jnp.stack([upper * 256, (1 - upper) * 256, (y_own % 2) * 256] + blocks + other_blocks)
    meta = meta.astype(jnp.int32)

    input_float = tokens.astype(F32)
    unit_one, scale_one = norm_forward(input_float)
    own_piece = (unit_one * first_gain).astype(BF16)
    pieces = [across(own_piece, i, j) for i, j in SQUARE]
    mlp_shard = remap(pack(gate_weight, up_weight, down_weight.T))
    mlp_own = lax.all_gather(
        mlp_shard, AXES, axis=0, tiled=True, axis_index_groups=column_groups()
    )
    begin, index = begin[:, None], index[:, None]
    attn_parts = lax.optimization_barrier((attn_parts, mlp_shard, pieces, cosine, sine, begin, index))[0]
    attn_own = place(attn_parts, where)
    attn_other = core_swap(attn_own)
    attn_w = [attn_own, attn_other]
    pair_gains = jnp.stack([query_gain, key_gain])
    shapes = [((512, 256), BF16)] * 2 + [((512, 384), F32)]
    query_0, kv_0, raw_0, normed_one = call(
        prep_kernel, shapes + [((512, 1024), BF16)], *pieces, attn_own, cosine, sine, pair_gains, micros=4
    )
    query_1, kv_1, raw_1 = call(
        prep_kernel, shapes, normed_one, attn_other, cosine, sine, pair_gains, micros=3
    )
    cotangent = remap(after(cotangent, *pieces))
    cot_pieces = [across(cotangent, i, j) for i, j in SQUARE]
    block = (128, 1024)
    keys, vals, probs_low, probs_high, attended, *parts = call(
        attend_kernel,
        [((2, 1024, 128), BF16)] * 2
        + [((4, 256, 512), BF16), ((4, 256, 768), BF16), ((512, 512), BF16), (block, F32)]
        + [(block, BF16)] * 3,
        meta,
        query_0,
        query_1,
        kv_0,
        kv_1,
        core_swap(kv_0),
        core_swap(kv_1),
        begin,
        index,
        *attn_w,
        smem=1,
        scratch=[((512, 1024), F32)],
        micros=8,
    )
    got = [across(parts[s], *SQUARE[s]) for s in (1, 2, 3)]
    mlp_own, cot_pieces = lax.optimization_barrier((mlp_own, cot_pieces, got))[:2]
    cot_all = jnp.concatenate(cot_pieces, 0)
    mlp_w = [mlp_own, core_swap(mlp_own)]
    gu_w = [w[:, :768] for w in mlp_w]
    down_w = [w[:, 768:] for w in mlp_w]
    hidden = input_float + parts[0]
    for value in got:
        hidden = hidden + value.astype(F32)

    unit_two, scale_two = norm_forward(hidden)
    normed_two = gather_tokens((unit_two * second_gain).astype(BF16))
    partial_two, acts, grad_gus = 0.0, [], []
    for j in range(2):
        gate_up = dot_nn(normed_two, gu_w[j])
        gate, up = gate_up[:, :384], gate_up[:, 384:]
        sig = jax.nn.sigmoid(gate)
        silu = gate * sig
        act = (silu * up).astype(BF16)
        grad_act = dot_nn(cot_all, down_w[j])
        grad_gate = (grad_act * up * (sig + silu * (1.0 - sig))).astype(BF16)
        grad_up = (grad_act * silu).astype(BF16)
        grad_gu = jnp.concatenate([grad_gate, grad_up], 1)
        partial_two = partial_two + dot_nt(grad_gu, gu_w[j])
        acts.append(act)
        grad_gus.append(grad_gu)
    grad_normed_two = scatter_tokens(partial_two)
    acts, grad_gus = lax.optimization_barrier((acts, grad_gus, partial_two))[:2]
    mlp_grads = [
        jnp.concatenate([dot_tn(normed_two, grad_gus[j]), dot_tn(cot_all, acts[j])], 1).astype(BF16)
        for j in range(2)
    ]
    branch = dot_nt(acts[0], down_w[0]) + dot_nt(acts[1], down_w[1])
    second_part = jnp.sum(partial_two * normed_two.astype(F32), 0) / second_gain

    grad_hidden = cotangent.astype(F32) + norm_backward(
        unit_two, scale_two, second_gain, grad_normed_two
    )
    grad_low = grad_hidden.astype(BF16)
    hidden_grads = [across(grad_low, i, j) for i, j in SQUARE]
    mlp_swapped = core_swap(mlp_grads[1])
    mlp_total = (mlp_grads[0].astype(F32) + mlp_swapped.astype(F32)).astype(BF16)
    hidden_grads, mlp_total = lax.optimization_barrier((hidden_grads, mlp_total))
    mlp_low = lax.psum_scatter(
        mlp_total, AXES, scatter_dimension=0, tiled=True, axis_index_groups=column_groups()
    )
    grad_query, back_own, back_other = call(
        attend_back_kernel,
        [((512, 512), F32), ((512, 512), F32), ((512, 512), BF16)],
        meta,
        *hidden_grads,
        *attn_w,
        query_0,
        query_1,
        keys,
        vals,
        probs_low,
        probs_high,
        smem=1,
        scratch=[
            ((512, 512), BF16),
            ((2, 1024, 128), F32),
            ((2, 1024, 128), F32),
            ((512, 1024), BF16),
        ],
        micros=8,
    )
    low_branch = branch.astype(BF16)
    branches = [
        across(low_branch[s * 128 : (s + 1) * 128], *SQUARE[s]) for s in (1, 2, 3)
    ]
    back_own, branches = lax.optimization_barrier((back_own, branches))
    *grad_raws, mine, piece_1, piece_2, piece_3 = call(
        tail_kernel,
        [((512, 512), BF16)] * 2 + [((144, 1024), F32)] + [((144, 1024), BF16)] * 3,
        grad_query,
        back_own,
        core_swap(back_other),
        raw_0,
        raw_1,
        cosine,
        sine,
        pair_gains,
        *attn_w,
        normed_one,
        second_part[None, :],
        first_gain[None, :],
        scratch=[((512, 1024), F32)],
        micros=9,
    )
    hidden_grad = jnp.concatenate(lax.optimization_barrier((hidden_grads, piece_1))[0], 0)
    attn_grads = [
        jnp.concatenate(
            [
                dot_tn(normed_one, after(grad_raws[j], piece_1)).astype(BF16),
                dot_tn(hidden_grad, attended[:, j * 256 : (j + 1) * 256]).astype(BF16),
            ],
            1,
        )
        for j in range(2)
    ]
    got = [across(p, *SQUARE[s + 1]) for s, p in enumerate((piece_1, piece_2, piece_3))]
    attn_swapped = core_swap(attn_grads[1])
    got = [p.astype(F32) for p in got]
    total = (mine + got[0]) + (got[1] + got[2])
    sums = total[128:131]
    sums = sums + core_swap(sums)
    sums = jnp.concatenate([sums[:, :768], jnp.pad(sums[:, 768:], ((0, 0), (0, 512)))], 0)
    sums = jnp.pad(sums, ((0, 10), (0, 0))).astype(BF16)
    parts = pick(attn_grads[0], attn_swapped, sums, where)
    got = [ring(parts[s], "z", s).astype(F32) for s in (1, 2, 3)]
    low = (parts[0].astype(F32) + got[1]) + (got[0] + got[2])
    low = low.astype(BF16)
    attn_owned = [
        shard_home(
            jnp.concatenate([low[k * 64 : (k + 1) * 64], low[256:]], 0), *SQUARE[k]
        ).astype(F32)
        for k in range(4)
    ]
    attn_owned = (attn_owned[0] + attn_owned[1]) + (attn_owned[2] + attn_owned[3])
    sums = jnp.concatenate([attn_owned[64:67], attn_owned[67:70, :256]], 1)
    attn_owned, out_owned = attn_owned[:64, :512], attn_owned[:64, 512:]
    grad_tokens = grad_hidden + norm_backward(unit_one, scale_one, first_gain, total[:128])
    layer_out = hidden + branch[:128]
    for value in branches:
        layer_out = layer_out + value.astype(F32)
    results = jnp.concatenate([grad_tokens.astype(BF16), layer_out.astype(BF16)], 0)
    results = remap_back(after(results, *parts))
    mlp_owned = remap_back(after(mlp_low, low)).astype(F32)
    layer_out, grad_tokens = results[128:], results[:128]
    return (
        layer_out,
        grad_tokens,
        sums[0],
        sums[2, :128],
        sums[2, 128:256],
        attn_owned[:, :256],
        attn_owned[:, 256:384],
        attn_owned[:, 384:],
        out_owned.T,
        sums[1],
        mlp_owned[:, :384],
        mlp_owned[:, 384:768],
        mlp_owned[:, 768:].T,
    )


def solution(mesh):
    fine = Mesh(mesh.devices.reshape(4, 2, 2, 4, 2), ("z", "h", "c", "y", "l"))
    dp, tensor = ("z", "h", "c"), ("y", "l")
    rows, cols, trans = P(dp + tensor, None), P(dp, tensor), P(tensor, dp)
    in_specs = (
        rows, P(dp, None), P(), P(), P(), cols, cols, cols, trans, P(), cols, cols, trans, rows,
    )
    out_specs = (rows, rows, P(), P(), P(), cols, cols, cols, trans, P(), cols, cols, trans)
    return jax.shard_map(
        per_device, mesh=fine, in_specs=in_specs, out_specs=out_specs, check_vma=False
    )
```

```python
import jax
import jax.numpy as jnp
from jax import lax
from jax.experimental import pallas as pl
from jax.experimental.pallas import tpu as pltpu
from jax.sharding import Mesh
from jax.sharding import PartitionSpec as P

EPSILON = 1e-06
ROPE_BASE = 1000000.0
NEG_LARGE = -1e30
BF16 = jnp.bfloat16
F32 = jnp.float32
SQUARE = ((0, 0), (0, 1), (1, 0), (1, 1))


def place_of(y, pair):
    return y if y // 2 == pair else 3 - y


def remap_pairs():
    pairs = []
    for c in range(2):
        for y in range(4):
            for l in range(2):
                pairs.append(((c * 4 + y) * 2 + l, ((y % 2) * 4 + place_of(y, c)) * 2 + l))
    return pairs


def remap(value):
    return lax.ppermute(value, ("c", "y", "l"), remap_pairs())


def remap_back(value):
    return lax.ppermute(value, ("c", "y", "l"), [(b, a) for a, b in remap_pairs()])


def shard_pairs(a, b):
    pairs = []
    for h in range(2):
        for c in range(2):
            for y in range(4):
                for l in range(2):
                    source = ((h * 2 + c) * 4 + y) * 2 + l
                    pairs.append((source, (((h ^ a) * 2 + y % 2) * 4 + place_of(y, c ^ b)) * 2 + l))
    return pairs


def shard_out(value, a, b):
    return lax.ppermute(value, ("h", "c", "y", "l"), shard_pairs(a, b))


def shard_home(value, a, b):
    return lax.ppermute(value, ("h", "c", "y", "l"), [(t, s) for s, t in shard_pairs(a, b)])


def ring(value, axis, step):
    return lax.ppermute(value, (axis,), [(i, (i + step) % 4) for i in range(4)])


def core_swap(value):
    return lax.ppermute(value, ("c",), [(0, 1), (1, 0)])


def across(value, i, j):
    if (i, j) == (0, 0):
        return value
    pairs = [(y * 2 + l, (y ^ i) * 2 + (l ^ j)) for y in range(4) for l in range(2)]
    return lax.ppermute(value, ("y", "l"), pairs)


def dot_nn(a, b):
    return lax.dot_general(a, b, (((1,), (0,)), ((), ())), preferred_element_type=F32)


def dot_nt(a, b):
    return lax.dot_general(a, b, (((1,), (1,)), ((), ())), preferred_element_type=F32)


def dot_tn(a, b):
    return lax.dot_general(a, b, (((0,), (0,)), ((), ())), preferred_element_type=F32)


def gather_tokens(block):
    return jnp.concatenate([across(block, i, j) for i, j in SQUARE], 0)


def place_kernel(where, *refs):
    *parts, out = refs
    if len(parts) == 5:
        parts[2:4] = [(parts[2], parts[3])]
    for s in range(4):
        for k in range(4):
            at = ((where[0] + s) % 4) * 4 + (where[1] ^ k)
            block = parts[s][k // 2][k % 2] if isinstance(parts[s], tuple) else parts[s][k]
            out[pl.ds(pl.multiple_of(at * 64, 64), 64), :] = block


def pick_kernel(where, *refs):
    outs, pairs = refs[-4:], len(refs) // 2 - 2
    for s in range(4):
        for k in range(4):
            place = ((where[0] + s) % 4) * 4 + (where[1] ^ k)
            rows = pl.ds(pl.multiple_of(place * 64, 64), 64)
            at = 0
            for own, swapped in zip(refs[:pairs], refs[pairs : 2 * pairs]):
                total = own[rows, :].astype(F32) + swapped[rows, :].astype(F32)
                outs[s][k, :, at : at + own.shape[1]] = total.astype(BF16)
                at += own.shape[1]


def prep_kernel(*refs):
    if len(refs) == 12:
        weight, cosine, sine, gains = refs[4:8]
        query, kv, raw, joined = refs[8:]
        for s in range(4):
            joined[s * 128 : (s + 1) * 128, :] = refs[s][:128, :]
    else:
        joined, weight, cosine, sine, gains, query, kv, raw = refs
    value = dot_nn(joined[...], weight[:, :512])
    kv[:, 128:] = value[:, 384:].astype(BF16)
    raw[...] = value[:, :384]
    for i in range(3):
        cols = slice(i * 128, (i + 1) * 128)
        head = raw[:, cols]
        scale = lax.rsqrt(jnp.mean(head * head, -1, keepdims=True) + EPSILON)
        head = head * scale * gains[i // 2 : i // 2 + 1, :]
        head = (head * cosine[...] + rolled(head, sine[...])).astype(BF16)
        if i == 2:
            kv[:, :128] = head
        else:
            query[:, cols] = head


def attend_kernel(meta, *refs):
    queries, kv_own, kv_other, begin, index, out_w = refs[:2], refs[2:4], refs[4:6], refs[6], refs[7], refs[8:10]
    keys, values, probs_low, probs_high, attended = refs[10:15]
    pieces, total = refs[15:19], refs[19]
    for t in range(8):
        rows = pl.ds(pl.multiple_of(meta[3 + t] * 128, 128), 128)
        at = slice((t % 4) * 128, (t % 4 + 1) * 128)
        for j in range(2):
            source = kv_own[j] if t < 4 else kv_other[1 - j]
            keys[j, rows, :] = source[at, :128]
            values[j, rows, :] = source[at, 128:]
    for half, (count, probs) in enumerate(((512, probs_low), (768, probs_high))):
        rows = pl.ds(pl.multiple_of(meta[half], 256), 256)
        first = 0 if half == 0 else pl.multiple_of(meta[2], 256)
        place = first + lax.broadcasted_iota(jnp.int32, (256, count), 1)
        allowed = (place >= begin[rows, :]) & (place <= index[rows, :])
        for j in range(2):
            key = keys[j, pl.ds(first, count), :]
            value = values[j, pl.ds(first, count), :]
            for i in range(2):
                n = j * 2 + i
                scores = dot_nt(queries[j][rows, i * 128 : (i + 1) * 128], key) * 128 ** (-0.5)
                scores = jnp.where(allowed, scores, NEG_LARGE)
                exponent = jnp.exp(scores - jnp.max(scores, -1, keepdims=True))
                prob = exponent * (1.0 / jnp.sum(exponent, -1, keepdims=True))
                prob = prob.astype(BF16)
                probs[n] = prob
                attended[rows, n * 128 : (n + 1) * 128] = dot_nn(prob, value).astype(BF16)
    total[...] = dot_nt(attended[:, :256], out_w[0][:, 512:])
    total[...] += dot_nt(attended[:, 256:], out_w[1][:, 512:])
    for s in range(4):
        pieces[s][...] = total[s * 128 : (s + 1) * 128, :].astype(pieces[s].dtype)


def attend_back_kernel(meta, *refs):
    grads, out_w, queries = refs[:4], refs[4:6], refs[6:8]
    keys, values, probs_low, probs_high = refs[8:12]
    grad_query, back_own, back_other = refs[12:15]
    grad_out, grad_keys, grad_values, joined = refs[15:]
    for s in range(4):
        joined[s * 128 : (s + 1) * 128, :] = grads[s][...]
    for j in range(2):
        grad_out[:, j * 256 : j * 256 + 256] = dot_nn(joined[...], out_w[j][:, 512:]).astype(BF16)
    grad_keys[...] = jnp.zeros_like(grad_keys)
    grad_values[...] = jnp.zeros_like(grad_values)
    for half, (count, probs) in enumerate(((512, probs_low), (768, probs_high))):
        rows = pl.ds(pl.multiple_of(meta[half], 256), 256)
        first = 0 if half == 0 else pl.multiple_of(meta[2], 256)
        span = pl.ds(first, count)
        for j in range(2):
            key = keys[j, span, :]
            value = values[j, span, :]
            for i in range(2):
                n = j * 2 + i
                cols = slice(n * 128, (n + 1) * 128)
                grad = grad_out[rows, cols]
                prob = probs[n]
                wide = prob.astype(F32)
                grad_prob = dot_nt(grad, value)
                inner = jnp.sum(wide * grad_prob, -1, keepdims=True)
                grad_scores = (wide * (grad_prob - inner)).astype(BF16)
                grad_query[rows, cols] = dot_nn(grad_scores, key) * 128 ** (-0.5)
                grad_keys[j, span, :] += dot_tn(
                    grad_scores, queries[j][rows, i * 128 : (i + 1) * 128]
                ) * 128 ** (-0.5)
                grad_values[j, span, :] += dot_tn(prob, grad)
    for t in range(8):
        rows = pl.ds(pl.multiple_of(meta[3 + t] * 128, 128), 128)
        target = back_own if t < 4 else back_other
        at = slice((t % 4) * 128, (t % 4 + 1) * 128)
        for j in range(2):
            jj = j if t < 4 else 1 - j
            target[at, jj * 128 : jj * 128 + 128] = grad_keys[j, rows, :].astype(target.dtype)
            target[at, 256 + jj * 128 : 384 + jj * 128] = grad_values[j, rows, :].astype(target.dtype)


def rolled(values, sine):
    return pltpu.roll(values, 64, 1) * sine


def tail_kernel(*refs):
    (grad_query, back_own, swapped, raw_own, raw_other, cosine, sine, gains, weight_own, weight_other) = refs[:10]
    normed, small, first_gain = refs[10:13]
    (low_own, low_other, mine, *pieces) = refs[13:19]
    partial = refs[19]
    sums = [0.0, 0.0]
    for j, (raw, low) in enumerate(((raw_own, low_own), (raw_other, low_other))):
        cols = slice(j * 128, (j + 1) * 128)
        grad_key = back_own[:, cols] + swapped[:, cols].astype(F32)
        cols = slice(256 + j * 128, 384 + j * 128)
        grad_value = back_own[:, cols] + swapped[:, cols].astype(F32)
        for i in range(3):
            cols = slice(i * 128, (i + 1) * 128)
            grad = grad_key if i == 2 else grad_query[:, (j * 2 + i) * 128 : (j * 2 + i + 1) * 128]
            grad = grad * cosine[...] - rolled(grad, sine[...])
            value = raw[:, cols]
            scale = lax.rsqrt(jnp.mean(value * value, -1, keepdims=True) + EPSILON)
            unit = value * scale
            sums[i // 2] = sums[i // 2] + jnp.sum(grad * unit, 0, keepdims=True)
            weighted = grad * gains[i // 2 : i // 2 + 1, :]
            back = scale * (weighted - unit * jnp.mean(unit * weighted, -1, keepdims=True))
            low[:, cols] = back.astype(BF16)
        low[:, 384:] = grad_value.astype(BF16)
    partial[...] = dot_nt(low_own[...], weight_own[:, :512])
    partial[...] += dot_nt(low_other[...], weight_other[:, :512])
    first = jnp.sum(partial[...] * normed[...].astype(F32), 0, keepdims=True)
    for s in range(4):
        rows = slice(s * 128, (s + 1) * 128)
        out = mine if s == 0 else pieces[s - 1]
        out[:128, :] = partial[rows, :].astype(out.dtype)
    gains_row = jnp.concatenate([sums[0], sums[1], jnp.zeros((1, 768), F32)], 1)
    block = jnp.concatenate(
        [first / first_gain[...], small[...], gains_row, jnp.zeros((13, 1024), F32)], 0
    ).astype(BF16)
    mine[128:, :] = block.astype(F32)
    for piece in pieces:
        piece[128:, :] = block


def pack_kernel(*refs):
    *shards, packed, done = refs
    copies, at = [], 0
    for n, ref in enumerate(shards):
        width = ref.shape[1]
        copies.append(pltpu.make_async_copy(ref, packed.at[:, at : at + width], done.at[n]))
        at += width
    for copy in copies:
        copy.start()
    for copy in copies:
        copy.wait()


def pick_with_kernel(where, own, swapped, extra, *outs):
    for s in range(4):
        for k in range(4):
            at = ((where[0] + s) % 4) * 4 + (where[1] ^ k)
            rows = pl.ds(pl.multiple_of(at * 64, 64), 64)
            total = own[rows, :].astype(F32) + swapped[rows, :].astype(F32)
            outs[s][k * 64 : (k + 1) * 64, :] = total.astype(BF16)
        outs[s][256:, :] = extra[...]


def vmem(n):
    return [pl.BlockSpec(memory_space=pltpu.VMEM)] * n


SMEM = pl.BlockSpec(memory_space=pltpu.SMEM)
PARAMS = pltpu.CompilerParams(vmem_limit_bytes=48 * 1024 * 1024)


def after(value, *others):
    return lax.optimization_barrier((value, *others))[0]


def gather_near(stage):
    return stage, ring(stage, "z", -1), ring(stage, "z", 1)


def gather_far(stage, ahead, behind):
    return [stage, ahead, (ring(ahead[:2], "z", -1), ring(behind[2:], "z", 1)), behind]


def place(parts, where):
    width = parts[0].shape[2]
    parts = jax.tree.leaves(parts)
    return pl.pallas_call(
        place_kernel,
        out_shape=jax.ShapeDtypeStruct((1024, width), BF16),
        in_specs=[SMEM] + vmem(len(parts)),
        out_specs=vmem(1)[0],
        compiler_params=PARAMS,
    )(where, *parts)


def pick(owns, swaps, where):
    width = sum(v.shape[1] for v in owns)
    return call(pick_kernel, [((4, 64, width), BF16)] * 4, where, *owns, *swaps, smem=1)


def pick_with(own, swapped, extra, where):
    shape = (272, own.shape[1])
    return call(pick_with_kernel, [(shape, BF16)] * 4, where, own, swapped, extra, smem=1)


def chain_first(parts):
    add = lambda a, b: (a.astype(F32) + b.astype(F32)).astype(BF16)
    up, down = ring(parts[2][:2], "z", 1), ring(parts[2][2:], "z", -1)
    ahead = jnp.concatenate([add(parts[1][:2], up), parts[1][2:]])
    behind = jnp.concatenate([parts[3][:2], add(parts[3][2:], down)])
    return parts[0], ahead, behind


def chain_send(own, ahead, behind):
    return own, ring(ahead, "z", 1), ring(behind, "z", -1)


def chain_total(own, ahead, behind):
    return (own.astype(F32) + ahead.astype(F32) + behind.astype(F32)).astype(BF16)


def call(kernel, shapes, *args, smem=0, scratch=(), micros=1):
    return pl.pallas_call(
        kernel,
        out_shape=[jax.ShapeDtypeStruct(shape, kind) for shape, kind in shapes],
        in_specs=[SMEM] * smem + vmem(len(args) - smem),
        out_specs=vmem(len(shapes)),
        scratch_shapes=[pltpu.VMEM(shape, kind) for shape, kind in scratch],
        compiler_params=PARAMS,
        cost_estimate=pl.CostEstimate(
            flops=micros * 10**9, bytes_accessed=micros * 3 * 10**6, transcendentals=0
        ),
    )(*args)


def pack(*shards):
    return pl.pallas_call(
        pack_kernel,
        out_shape=jax.ShapeDtypeStruct((64, sum(v.shape[1] for v in shards)), BF16),
        in_specs=[pl.BlockSpec(memory_space=pl.ANY)] * len(shards),
        out_specs=vmem(1)[0],
        scratch_shapes=[pltpu.SemaphoreType.DMA((len(shards),))],
    )(*shards)


def norm_forward(values):
    scale = lax.rsqrt(jnp.mean(values * values, -1, keepdims=True) + EPSILON)
    return values * scale, scale


def norm_backward(unit, scale, gain, grad):
    weighted = grad * gain
    return scale * (weighted - unit * jnp.mean(unit * weighted, -1, keepdims=True))


def per_device(
    tokens,
    segment_ids,
    first_gain,
    query_gain,
    key_gain,
    query_weight,
    key_weight,
    value_weight,
    out_weight,
    second_gain,
    gate_weight,
    up_weight,
    down_weight,
    cotangent,
):
    z, h, c = lax.axis_index("z"), lax.axis_index("h"), lax.axis_index("c")
    y, l = lax.axis_index("y"), lax.axis_index("l")
    where = jnp.stack([z, h * 2 + y // 2]).astype(jnp.int32)
    y_own = jnp.where(y % 2 == c, y, 3 - y)
    both = remap(jnp.concatenate([tokens, cotangent], 0))
    tokens, cotangent = both[:128], both[128:]
    shards = pack(
        query_weight, key_weight, value_weight, out_weight.T, gate_weight, up_weight, down_weight.T
    )
    stages = [shard_out(shards, a, b) for a, b in SQUARE]
    attn_stage = jnp.stack([v[:, :768] for v in stages])
    mlp_stage = jnp.stack([v[:, 768:] for v in stages])
    attn_near = gather_near(attn_stage)
    attn_parts = gather_far(*attn_near)
    segment_ids = after(segment_ids, attn_near[1])
    seg_row = jnp.where(y // 2 == c, segment_ids, core_swap(segment_ids))[0]

    blocks = [(y_own ^ (2 * i)) * 2 + (l ^ j) for i, j in SQUARE]
    other_blocks = [((3 - y_own) ^ (2 * i)) * 2 + (l ^ j) for i, j in SQUARE]
    index = jnp.concatenate([b * 128 + jnp.arange(128, dtype=jnp.int32) for b in blocks])
    seg = jnp.concatenate([lax.dynamic_slice_in_dim(seg_row, b * 128, 128, 0) for b in blocks])
    begin = jnp.zeros((512,), jnp.int32)
    for v in range(1, 4):
        begin = begin + jnp.where(seg == v, jnp.sum((seg_row < v).astype(jnp.int32)), 0)
    places = (index - begin).astype(F32)
    inverse = ROPE_BASE ** (-jnp.arange(0, 128, 2, dtype=F32) / 128)
    phases = places[:, None] * inverse[None, :]
    cosine, sine = jnp.cos(phases), jnp.sin(phases)
    cosine = jnp.concatenate([cosine, cosine], -1)
    sine = jnp.concatenate([-sine, sine], -1)
    upper = y_own // 2
    meta = jnp.stack([upper * 256, (1 - upper) * 256, (y_own % 2) * 256] + blocks + other_blocks)
    meta = meta.astype(jnp.int32)

    input_float = tokens.astype(F32)
    unit_one, scale_one = norm_forward(input_float)
    own_piece = (unit_one * first_gain).astype(BF16)
    own_piece = jnp.concatenate([own_piece, cotangent], 0)
    pieces = [across(own_piece, i, j) for i, j in SQUARE]
    begin, index = begin[:, None], index[:, None]
    attn_parts = lax.optimization_barrier((attn_parts, pieces, cosine, sine, begin, index))[0]
    attn_own = place(attn_parts, where)
    attn_other = core_swap(attn_own)
    attn_w = [attn_own, attn_other]
    pair_gains = jnp.stack([query_gain, key_gain])
    shapes = [((512, 256), BF16)] * 2 + [((512, 384), F32)]
    query_0, kv_0, raw_0, normed_one = call(
        prep_kernel, shapes + [((512, 1024), BF16)], *pieces, attn_own, cosine, sine, pair_gains, micros=4
    )
    query_1, kv_1, raw_1 = call(
        prep_kernel, shapes, normed_one, attn_other, cosine, sine, pair_gains, micros=3
    )
    block = (128, 1024)
    keys, vals, probs_low, probs_high, attended, *parts = call(
        attend_kernel,
        [((2, 1024, 128), BF16)] * 2
        + [((4, 256, 512), BF16), ((4, 256, 768), BF16), ((512, 512), BF16), (block, F32)]
        + [(block, BF16)] * 3,
        meta,
        query_0,
        query_1,
        kv_0,
        kv_1,
        core_swap(kv_0),
        core_swap(kv_1),
        begin,
        index,
        *attn_w,
        smem=1,
        scratch=[((512, 1024), F32)],
        micros=8,
    )
    mlp_parts = gather_far(*gather_near(after(mlp_stage, attn_own)))
    got = [across(parts[s], *SQUARE[s]) for s in (1, 2, 3)]
    mlp_parts, pieces = lax.optimization_barrier((mlp_parts, pieces, got))[:2]
    cot_all = jnp.concatenate([p[128:] for p in pieces], 0)
    mlp_own = place(mlp_parts, where)
    mlp_w = [mlp_own, core_swap(mlp_own)]
    gu_w = [w[:, :768] for w in mlp_w]
    down_w = [w[:, 768:] for w in mlp_w]
    hidden = input_float + parts[0]
    for value in got:
        hidden = hidden + value.astype(F32)

    unit_two, scale_two = norm_forward(hidden)
    normed_two = gather_tokens((unit_two * second_gain).astype(BF16))
    partial_two, acts, grad_gus = 0.0, [], []
    for j in range(2):
        gate_up = dot_nn(normed_two, gu_w[j])
        gate, up = gate_up[:, :384], gate_up[:, 384:]
        sig = jax.nn.sigmoid(gate)
        silu = gate * sig
        act = (silu * up).astype(BF16)
        grad_act = dot_nn(cot_all, down_w[j])
        grad_gate = (grad_act * up * (sig + silu * (1.0 - sig))).astype(BF16)
        grad_up = (grad_act * silu).astype(BF16)
        grad_gu = jnp.concatenate([grad_gate, grad_up], 1)
        partial_two = partial_two + dot_nt(grad_gu, gu_w[j])
        acts.append(act)
        grad_gus.append(grad_gu)
    low = partial_two.astype(BF16)
    got = [across(low[s * 128 : (s + 1) * 128], *SQUARE[s]) for s in (1, 2, 3)]
    grad_normed_two = partial_two[:128]
    for value in got:
        grad_normed_two = grad_normed_two + value.astype(F32)
    acts, grad_gus = lax.optimization_barrier((acts, grad_gus, got))[:2]
    mlp_grads = [
        jnp.concatenate([dot_tn(normed_two, grad_gus[j]), dot_tn(cot_all, acts[j])], 1).astype(BF16)
        for j in range(2)
    ]
    second_part = jnp.sum(partial_two * normed_two.astype(F32), 0) / second_gain

    grad_hidden = cotangent.astype(F32) + norm_backward(
        unit_two, scale_two, second_gain, grad_normed_two
    )
    grad_low = grad_hidden.astype(BF16)
    hidden_grads = [across(grad_low, i, j) for i, j in SQUARE]
    mlp_picked = pick(mlp_grads[:1], [core_swap(mlp_grads[1])], where)
    mlp_chain = chain_first(mlp_picked)
    mlp_far = chain_send(*mlp_chain)
    hidden_grads = lax.optimization_barrier((hidden_grads, mlp_picked))[0]
    grad_query, back_own, back_other = call(
        attend_back_kernel,
        [((512, 512), F32), ((512, 512), F32), ((512, 512), BF16)],
        meta,
        *hidden_grads,
        *attn_w,
        query_0,
        query_1,
        keys,
        vals,
        probs_low,
        probs_high,
        smem=1,
        scratch=[
            ((512, 512), BF16),
            ((2, 1024, 128), F32),
            ((2, 1024, 128), F32),
            ((512, 1024), BF16),
        ],
        micros=8,
    )
    *grad_raws, mine, piece_1, piece_2, piece_3 = call(
        tail_kernel,
        [((512, 512), BF16)] * 2 + [((144, 1024), F32)] + [((144, 1024), BF16)] * 3,
        grad_query,
        back_own,
        core_swap(back_other),
        raw_0,
        raw_1,
        cosine,
        sine,
        pair_gains,
        *attn_w,
        normed_one,
        second_part[None, :],
        first_gain[None, :],
        scratch=[((512, 1024), F32)],
        micros=9,
    )
    hidden_grad = jnp.concatenate(lax.optimization_barrier((hidden_grads, piece_1))[0], 0)
    attn_grads = [
        jnp.concatenate(
            [
                dot_tn(normed_one, after(grad_raws[j], piece_1)).astype(BF16),
                dot_tn(hidden_grad, attended[:, j * 256 : (j + 1) * 256]).astype(BF16),
            ],
            1,
        )
        for j in range(2)
    ]
    got = [across(p, *SQUARE[s + 1]) for s, p in enumerate((piece_1, piece_2, piece_3))]
    attn_swapped, mlp_far = lax.optimization_barrier((core_swap(attn_grads[1]), mlp_far))
    got = [p.astype(F32) for p in got]
    total = (mine + got[0]) + (got[1] + got[2])
    sums = total[128:131]
    sums = sums + core_swap(sums)
    sums = jnp.concatenate([sums[:, :768], jnp.pad(sums[:, 768:], ((0, 0), (0, 512)))], 0)
    sums = jnp.pad(sums, ((0, 10), (0, 0))).astype(BF16)
    parts = pick_with(attn_grads[0], attn_swapped, sums, where)
    got = [ring(parts[s], "z", s) for s in (1, 2, 3)]
    mlp_low = after(chain_total(*mlp_far), got[0])
    mlp_home = [shard_home(mlp_low[k], *SQUARE[k]) for k in range(4)]
    mlp_owned = sum(v.astype(F32) for v in mlp_home)
    acts = lax.optimization_barrier((acts, got[0]))[0]
    low = (dot_nt(acts[0], down_w[0]) + dot_nt(acts[1], down_w[1])).astype(BF16)
    branches = [across(low[s * 128 : (s + 1) * 128], *SQUARE[s]) for s in range(4)]
    got = lax.optimization_barrier((got, mlp_home))[0]
    grad_tokens = grad_hidden + norm_backward(unit_one, scale_one, first_gain, total[:128])
    layer_out = hidden
    for value in branches:
        layer_out = layer_out + value.astype(F32)
    results = jnp.concatenate([grad_tokens.astype(BF16), layer_out.astype(BF16)], 0)
    results = remap_back(results)
    got = [p.astype(F32) for p in got]
    low = ((parts[0].astype(F32) + got[1]) + (got[0] + got[2])).astype(BF16)
    attn_owned = [
        shard_home(
            jnp.concatenate([low[k * 64 : (k + 1) * 64], low[256:]], 0), *SQUARE[k]
        ).astype(F32)
        for k in range(4)
    ]
    attn_owned = (attn_owned[0] + attn_owned[1]) + (attn_owned[2] + attn_owned[3])
    sums = jnp.concatenate([attn_owned[64:67], attn_owned[67:70, :256]], 1)
    attn_owned, out_owned = attn_owned[:64, :512], attn_owned[:64, 512:]
    layer_out, grad_tokens = results[128:], results[:128]
    return (
        layer_out,
        grad_tokens,
        sums[0],
        sums[2, :128],
        sums[2, 128:256],
        attn_owned[:, :256],
        attn_owned[:, 256:384],
        attn_owned[:, 384:],
        out_owned.T,
        sums[1],
        mlp_owned[:, :384],
        mlp_owned[:, 384:768],
        mlp_owned[:, 768:].T,
    )


def solution(mesh):
    fine = Mesh(mesh.devices.reshape(4, 2, 2, 4, 2), ("z", "h", "c", "y", "l"))
    dp, tensor = ("z", "h", "c"), ("y", "l")
    rows, cols, trans = P(dp + tensor, None), P(dp, tensor), P(tensor, dp)
    in_specs = (
        rows, P(dp, None), P(), P(), P(), cols, cols, cols, trans, P(), cols, cols, trans, rows,
    )
    out_specs = (rows, rows, P(), P(), P(), cols, cols, cols, trans, P(), cols, cols, trans)
    return jax.shard_map(
        per_device, mesh=fine, in_specs=in_specs, out_specs=out_specs, check_vma=False
    )
```

```python
import jax
import jax.numpy as jnp
from jax import lax
from jax.experimental import pallas as pl
from jax.experimental.pallas import tpu as pltpu
from jax.sharding import Mesh
from jax.sharding import PartitionSpec as P

EPSILON = 1e-06
ROPE_BASE = 1000000.0
NEG_LARGE = -1e30
BF16 = jnp.bfloat16
F32 = jnp.float32
SQUARE = ((0, 0), (0, 1), (1, 0), (1, 1))


def place_of(y, pair):
    return y if y // 2 == pair else 3 - y


def remap_pairs():
    pairs = []
    for c in range(2):
        for y in range(4):
            for l in range(2):
                pairs.append(((c * 4 + y) * 2 + l, ((y % 2) * 4 + place_of(y, c)) * 2 + l))
    return pairs


def remap(value):
    return lax.ppermute(value, ("c", "y", "l"), remap_pairs())


def remap_back(value):
    return lax.ppermute(value, ("c", "y", "l"), [(b, a) for a, b in remap_pairs()])


def shard_pairs(a, b):
    pairs = []
    for h in range(2):
        for c in range(2):
            for y in range(4):
                for l in range(2):
                    source = ((h * 2 + c) * 4 + y) * 2 + l
                    pairs.append((source, (((h ^ a) * 2 + y % 2) * 4 + place_of(y, c ^ b)) * 2 + l))
    return pairs


def shard_out(value, a, b):
    return lax.ppermute(value, ("h", "c", "y", "l"), shard_pairs(a, b))


def shard_home(value, a, b):
    return lax.ppermute(value, ("h", "c", "y", "l"), [(t, s) for s, t in shard_pairs(a, b)])


def ring(value, axis, step):
    return lax.ppermute(value, (axis,), [(i, (i + step) % 4) for i in range(4)])


def core_swap(value):
    return lax.ppermute(value, ("c",), [(0, 1), (1, 0)])


def across(value, i, j):
    if (i, j) == (0, 0):
        return value
    pairs = [(y * 2 + l, (y ^ i) * 2 + (l ^ j)) for y in range(4) for l in range(2)]
    return lax.ppermute(value, ("y", "l"), pairs)


def dot_nn(a, b):
    return lax.dot_general(a, b, (((1,), (0,)), ((), ())), preferred_element_type=F32)


def dot_nt(a, b):
    return lax.dot_general(a, b, (((1,), (1,)), ((), ())), preferred_element_type=F32)


def dot_tn(a, b):
    return lax.dot_general(a, b, (((0,), (0,)), ((), ())), preferred_element_type=F32)


def gather_tokens(block):
    return jnp.concatenate([across(block, i, j) for i, j in SQUARE], 0)


def place_kernel(where, *refs):
    *parts, out = refs
    if len(parts) == 5:
        parts[2:4] = [(parts[2], parts[3])]
    for s in range(4):
        for k in range(4):
            at = ((where[0] + s) % 4) * 4 + (where[1] ^ k)
            block = parts[s][k // 2][k % 2] if isinstance(parts[s], tuple) else parts[s][k]
            out[pl.ds(pl.multiple_of(at * 64, 64), 64), :] = block


def pick_kernel(where, *refs):
    outs, pairs = refs[-4:], len(refs) // 2 - 2
    for s in range(4):
        for k in range(4):
            place = ((where[0] + s) % 4) * 4 + (where[1] ^ k)
            rows = pl.ds(pl.multiple_of(place * 64, 64), 64)
            at = 0
            for own, swapped in zip(refs[:pairs], refs[pairs : 2 * pairs]):
                total = own[rows, :].astype(F32) + swapped[rows, :].astype(F32)
                outs[s][k, :, at : at + own.shape[1]] = total.astype(BF16)
                at += own.shape[1]


def prep_kernel(*refs):
    if len(refs) == 12:
        weight, cosine, sine, gains = refs[4:8]
        query, kv, raw, joined = refs[8:]
        for s in range(4):
            joined[s * 128 : (s + 1) * 128, :] = refs[s][:128, :]
    else:
        joined, weight, cosine, sine, gains, query, kv, raw = refs
    value = dot_nn(joined[...], weight[:, :512])
    kv[:, 128:] = value[:, 384:].astype(BF16)
    raw[...] = value[:, :384]
    for i in range(3):
        cols = slice(i * 128, (i + 1) * 128)
        head = raw[:, cols]
        scale = lax.rsqrt(jnp.mean(head * head, -1, keepdims=True) + EPSILON)
        head = head * scale * gains[i // 2 : i // 2 + 1, :]
        head = (head * cosine[...] + rolled(head, sine[...])).astype(BF16)
        if i == 2:
            kv[:, :128] = head
        else:
            query[:, cols] = head


def attend_kernel(meta, *refs):
    queries, kv_own, kv_other, begin, index, out_w = refs[:2], refs[2:4], refs[4:6], refs[6], refs[7], refs[8:10]
    keys, values, probs_low, probs_high, attended = refs[10:15]
    pieces, total = refs[15:19], refs[19]
    for t in range(8):
        rows = pl.ds(pl.multiple_of(meta[3 + t] * 128, 128), 128)
        at = slice((t % 4) * 128, (t % 4 + 1) * 128)
        for j in range(2):
            source = kv_own[j] if t < 4 else kv_other[1 - j]
            keys[j, rows, :] = source[at, :128]
            values[j, rows, :] = source[at, 128:]
    for half, (count, probs) in enumerate(((512, probs_low), (768, probs_high))):
        rows = pl.ds(pl.multiple_of(meta[half], 256), 256)
        first = 0 if half == 0 else pl.multiple_of(meta[2], 256)
        place = first + lax.broadcasted_iota(jnp.int32, (256, count), 1)
        allowed = (place >= begin[rows, :]) & (place <= index[rows, :])
        for j in range(2):
            key = keys[j, pl.ds(first, count), :]
            value = values[j, pl.ds(first, count), :]
            for i in range(2):
                n = j * 2 + i
                scores = dot_nt(queries[j][rows, i * 128 : (i + 1) * 128], key) * 128 ** (-0.5)
                scores = jnp.where(allowed, scores, NEG_LARGE)
                exponent = jnp.exp(scores - jnp.max(scores, -1, keepdims=True))
                prob = exponent * (1.0 / jnp.sum(exponent, -1, keepdims=True))
                prob = prob.astype(BF16)
                probs[n] = prob
                attended[rows, n * 128 : (n + 1) * 128] = dot_nn(prob, value).astype(BF16)
    total[...] = dot_nt(attended[:, :256], out_w[0][:, 512:])
    total[...] += dot_nt(attended[:, 256:], out_w[1][:, 512:])
    for s in range(4):
        pieces[s][...] = total[s * 128 : (s + 1) * 128, :].astype(pieces[s].dtype)


def attend_back_kernel(meta, *refs):
    grads, out_w, queries = refs[:4], refs[4:6], refs[6:8]
    keys, values, probs_low, probs_high = refs[8:12]
    grad_query, back_own, back_other = refs[12:15]
    grad_out, grad_keys, grad_values, joined = refs[15:]
    for s in range(4):
        joined[s * 128 : (s + 1) * 128, :] = grads[s][...]
    for j in range(2):
        grad_out[:, j * 256 : j * 256 + 256] = dot_nn(joined[...], out_w[j][:, 512:]).astype(BF16)
    grad_keys[...] = jnp.zeros_like(grad_keys)
    grad_values[...] = jnp.zeros_like(grad_values)
    for half, (count, probs) in enumerate(((512, probs_low), (768, probs_high))):
        rows = pl.ds(pl.multiple_of(meta[half], 256), 256)
        first = 0 if half == 0 else pl.multiple_of(meta[2], 256)
        span = pl.ds(first, count)
        for j in range(2):
            key = keys[j, span, :]
            value = values[j, span, :]
            for i in range(2):
                n = j * 2 + i
                cols = slice(n * 128, (n + 1) * 128)
                grad = grad_out[rows, cols]
                prob = probs[n]
                wide = prob.astype(F32)
                grad_prob = dot_nt(grad, value)
                inner = jnp.sum(wide * grad_prob, -1, keepdims=True)
                grad_scores = (wide * (grad_prob - inner)).astype(BF16)
                grad_query[rows, cols] = dot_nn(grad_scores, key) * 128 ** (-0.5)
                grad_keys[j, span, :] += dot_tn(
                    grad_scores, queries[j][rows, i * 128 : (i + 1) * 128]
                ) * 128 ** (-0.5)
                grad_values[j, span, :] += dot_tn(prob, grad)
    for t in range(8):
        rows = pl.ds(pl.multiple_of(meta[3 + t] * 128, 128), 128)
        target = back_own if t < 4 else back_other
        at = slice((t % 4) * 128, (t % 4 + 1) * 128)
        for j in range(2):
            jj = j if t < 4 else 1 - j
            target[at, jj * 128 : jj * 128 + 128] = grad_keys[j, rows, :].astype(target.dtype)
            target[at, 256 + jj * 128 : 384 + jj * 128] = grad_values[j, rows, :].astype(target.dtype)


def rolled(values, sine):
    return pltpu.roll(values, 64, 1) * sine


def tail_kernel(*refs):
    (grad_query, back_own, swapped, raw_own, raw_other, cosine, sine, gains, weight_own, weight_other) = refs[:10]
    normed, small, first_gain = refs[10:13]
    (low_own, low_other, mine, *pieces) = refs[13:19]
    partial = refs[19]
    sums = [0.0, 0.0]
    for j, (raw, low) in enumerate(((raw_own, low_own), (raw_other, low_other))):
        cols = slice(j * 128, (j + 1) * 128)
        grad_key = back_own[:, cols] + swapped[:, cols].astype(F32)
        cols = slice(256 + j * 128, 384 + j * 128)
        grad_value = back_own[:, cols] + swapped[:, cols].astype(F32)
        for i in range(3):
            cols = slice(i * 128, (i + 1) * 128)
            grad = grad_key if i == 2 else grad_query[:, (j * 2 + i) * 128 : (j * 2 + i + 1) * 128]
            grad = grad * cosine[...] - rolled(grad, sine[...])
            value = raw[:, cols]
            scale = lax.rsqrt(jnp.mean(value * value, -1, keepdims=True) + EPSILON)
            unit = value * scale
            sums[i // 2] = sums[i // 2] + jnp.sum(grad * unit, 0, keepdims=True)
            weighted = grad * gains[i // 2 : i // 2 + 1, :]
            back = scale * (weighted - unit * jnp.mean(unit * weighted, -1, keepdims=True))
            low[:, cols] = back.astype(BF16)
        low[:, 384:] = grad_value.astype(BF16)
    partial[...] = dot_nt(low_own[...], weight_own[:, :512])
    partial[...] += dot_nt(low_other[...], weight_other[:, :512])
    first = jnp.sum(partial[...] * normed[...].astype(F32), 0, keepdims=True)
    for s in range(4):
        rows = slice(s * 128, (s + 1) * 128)
        out = mine if s == 0 else pieces[s - 1]
        out[:128, :] = partial[rows, :].astype(out.dtype)
    gains_row = jnp.concatenate([sums[0], sums[1], jnp.zeros((1, 768), F32)], 1)
    block = jnp.concatenate(
        [first / first_gain[...], small[...], gains_row, jnp.zeros((13, 1024), F32)], 0
    ).astype(BF16)
    mine[128:, :] = block.astype(F32)
    for piece in pieces:
        piece[128:, :] = block


def pack_kernel(*refs):
    *shards, packed, done = refs
    copies, at = [], 0
    for n, ref in enumerate(shards):
        width = ref.shape[1]
        copies.append(pltpu.make_async_copy(ref, packed.at[:, at : at + width], done.at[n]))
        at += width
    for copy in copies:
        copy.start()
    for copy in copies:
        copy.wait()


def pick_with_kernel(where, own, swapped, extra, *outs):
    for s in range(4):
        for k in range(4):
            at = ((where[0] + s) % 4) * 4 + (where[1] ^ k)
            rows = pl.ds(pl.multiple_of(at * 64, 64), 64)
            total = own[rows, :].astype(F32) + swapped[rows, :].astype(F32)
            outs[s][k * 64 : (k + 1) * 64, :] = total.astype(BF16)
        outs[s][256:, :] = extra[...]


def vmem(n):
    return [pl.BlockSpec(memory_space=pltpu.VMEM)] * n


SMEM = pl.BlockSpec(memory_space=pltpu.SMEM)
PARAMS = pltpu.CompilerParams(vmem_limit_bytes=20 * 1024 * 1024)


def after(value, *others):
    return lax.optimization_barrier((value, *others))[0]


def gather_near(stage):
    return stage, ring(stage, "z", -1), ring(stage, "z", 1)


def gather_far(stage, ahead, behind):
    return [stage, ahead, (ring(ahead[:2], "z", -1), ring(behind[2:], "z", 1)), behind]


def place(parts, where):
    width = parts[0].shape[2]
    parts = jax.tree.leaves(parts)
    return pl.pallas_call(
        place_kernel,
        out_shape=jax.ShapeDtypeStruct((1024, width), BF16),
        in_specs=[SMEM] + vmem(len(parts)),
        out_specs=vmem(1)[0],
        compiler_params=PARAMS,
    )(where, *parts)


def pick(owns, swaps, where):
    width = sum(v.shape[1] for v in owns)
    return call(pick_kernel, [((4, 64, width), BF16)] * 4, where, *owns, *swaps, smem=1)


def pick_with(own, swapped, extra, where):
    shape = (272, own.shape[1])
    return call(pick_with_kernel, [(shape, BF16)] * 4, where, own, swapped, extra, smem=1)


def chain_first(parts):
    return ring(parts[2][:2], "z", 1), ring(parts[2][2:], "z", -1)


def chain_join(parts, up, down):
    add = lambda a, b: (a.astype(F32) + b.astype(F32)).astype(BF16)
    ahead = jnp.concatenate([add(parts[1][:2], up), parts[1][2:]])
    behind = jnp.concatenate([parts[3][:2], add(parts[3][2:], down)])
    return parts[0], ahead, behind


def chain_send(own, ahead, behind):
    return own, ring(ahead, "z", 1), ring(behind, "z", -1)


def chain_total(own, ahead, behind):
    return (own.astype(F32) + ahead.astype(F32) + behind.astype(F32)).astype(BF16)


def call(kernel, shapes, *args, smem=0, scratch=(), micros=1):
    return pl.pallas_call(
        kernel,
        out_shape=[jax.ShapeDtypeStruct(shape, kind) for shape, kind in shapes],
        in_specs=[SMEM] * smem + vmem(len(args) - smem),
        out_specs=vmem(len(shapes)),
        scratch_shapes=[pltpu.VMEM(shape, kind) for shape, kind in scratch],
        compiler_params=PARAMS,
        cost_estimate=pl.CostEstimate(
            flops=micros * 10**9, bytes_accessed=micros * 3 * 10**6, transcendentals=0
        ),
    )(*args)


def pack(*shards):
    return pl.pallas_call(
        pack_kernel,
        out_shape=jax.ShapeDtypeStruct((64, sum(v.shape[1] for v in shards)), BF16),
        in_specs=[pl.BlockSpec(memory_space=pl.ANY)] * len(shards),
        out_specs=vmem(1)[0],
        scratch_shapes=[pltpu.SemaphoreType.DMA((len(shards),))],
    )(*shards)


def norm_forward(values):
    scale = lax.rsqrt(jnp.mean(values * values, -1, keepdims=True) + EPSILON)
    return values * scale, scale


def norm_backward(unit, scale, gain, grad):
    weighted = grad * gain
    return scale * (weighted - unit * jnp.mean(unit * weighted, -1, keepdims=True))


def per_device(
    tokens,
    segment_ids,
    first_gain,
    query_gain,
    key_gain,
    query_weight,
    key_weight,
    value_weight,
    out_weight,
    second_gain,
    gate_weight,
    up_weight,
    down_weight,
    cotangent,
):
    z, h, c = lax.axis_index("z"), lax.axis_index("h"), lax.axis_index("c")
    y, l = lax.axis_index("y"), lax.axis_index("l")
    where = jnp.stack([z, h * 2 + y // 2]).astype(jnp.int32)
    y_own = jnp.where(y % 2 == c, y, 3 - y)
    both = remap(jnp.concatenate([tokens, cotangent], 0))
    tokens, cotangent = both[:128], both[128:]
    shards = pack(
        query_weight, key_weight, value_weight, out_weight.T, gate_weight, up_weight, down_weight.T
    )
    stages = [shard_out(shards, a, b) for a, b in SQUARE]
    attn_stage = jnp.stack([v[:, :768] for v in stages])
    mlp_stage = jnp.stack([v[:, 768:] for v in stages])
    attn_near = gather_near(attn_stage)
    attn_parts = gather_far(*attn_near)
    segment_ids = after(segment_ids, both)
    seg_row = jnp.where(y // 2 == c, segment_ids, core_swap(segment_ids))[0]

    blocks = [(y_own ^ (2 * i)) * 2 + (l ^ j) for i, j in SQUARE]
    other_blocks = [((3 - y_own) ^ (2 * i)) * 2 + (l ^ j) for i, j in SQUARE]
    index = jnp.concatenate([b * 128 + jnp.arange(128, dtype=jnp.int32) for b in blocks])
    seg = jnp.concatenate([lax.dynamic_slice_in_dim(seg_row, b * 128, 128, 0) for b in blocks])
    begin = jnp.zeros((512,), jnp.int32)
    for v in range(1, 4):
        begin = begin + jnp.where(seg == v, jnp.sum((seg_row < v).astype(jnp.int32)), 0)
    places = (index - begin).astype(F32)
    inverse = ROPE_BASE ** (-jnp.arange(0, 128, 2, dtype=F32) / 128)
    phases = places[:, None] * inverse[None, :]
    cosine, sine = jnp.cos(phases), jnp.sin(phases)
    cosine = jnp.concatenate([cosine, cosine], -1)
    sine = jnp.concatenate([-sine, sine], -1)
    upper = y_own // 2
    meta = jnp.stack([upper * 256, (1 - upper) * 256, (y_own % 2) * 256] + blocks + other_blocks)
    meta = meta.astype(jnp.int32)

    input_float = tokens.astype(F32)
    unit_one, scale_one = norm_forward(input_float)
    own_piece = (unit_one * first_gain).astype(BF16)
    own_piece = jnp.concatenate([own_piece, cotangent], 0)
    pieces = [across(own_piece, i, j) for i, j in SQUARE]
    begin, index = begin[:, None], index[:, None]
    attn_parts = lax.optimization_barrier((attn_parts, pieces, cosine, sine, begin, index))[0]
    attn_own = place(attn_parts, where)
    attn_other = core_swap(attn_own)
    attn_w = [attn_own, attn_other]
    pair_gains = jnp.stack([query_gain, key_gain])
    shapes = [((512, 256), BF16)] * 2 + [((512, 384), F32)]
    query_0, kv_0, raw_0, normed_one = call(
        prep_kernel, shapes + [((512, 1024), BF16)], *pieces, attn_own, cosine, sine, pair_gains, micros=4
    )
    query_1, kv_1, raw_1 = call(
        prep_kernel, shapes, normed_one, attn_other, cosine, sine, pair_gains, micros=3
    )
    block = (128, 1024)
    keys, vals, probs_low, probs_high, attended, *parts = call(
        attend_kernel,
        [((2, 1024, 128), BF16)] * 2
        + [((4, 256, 512), BF16), ((4, 256, 768), BF16), ((512, 512), BF16), (block, F32)]
        + [(block, BF16)] * 3,
        meta,
        query_0,
        query_1,
        kv_0,
        kv_1,
        core_swap(kv_0),
        core_swap(kv_1),
        begin,
        index,
        *attn_w,
        smem=1,
        scratch=[((512, 1024), F32)],
        micros=8,
    )
    mlp_near = gather_near(after(mlp_stage, attn_own))
    mlp_parts = gather_far(*lax.optimization_barrier((mlp_near, attended))[0])
    got = [across(parts[s], *SQUARE[s]) for s in (1, 2, 3)]
    mlp_parts, pieces = lax.optimization_barrier((mlp_parts, pieces, got))[:2]
    cot_all = jnp.concatenate([p[128:] for p in pieces], 0)
    mlp_own = place(mlp_parts, where)
    mlp_w = [mlp_own, core_swap(mlp_own)]
    gu_w = [w[:, :768] for w in mlp_w]
    down_w = [w[:, 768:] for w in mlp_w]
    hidden = input_float + parts[0]
    for value in got:
        hidden = hidden + value.astype(F32)

    unit_two, scale_two = norm_forward(hidden)
    normed_two = gather_tokens((unit_two * second_gain).astype(BF16))
    partial_two, acts, grad_gus = 0.0, [], []
    for j in range(2):
        gate_up = dot_nn(normed_two, gu_w[j])
        gate, up = gate_up[:, :384], gate_up[:, 384:]
        sig = jax.nn.sigmoid(gate)
        silu = gate * sig
        act = (silu * up).astype(BF16)
        grad_act = dot_nn(cot_all, down_w[j])
        grad_gate = (grad_act * up * (sig + silu * (1.0 - sig))).astype(BF16)
        grad_up = (grad_act * silu).astype(BF16)
        grad_gu = jnp.concatenate([grad_gate, grad_up], 1)
        partial_two = partial_two + dot_nt(grad_gu, gu_w[j])
        acts.append(act)
        grad_gus.append(grad_gu)
    low = partial_two.astype(BF16)
    got = [across(low[s * 128 : (s + 1) * 128], *SQUARE[s]) for s in (1, 2, 3)]
    grad_normed_two = partial_two[:128]
    for value in got:
        grad_normed_two = grad_normed_two + value.astype(F32)
    acts, grad_gus = lax.optimization_barrier((acts, grad_gus, got))[:2]
    mlp_grads = [
        jnp.concatenate([dot_tn(normed_two, grad_gus[j]), dot_tn(cot_all, acts[j])], 1).astype(BF16)
        for j in range(2)
    ]
    second_part = jnp.sum(partial_two * normed_two.astype(F32), 0) / second_gain

    grad_hidden = cotangent.astype(F32) + norm_backward(
        unit_two, scale_two, second_gain, grad_normed_two
    )
    grad_low = grad_hidden.astype(BF16)
    hidden_grads = [across(grad_low, i, j) for i, j in SQUARE]
    mlp_picked = pick(mlp_grads[:1], [core_swap(mlp_grads[1])], where)
    mlp_came = chain_first(mlp_picked)
    hidden_grads = lax.optimization_barrier((hidden_grads, mlp_picked))[0]
    grad_query, back_own, back_other = call(
        attend_back_kernel,
        [((512, 512), F32), ((512, 512), F32), ((512, 512), BF16)],
        meta,
        *hidden_grads,
        *attn_w,
        query_0,
        query_1,
        keys,
        vals,
        probs_low,
        probs_high,
        smem=1,
        scratch=[
            ((512, 512), BF16),
            ((2, 1024, 128), F32),
            ((2, 1024, 128), F32),
            ((512, 1024), BF16),
        ],
        micros=8,
    )
    *grad_raws, mine, piece_1, piece_2, piece_3 = call(
        tail_kernel,
        [((512, 512), BF16)] * 2 + [((144, 1024), F32)] + [((144, 1024), BF16)] * 3,
        grad_query,
        back_own,
        core_swap(back_other),
        raw_0,
        raw_1,
        cosine,
        sine,
        pair_gains,
        *attn_w,
        normed_one,
        second_part[None, :],
        first_gain[None, :],
        scratch=[((512, 1024), F32)],
        micros=9,
    )
    hidden_grad = jnp.concatenate(lax.optimization_barrier((hidden_grads, piece_1))[0], 0)
    attn_grads = [
        jnp.concatenate(
            [
                dot_tn(normed_one, after(grad_raws[j], piece_1)).astype(BF16),
                dot_tn(hidden_grad, attended[:, j * 256 : (j + 1) * 256]).astype(BF16),
            ],
            1,
        )
        for j in range(2)
    ]
    got = [across(p, *SQUARE[s + 1]) for s, p in enumerate((piece_1, piece_2, piece_3))]
    mlp_came = lax.optimization_barrier((mlp_came, piece_1))[0]
    mlp_far = chain_send(*chain_join(mlp_picked, *mlp_came))
    attn_swapped, mlp_far = lax.optimization_barrier((core_swap(attn_grads[1]), mlp_far))
    got = [p.astype(F32) for p in got]
    total = (mine + got[0]) + (got[1] + got[2])
    sums = total[128:131]
    sums = sums + core_swap(sums)
    sums = jnp.concatenate([sums[:, :768], jnp.pad(sums[:, 768:], ((0, 0), (0, 512)))], 0)
    sums = jnp.pad(sums, ((0, 10), (0, 0))).astype(BF16)
    parts = pick_with(attn_grads[0], attn_swapped, sums, where)
    got = [ring(parts[s], "z", s) for s in (1, 2, 3)]
    mlp_low = after(chain_total(*mlp_far), got[0])
    mlp_home = [shard_home(mlp_low[k], *SQUARE[k]) for k in range(4)]
    mlp_owned = sum(v.astype(F32) for v in mlp_home)
    acts = lax.optimization_barrier((acts, got[0]))[0]
    low = (dot_nt(acts[0], down_w[0]) + dot_nt(acts[1], down_w[1])).astype(BF16)
    branches = [across(low[s * 128 : (s + 1) * 128], *SQUARE[s]) for s in range(4)]
    got = lax.optimization_barrier((got, mlp_home))[0]
    grad_tokens = grad_hidden + norm_backward(unit_one, scale_one, first_gain, total[:128])
    layer_out = hidden
    for value in branches:
        layer_out = layer_out + value.astype(F32)
    results = jnp.concatenate([grad_tokens.astype(BF16), layer_out.astype(BF16)], 0)
    results = remap_back(results)
    got = [p.astype(F32) for p in got]
    low = ((parts[0].astype(F32) + got[1]) + (got[0] + got[2])).astype(BF16)
    attn_owned = [
        shard_home(
            jnp.concatenate([low[k * 64 : (k + 1) * 64], low[256:]], 0), *SQUARE[k]
        ).astype(F32)
        for k in range(4)
    ]
    attn_owned = (attn_owned[0] + attn_owned[1]) + (attn_owned[2] + attn_owned[3])
    sums = jnp.concatenate([attn_owned[64:67], attn_owned[67:70, :256]], 1)
    attn_owned, out_owned = attn_owned[:64, :512], attn_owned[:64, 512:]
    layer_out, grad_tokens = results[128:], results[:128]
    return (
        layer_out,
        grad_tokens,
        sums[0],
        sums[2, :128],
        sums[2, 128:256],
        attn_owned[:, :256],
        attn_owned[:, 256:384],
        attn_owned[:, 384:],
        out_owned.T,
        sums[1],
        mlp_owned[:, :384],
        mlp_owned[:, 384:768],
        mlp_owned[:, 768:].T,
    )


def solution(mesh):
    fine = Mesh(mesh.devices.reshape(4, 2, 2, 4, 2), ("z", "h", "c", "y", "l"))
    dp, tensor = ("z", "h", "c"), ("y", "l")
    rows, cols, trans = P(dp + tensor, None), P(dp, tensor), P(tensor, dp)
    in_specs = (
        rows, P(dp, None), P(), P(), P(), cols, cols, cols, trans, P(), cols, cols, trans, rows,
    )
    out_specs = (rows, rows, P(), P(), P(), cols, cols, cols, trans, P(), cols, cols, trans)
    return jax.shard_map(
        per_device, mesh=fine, in_specs=in_specs, out_specs=out_specs, check_vma=False
    )
```

```python
import jax
import jax.numpy as jnp
from jax import lax
from jax.experimental import pallas as pl
from jax.experimental.pallas import tpu as pltpu
from jax.sharding import Mesh
from jax.sharding import PartitionSpec as P

EPSILON = 1e-06
ROPE_BASE = 1000000.0
NEG_LARGE = -1e30
BF16 = jnp.bfloat16
F32 = jnp.float32
SQUARE = ((0, 0), (0, 1), (1, 0), (1, 1))


def place_of(y, pair):
    return y if y // 2 == pair else 3 - y


def remap_pairs():
    pairs = []
    for c in range(2):
        for y in range(4):
            for l in range(2):
                pairs.append(((c * 4 + y) * 2 + l, ((y % 2) * 4 + place_of(y, c)) * 2 + l))
    return pairs


def remap(value):
    return lax.ppermute(value, ("c", "y", "l"), remap_pairs())


def remap_back(value):
    return lax.ppermute(value, ("c", "y", "l"), [(b, a) for a, b in remap_pairs()])


def shard_pairs(a, b):
    pairs = []
    for h in range(2):
        for c in range(2):
            for y in range(4):
                for l in range(2):
                    source = ((h * 2 + c) * 4 + y) * 2 + l
                    pairs.append((source, (((h ^ a) * 2 + y % 2) * 4 + place_of(y, c ^ b)) * 2 + l))
    return pairs


def shard_out(value, a, b):
    return lax.ppermute(value, ("h", "c", "y", "l"), shard_pairs(a, b))


def shard_home(value, a, b):
    return lax.ppermute(value, ("h", "c", "y", "l"), [(t, s) for s, t in shard_pairs(a, b)])


def ring(value, axis, step):
    return lax.ppermute(value, (axis,), [(i, (i + step) % 4) for i in range(4)])


def core_swap(value):
    return lax.ppermute(value, ("c",), [(0, 1), (1, 0)])


def across(value, i, j):
    if (i, j) == (0, 0):
        return value
    pairs = [(y * 2 + l, (y ^ i) * 2 + (l ^ j)) for y in range(4) for l in range(2)]
    return lax.ppermute(value, ("y", "l"), pairs)


def dot_nn(a, b):
    return lax.dot_general(a, b, (((1,), (0,)), ((), ())), preferred_element_type=F32)


def dot_nt(a, b):
    return lax.dot_general(a, b, (((1,), (1,)), ((), ())), preferred_element_type=F32)


def dot_tn(a, b):
    return lax.dot_general(a, b, (((0,), (0,)), ((), ())), preferred_element_type=F32)


def gather_tokens(block):
    return jnp.concatenate([across(block, i, j) for i, j in SQUARE], 0)


def place_kernel(where, *refs):
    *parts, out = refs
    if len(parts) == 5:
        parts[2:4] = [(parts[2], parts[3])]
    for s in range(4):
        for k in range(4):
            at = ((where[0] + s) % 4) * 4 + (where[1] ^ k)
            block = parts[s][k // 2][k % 2] if isinstance(parts[s], tuple) else parts[s][k]
            out[pl.ds(pl.multiple_of(at * 64, 64), 64), :] = block


def pick_kernel(where, *refs):
    outs, pairs = refs[-4:], len(refs) // 2 - 2
    for s in range(4):
        for k in range(4):
            place = ((where[0] + s) % 4) * 4 + (where[1] ^ k)
            rows = pl.ds(pl.multiple_of(place * 64, 64), 64)
            at = 0
            for own, swapped in zip(refs[:pairs], refs[pairs : 2 * pairs]):
                total = own[rows, :].astype(F32) + swapped[rows, :].astype(F32)
                outs[s][k, :, at : at + own.shape[1]] = total.astype(BF16)
                at += own.shape[1]


def prep_kernel(*refs):
    if len(refs) == 12:
        weight, cosine, sine, gains = refs[4:8]
        query, kv, raw, joined = refs[8:]
        for s in range(4):
            joined[s * 128 : (s + 1) * 128, :] = refs[s][:128, :]
    else:
        joined, weight, cosine, sine, gains, query, kv, raw = refs
    value = dot_nn(joined[...], weight[:, :512])
    kv[:, 128:] = value[:, 384:].astype(BF16)
    raw[...] = value[:, :384]
    for i in range(3):
        cols = slice(i * 128, (i + 1) * 128)
        head = raw[:, cols]
        scale = lax.rsqrt(jnp.mean(head * head, -1, keepdims=True) + EPSILON)
        head = head * scale * gains[i // 2 : i // 2 + 1, :]
        head = (head * cosine[...] + rolled(head, sine[...])).astype(BF16)
        if i == 2:
            kv[:, :128] = head
        else:
            query[:, cols] = head


def attend_kernel(meta, *refs):
    queries, kv_own, kv_other, begin, index, out_w = refs[:2], refs[2:4], refs[4:6], refs[6], refs[7], refs[8:10]
    keys, values, probs_low, probs_high, attended = refs[10:15]
    pieces, total = refs[15:19], refs[19]
    for t in range(8):
        rows = pl.ds(pl.multiple_of(meta[3 + t] * 128, 128), 128)
        at = slice((t % 4) * 128, (t % 4 + 1) * 128)
        for j in range(2):
            source = kv_own[j] if t < 4 else kv_other[1 - j]
            keys[j, rows, :] = source[at, :128]
            values[j, rows, :] = source[at, 128:]
    for half, (count, probs) in enumerate(((512, probs_low), (768, probs_high))):
        rows = pl.ds(pl.multiple_of(meta[half], 256), 256)
        first = 0 if half == 0 else pl.multiple_of(meta[2], 256)
        place = first + lax.broadcasted_iota(jnp.int32, (256, count), 1)
        allowed = (place >= begin[rows, :]) & (place <= index[rows, :])
        for j in range(2):
            key = keys[j, pl.ds(first, count), :]
            value = values[j, pl.ds(first, count), :]
            for i in range(2):
                n = j * 2 + i
                scores = dot_nt(queries[j][rows, i * 128 : (i + 1) * 128], key) * 128 ** (-0.5)
                scores = jnp.where(allowed, scores, NEG_LARGE)
                exponent = jnp.exp(scores - jnp.max(scores, -1, keepdims=True))
                prob = exponent * (1.0 / jnp.sum(exponent, -1, keepdims=True))
                prob = prob.astype(BF16)
                probs[n] = prob
                attended[rows, n * 128 : (n + 1) * 128] = dot_nn(prob, value).astype(BF16)
    total[...] = dot_nt(attended[:, :256], out_w[0][:, 512:])
    total[...] += dot_nt(attended[:, 256:], out_w[1][:, 512:])
    for s in range(4):
        pieces[s][...] = total[s * 128 : (s + 1) * 128, :].astype(pieces[s].dtype)


def attend_back_kernel(meta, *refs):
    grads, out_w, queries = refs[:4], refs[4:6], refs[6:8]
    keys, values, probs_low, probs_high = refs[8:12]
    grad_query, back_own, back_other = refs[12:15]
    grad_out, grad_keys, grad_values, joined = refs[15:]
    for s in range(4):
        joined[s * 128 : (s + 1) * 128, :] = grads[s][...]
    for j in range(2):
        grad_out[:, j * 256 : j * 256 + 256] = dot_nn(joined[...], out_w[j][:, 512:]).astype(BF16)
    grad_keys[...] = jnp.zeros_like(grad_keys)
    grad_values[...] = jnp.zeros_like(grad_values)
    for half, (count, probs) in enumerate(((512, probs_low), (768, probs_high))):
        rows = pl.ds(pl.multiple_of(meta[half], 256), 256)
        first = 0 if half == 0 else pl.multiple_of(meta[2], 256)
        span = pl.ds(first, count)
        for j in range(2):
            key = keys[j, span, :]
            value = values[j, span, :]
            for i in range(2):
                n = j * 2 + i
                cols = slice(n * 128, (n + 1) * 128)
                grad = grad_out[rows, cols]
                prob = probs[n]
                wide = prob.astype(F32)
                grad_prob = dot_nt(grad, value)
                inner = jnp.sum(wide * grad_prob, -1, keepdims=True)
                grad_scores = (wide * (grad_prob - inner)).astype(BF16)
                grad_query[rows, cols] = dot_nn(grad_scores, key) * 128 ** (-0.5)
                grad_keys[j, span, :] += dot_tn(
                    grad_scores, queries[j][rows, i * 128 : (i + 1) * 128]
                ) * 128 ** (-0.5)
                grad_values[j, span, :] += dot_tn(prob, grad)
    for t in range(8):
        rows = pl.ds(pl.multiple_of(meta[3 + t] * 128, 128), 128)
        target = back_own if t < 4 else back_other
        at = slice((t % 4) * 128, (t % 4 + 1) * 128)
        for j in range(2):
            jj = j if t < 4 else 1 - j
            target[at, jj * 128 : jj * 128 + 128] = grad_keys[j, rows, :].astype(target.dtype)
            target[at, 256 + jj * 128 : 384 + jj * 128] = grad_values[j, rows, :].astype(target.dtype)


def rolled(values, sine):
    return pltpu.roll(values, 64, 1) * sine


def tail_kernel(*refs):
    (grad_query, back_own, swapped, raw_own, raw_other, cosine, sine, gains, weight_own, weight_other) = refs[:10]
    normed, small, first_gain = refs[10:13]
    (low_own, low_other, mine, *pieces) = refs[13:19]
    partial = refs[19]
    sums = [0.0, 0.0]
    for j, (raw, low) in enumerate(((raw_own, low_own), (raw_other, low_other))):
        cols = slice(j * 128, (j + 1) * 128)
        grad_key = back_own[:, cols] + swapped[:, cols].astype(F32)
        cols = slice(256 + j * 128, 384 + j * 128)
        grad_value = back_own[:, cols] + swapped[:, cols].astype(F32)
        for i in range(3):
            cols = slice(i * 128, (i + 1) * 128)
            grad = grad_key if i == 2 else grad_query[:, (j * 2 + i) * 128 : (j * 2 + i + 1) * 128]
            grad = grad * cosine[...] - rolled(grad, sine[...])
            value = raw[:, cols]
            scale = lax.rsqrt(jnp.mean(value * value, -1, keepdims=True) + EPSILON)
            unit = value * scale
            sums[i // 2] = sums[i // 2] + jnp.sum(grad * unit, 0, keepdims=True)
            weighted = grad * gains[i // 2 : i // 2 + 1, :]
            back = scale * (weighted - unit * jnp.mean(unit * weighted, -1, keepdims=True))
            low[:, cols] = back.astype(BF16)
        low[:, 384:] = grad_value.astype(BF16)
    partial[...] = dot_nt(low_own[...], weight_own[:, :512])
    partial[...] += dot_nt(low_other[...], weight_other[:, :512])
    first = jnp.sum(partial[...] * normed[...].astype(F32), 0, keepdims=True)
    for s in range(4):
        rows = slice(s * 128, (s + 1) * 128)
        out = mine if s == 0 else pieces[s - 1]
        out[:128, :] = partial[rows, :].astype(out.dtype)
    gains_row = jnp.concatenate([sums[0], sums[1], jnp.zeros((1, 768), F32)], 1)
    block = jnp.concatenate(
        [first / first_gain[...], small[...], gains_row, jnp.zeros((13, 1024), F32)], 0
    ).astype(BF16)
    mine[128:, :] = block.astype(F32)
    for piece in pieces:
        piece[128:, :] = block


def pack_kernel(*refs):
    *shards, packed, done = refs
    copies, at = [], 0
    for n, ref in enumerate(shards):
        width = ref.shape[1]
        copies.append(pltpu.make_async_copy(ref, packed.at[:, at : at + width], done.at[n]))
        at += width
    for copy in copies:
        copy.start()
    for copy in copies:
        copy.wait()


def pick_with_kernel(where, own, swapped, extra, *outs):
    for s in range(4):
        for k in range(4):
            at = ((where[0] + s) % 4) * 4 + (where[1] ^ k)
            rows = pl.ds(pl.multiple_of(at * 64, 64), 64)
            total = own[rows, :].astype(F32) + swapped[rows, :].astype(F32)
            outs[s][k * 64 : (k + 1) * 64, :] = total.astype(BF16)
        outs[s][256:, :] = extra[...]


def vmem(n):
    return [pl.BlockSpec(memory_space=pltpu.VMEM)] * n


SMEM = pl.BlockSpec(memory_space=pltpu.SMEM)
PARAMS = pltpu.CompilerParams(vmem_limit_bytes=20 * 1024 * 1024)


def after(value, *others):
    return lax.optimization_barrier((value, *others))[0]


def gather_near(stage):
    return stage, ring(stage, "z", -1), ring(stage, "z", 1)


def gather_far(stage, ahead, behind):
    return [stage, ahead, (ring(ahead[:2], "z", -1), ring(behind[2:], "z", 1)), behind]


def place(parts, where):
    width = parts[0].shape[2]
    parts = jax.tree.leaves(parts)
    return pl.pallas_call(
        place_kernel,
        out_shape=jax.ShapeDtypeStruct((1024, width), BF16),
        in_specs=[SMEM] + vmem(len(parts)),
        out_specs=vmem(1)[0],
        compiler_params=PARAMS,
    )(where, *parts)


def pick(owns, swaps, where):
    width = sum(v.shape[1] for v in owns)
    return call(pick_kernel, [((4, 64, width), BF16)] * 4, where, *owns, *swaps, smem=1)


def pick_with(own, swapped, extra, where):
    shape = (272, own.shape[1])
    return call(pick_with_kernel, [(shape, BF16)] * 4, where, own, swapped, extra, smem=1)


def chain_first(parts):
    return ring(parts[2][:2], "z", 1), ring(parts[2][2:], "z", -1)


def chain_join(parts, up, down):
    add = lambda a, b: (a.astype(F32) + b.astype(F32)).astype(BF16)
    ahead = jnp.concatenate([add(parts[1][:2], up), parts[1][2:]])
    behind = jnp.concatenate([parts[3][:2], add(parts[3][2:], down)])
    return parts[0], ahead, behind


def chain_send(own, ahead, behind):
    return own, ring(ahead, "z", 1), ring(behind, "z", -1)


def chain_total(own, ahead, behind):
    return (own.astype(F32) + ahead.astype(F32) + behind.astype(F32)).astype(BF16)


def call(kernel, shapes, *args, smem=0, scratch=(), micros=1):
    return pl.pallas_call(
        kernel,
        out_shape=[jax.ShapeDtypeStruct(shape, kind) for shape, kind in shapes],
        in_specs=[SMEM] * smem + vmem(len(args) - smem),
        out_specs=vmem(len(shapes)),
        scratch_shapes=[pltpu.VMEM(shape, kind) for shape, kind in scratch],
        compiler_params=PARAMS,
        cost_estimate=pl.CostEstimate(
            flops=micros * 10**9, bytes_accessed=micros * 3 * 10**6, transcendentals=0
        ),
    )(*args)


def pack(*shards):
    return pl.pallas_call(
        pack_kernel,
        out_shape=jax.ShapeDtypeStruct((64, sum(v.shape[1] for v in shards)), BF16),
        in_specs=[pl.BlockSpec(memory_space=pl.ANY)] * len(shards),
        out_specs=vmem(1)[0],
        scratch_shapes=[pltpu.SemaphoreType.DMA((len(shards),))],
    )(*shards)


def norm_forward(values):
    scale = lax.rsqrt(jnp.mean(values * values, -1, keepdims=True) + EPSILON)
    return values * scale, scale


def norm_backward(unit, scale, gain, grad):
    weighted = grad * gain
    return scale * (weighted - unit * jnp.mean(unit * weighted, -1, keepdims=True))


def per_device(
    tokens,
    segment_ids,
    first_gain,
    query_gain,
    key_gain,
    query_weight,
    key_weight,
    value_weight,
    out_weight,
    second_gain,
    gate_weight,
    up_weight,
    down_weight,
    cotangent,
):
    z, h, c = lax.axis_index("z"), lax.axis_index("h"), lax.axis_index("c")
    y, l = lax.axis_index("y"), lax.axis_index("l")
    where = jnp.stack([z, h * 2 + y // 2]).astype(jnp.int32)
    y_own = jnp.where(y % 2 == c, y, 3 - y)
    seg_rows = jnp.broadcast_to(segment_ids.astype(BF16), (16, 1024))
    both = remap(jnp.concatenate([tokens, cotangent, seg_rows], 0))
    tokens, cotangent, seg_row = both[:128], both[128:256], both[256:257].astype(F32)
    shards = pack(
        query_weight, key_weight, value_weight, out_weight.T, gate_weight, up_weight, down_weight.T
    )
    stages = [shard_out(shards, a, b) for a, b in SQUARE]
    attn_stage = jnp.stack([v[:, :768] for v in stages])
    mlp_stage = jnp.stack([v[:, 768:] for v in stages])
    attn_near = gather_near(attn_stage)
    attn_parts = gather_far(*attn_near)
    input_float = tokens.astype(F32)
    unit_one, scale_one = norm_forward(input_float)
    own_piece = (unit_one * first_gain).astype(BF16)
    own_piece = jnp.concatenate([own_piece, cotangent], 0)
    pieces = [across(own_piece, i, j) for i, j in SQUARE]

    blocks = [(y_own ^ (2 * i)) * 2 + (l ^ j) for i, j in SQUARE]
    other_blocks = [((3 - y_own) ^ (2 * i)) * 2 + (l ^ j) for i, j in SQUARE]
    row = lax.broadcasted_iota(jnp.int32, (512, 1), 0)
    block = jnp.where(row < 256, jnp.where(row < 128, blocks[0], blocks[1]), jnp.where(row < 384, blocks[2], blocks[3]))
    index = block * 128 + row % 128
    begin = jnp.zeros((512, 1), jnp.int32)
    for v in range(1, 4):
        bound = jnp.sum((seg_row < v).astype(jnp.int32))
        begin = jnp.maximum(begin, jnp.where(bound <= index, bound, 0))
    places = (index - begin).astype(F32)
    inverse = ROPE_BASE ** (-jnp.arange(0, 128, 2, dtype=F32) / 128)
    phases = places * inverse[None, :]
    cosine, sine = jnp.cos(phases), jnp.sin(phases)
    cosine = jnp.concatenate([cosine, cosine], -1)
    sine = jnp.concatenate([-sine, sine], -1)
    upper = y_own // 2
    meta = jnp.stack([upper * 256, (1 - upper) * 256, (y_own % 2) * 256] + blocks + other_blocks)
    meta = meta.astype(jnp.int32)

    attn_parts = lax.optimization_barrier((attn_parts, pieces, cosine, sine, begin, index))[0]
    attn_own = place(attn_parts, where)
    attn_other = core_swap(attn_own)
    attn_w = [attn_own, attn_other]
    pair_gains = jnp.stack([query_gain, key_gain])
    shapes = [((512, 256), BF16)] * 2 + [((512, 384), F32)]
    query_0, kv_0, raw_0, normed_one = call(
        prep_kernel, shapes + [((512, 1024), BF16)], *pieces, attn_own, cosine, sine, pair_gains, micros=4
    )
    query_1, kv_1, raw_1 = call(
        prep_kernel, shapes, normed_one, attn_other, cosine, sine, pair_gains, micros=3
    )
    block = (128, 1024)
    keys, vals, probs_low, probs_high, attended, *parts = call(
        attend_kernel,
        [((2, 1024, 128), BF16)] * 2
        + [((4, 256, 512), BF16), ((4, 256, 768), BF16), ((512, 512), BF16), (block, F32)]
        + [(block, BF16)] * 3,
        meta,
        query_0,
        query_1,
        kv_0,
        kv_1,
        core_swap(kv_0),
        core_swap(kv_1),
        begin,
        index,
        *attn_w,
        smem=1,
        scratch=[((512, 1024), F32)],
        micros=8,
    )
    mlp_near = gather_near(after(mlp_stage, attn_own))
    mlp_parts = gather_far(*lax.optimization_barrier((mlp_near, attended))[0])
    got = [across(parts[s], *SQUARE[s]) for s in (1, 2, 3)]
    mlp_parts, pieces = lax.optimization_barrier((mlp_parts, pieces, got))[:2]
    cot_all = jnp.concatenate([p[128:] for p in pieces], 0)
    mlp_own = place(mlp_parts, where)
    mlp_w = [mlp_own, core_swap(mlp_own)]
    gu_w = [w[:, :768] for w in mlp_w]
    down_w = [w[:, 768:] for w in mlp_w]
    hidden = input_float + parts[0]
    for value in got:
        hidden = hidden + value.astype(F32)

    unit_two, scale_two = norm_forward(hidden)
    normed_two = gather_tokens((unit_two * second_gain).astype(BF16))
    partial_two, acts, grad_gus = 0.0, [], []
    for j in range(2):
        gate_up = dot_nn(normed_two, gu_w[j])
        gate, up = gate_up[:, :384], gate_up[:, 384:]
        sig = jax.nn.sigmoid(gate)
        silu = gate * sig
        act = (silu * up).astype(BF16)
        grad_act = dot_nn(cot_all, down_w[j])
        grad_gate = (grad_act * up * (sig + silu * (1.0 - sig))).astype(BF16)
        grad_up = (grad_act * silu).astype(BF16)
        grad_gu = jnp.concatenate([grad_gate, grad_up], 1)
        partial_two = partial_two + dot_nt(grad_gu, gu_w[j])
        acts.append(act)
        grad_gus.append(grad_gu)
    low = partial_two.astype(BF16)
    got = [across(low[s * 128 : (s + 1) * 128], *SQUARE[s]) for s in (1, 2, 3)]
    grad_normed_two = partial_two[:128]
    for value in got:
        grad_normed_two = grad_normed_two + value.astype(F32)
    acts, grad_gus = lax.optimization_barrier((acts, grad_gus, got))[:2]
    mlp_grads = [
        jnp.concatenate([dot_tn(normed_two, grad_gus[j]), dot_tn(cot_all, acts[j])], 1).astype(BF16)
        for j in range(2)
    ]
    second_part = jnp.sum(partial_two * normed_two.astype(F32), 0) / second_gain

    grad_hidden = cotangent.astype(F32) + norm_backward(
        unit_two, scale_two, second_gain, grad_normed_two
    )
    grad_low = grad_hidden.astype(BF16)
    hidden_grads = [across(grad_low, i, j) for i, j in SQUARE]
    mlp_picked = pick(mlp_grads[:1], [core_swap(mlp_grads[1])], where)
    mlp_came = chain_first(mlp_picked)
    hidden_grads = lax.optimization_barrier((hidden_grads, mlp_picked))[0]
    grad_query, back_own, back_other = call(
        attend_back_kernel,
        [((512, 512), F32), ((512, 512), F32), ((512, 512), BF16)],
        meta,
        *hidden_grads,
        *attn_w,
        query_0,
        query_1,
        keys,
        vals,
        probs_low,
        probs_high,
        smem=1,
        scratch=[
            ((512, 512), BF16),
            ((2, 1024, 128), F32),
            ((2, 1024, 128), F32),
            ((512, 1024), BF16),
        ],
        micros=8,
    )
    low = (dot_nt(acts[0], down_w[0]) + dot_nt(acts[1], down_w[1])).astype(BF16)
    low = after(low, hidden_grads[1])
    branches = [across(low[s * 128 : (s + 1) * 128], *SQUARE[s]) for s in range(4)]
    back_own, branches = lax.optimization_barrier((back_own, branches))
    *grad_raws, mine, piece_1, piece_2, piece_3 = call(
        tail_kernel,
        [((512, 512), BF16)] * 2 + [((144, 1024), F32)] + [((144, 1024), BF16)] * 3,
        grad_query,
        back_own,
        core_swap(back_other),
        raw_0,
        raw_1,
        cosine,
        sine,
        pair_gains,
        *attn_w,
        normed_one,
        second_part[None, :],
        first_gain[None, :],
        scratch=[((512, 1024), F32)],
        micros=9,
    )
    hidden_grad = jnp.concatenate(lax.optimization_barrier((hidden_grads, piece_1))[0], 0)
    attn_grads = [
        jnp.concatenate(
            [
                dot_tn(normed_one, after(grad_raws[j], piece_1)).astype(BF16),
                dot_tn(hidden_grad, attended[:, j * 256 : (j + 1) * 256]).astype(BF16),
            ],
            1,
        )
        for j in range(2)
    ]
    got = [across(p, *SQUARE[s + 1]) for s, p in enumerate((piece_1, piece_2, piece_3))]
    mlp_came = lax.optimization_barrier((mlp_came, piece_1))[0]
    mlp_far = chain_send(*chain_join(mlp_picked, *mlp_came))
    attn_swapped = core_swap(attn_grads[1])
    got = [p.astype(F32) for p in got]
    total = (mine + got[0]) + (got[1] + got[2])
    sums = total[128:131]
    sums = sums + core_swap(sums)
    sums = jnp.concatenate([sums[:, :768], jnp.pad(sums[:, 768:], ((0, 0), (0, 512)))], 0)
    sums = jnp.pad(sums, ((0, 10), (0, 0))).astype(BF16)
    parts = pick_with(attn_grads[0], attn_swapped, sums, where)
    got = [ring(parts[s], "z", s) for s in (1, 2, 3)]
    near_done = got[0]
    mlp_low = chain_total(*lax.optimization_barrier((mlp_far, got[0]))[0])
    mlp_home = [shard_home(mlp_low[k], *SQUARE[k]) for k in range(4)]
    mlp_owned = sum(v.astype(F32) for v in mlp_home)
    got = lax.optimization_barrier((got, mlp_home))[0]
    grad_tokens = grad_hidden + norm_backward(unit_one, scale_one, first_gain, total[:128])
    layer_out = hidden
    for value in branches:
        layer_out = layer_out + value.astype(F32)
    results = jnp.concatenate([grad_tokens.astype(BF16), layer_out.astype(BF16)], 0)
    results = remap_back(after(results, near_done))
    got = [p.astype(F32) for p in got]
    low = ((parts[0].astype(F32) + got[1]) + (got[0] + got[2])).astype(BF16)
    attn_owned = [
        shard_home(
            jnp.concatenate([low[k * 64 : (k + 1) * 64], low[256:]], 0), *SQUARE[k]
        ).astype(F32)
        for k in range(4)
    ]
    attn_owned = (attn_owned[0] + attn_owned[1]) + (attn_owned[2] + attn_owned[3])
    sums = jnp.concatenate([attn_owned[64:67], attn_owned[67:70, :256]], 1)
    attn_owned, out_owned = attn_owned[:64, :512], attn_owned[:64, 512:]
    layer_out, grad_tokens = results[128:], results[:128]
    return (
        layer_out,
        grad_tokens,
        sums[0],
        sums[2, :128],
        sums[2, 128:256],
        attn_owned[:, :256],
        attn_owned[:, 256:384],
        attn_owned[:, 384:],
        out_owned.T,
        sums[1],
        mlp_owned[:, :384],
        mlp_owned[:, 384:768],
        mlp_owned[:, 768:].T,
    )


def solution(mesh):
    fine = Mesh(mesh.devices.reshape(4, 2, 2, 4, 2), ("z", "h", "c", "y", "l"))
    dp, tensor = ("z", "h", "c"), ("y", "l")
    rows, cols, trans = P(dp + tensor, None), P(dp, tensor), P(tensor, dp)
    in_specs = (
        rows, P(dp, None), P(), P(), P(), cols, cols, cols, trans, P(), cols, cols, trans, rows,
    )
    out_specs = (rows, rows, P(), P(), P(), cols, cols, cols, trans, P(), cols, cols, trans)
    return jax.shard_map(
        per_device, mesh=fine, in_specs=in_specs, out_specs=out_specs, check_vma=False
    )
```

```python
import jax
import jax.numpy as jnp
from jax import lax
from jax.experimental import pallas as pl
from jax.experimental.pallas import tpu as pltpu
from jax.sharding import Mesh
from jax.sharding import PartitionSpec as P

EPSILON = 1e-06
ROPE_BASE = 1000000.0
NEG_LARGE = -1e30
BF16 = jnp.bfloat16
F32 = jnp.float32
SQUARE = ((0, 0), (0, 1), (1, 0), (1, 1))


def place_of(y, pair):
    return y if y // 2 == pair else 3 - y


def remap_pairs():
    pairs = []
    for c in range(2):
        for y in range(4):
            for l in range(2):
                pairs.append(((c * 4 + y) * 2 + l, ((y % 2) * 4 + place_of(y, c)) * 2 + l))
    return pairs


def remap(value):
    return lax.ppermute(value, ("c", "y", "l"), remap_pairs())


def remap_back(value):
    return lax.ppermute(value, ("c", "y", "l"), [(b, a) for a, b in remap_pairs()])


def shard_pairs(a, b):
    pairs = []
    for h in range(2):
        for c in range(2):
            for y in range(4):
                for l in range(2):
                    source = ((h * 2 + c) * 4 + y) * 2 + l
                    pairs.append((source, (((h ^ a) * 2 + y % 2) * 4 + place_of(y, c ^ b)) * 2 + l))
    return pairs


def shard_out(value, a, b):
    return lax.ppermute(value, ("h", "c", "y", "l"), shard_pairs(a, b))


def shard_home(value, a, b):
    return lax.ppermute(value, ("h", "c", "y", "l"), [(t, s) for s, t in shard_pairs(a, b)])


def ring(value, axis, step):
    return lax.ppermute(value, (axis,), [(i, (i + step) % 4) for i in range(4)])


def core_swap(value):
    return lax.ppermute(value, ("c",), [(0, 1), (1, 0)])


def across(value, i, j):
    if (i, j) == (0, 0):
        return value
    pairs = [(y * 2 + l, (y ^ i) * 2 + (l ^ j)) for y in range(4) for l in range(2)]
    return lax.ppermute(value, ("y", "l"), pairs)


def dot_nn(a, b):
    return lax.dot_general(a, b, (((1,), (0,)), ((), ())), preferred_element_type=F32)


def dot_nt(a, b):
    return lax.dot_general(a, b, (((1,), (1,)), ((), ())), preferred_element_type=F32)


def dot_tn(a, b):
    return lax.dot_general(a, b, (((0,), (0,)), ((), ())), preferred_element_type=F32)


def gather_tokens(block):
    return jnp.concatenate([across(block, i, j) for i, j in SQUARE], 0)


def place_kernel(where, *refs):
    *parts, out = refs
    if len(parts) == 5:
        parts[2:4] = [(parts[2], parts[3])]
    for s in range(4):
        for k in range(4):
            at = ((where[0] + s) % 4) * 4 + (where[1] ^ k)
            block = parts[s][k // 2][k % 2] if isinstance(parts[s], tuple) else parts[s][k]
            out[pl.ds(pl.multiple_of(at * 64, 64), 64), :] = block


def pick_kernel(where, *refs):
    outs, pairs = refs[-4:], len(refs) // 2 - 2
    for s in range(4):
        for k in range(4):
            place = ((where[0] + s) % 4) * 4 + (where[1] ^ k)
            rows = pl.ds(pl.multiple_of(place * 64, 64), 64)
            at = 0
            for own, swapped in zip(refs[:pairs], refs[pairs : 2 * pairs]):
                total = own[rows, :].astype(F32) + swapped[rows, :].astype(F32)
                outs[s][k, :, at : at + own.shape[1]] = total.astype(BF16)
                at += own.shape[1]


def prep_kernel(*refs):
    if len(refs) == 12:
        weight, cosine, sine, gains = refs[4:8]
        query, kv, raw, joined = refs[8:]
        for s in range(4):
            joined[s * 128 : (s + 1) * 128, :] = refs[s][:128, :]
    else:
        joined, weight, cosine, sine, gains, query, kv, raw = refs
    value = dot_nn(joined[...], weight[:, :512])
    kv[:, 128:] = value[:, 384:].astype(BF16)
    raw[...] = value[:, :384]
    for i in range(3):
        cols = slice(i * 128, (i + 1) * 128)
        head = raw[:, cols]
        scale = lax.rsqrt(jnp.mean(head * head, -1, keepdims=True) + EPSILON)
        head = head * scale * gains[i // 2 : i // 2 + 1, :]
        head = (head * cosine[...] + rolled(head, sine[...])).astype(BF16)
        if i == 2:
            kv[:, :128] = head
        else:
            query[:, cols] = head


def attend_kernel(meta, *refs):
    queries, kv_own, kv_other, begin, index, out_w = refs[:2], refs[2:4], refs[4:6], refs[6], refs[7], refs[8:10]
    keys, values, probs_low, probs_high, attended = refs[10:15]
    pieces, total = refs[15:19], refs[19]
    for t in range(8):
        rows = pl.ds(pl.multiple_of(meta[3 + t] * 128, 128), 128)
        at = slice((t % 4) * 128, (t % 4 + 1) * 128)
        for j in range(2):
            source = kv_own[j] if t < 4 else kv_other[1 - j]
            keys[j, rows, :] = source[at, :128]
            values[j, rows, :] = source[at, 128:]
    for half, (count, probs) in enumerate(((512, probs_low), (768, probs_high))):
        rows = pl.ds(pl.multiple_of(meta[half], 256), 256)
        first = 0 if half == 0 else pl.multiple_of(meta[2], 256)
        place = first + lax.broadcasted_iota(jnp.int32, (256, count), 1)
        allowed = (place >= begin[rows, :]) & (place <= index[rows, :])
        for j in range(2):
            key = keys[j, pl.ds(first, count), :]
            value = values[j, pl.ds(first, count), :]
            for i in range(2):
                n = j * 2 + i
                scores = dot_nt(queries[j][rows, i * 128 : (i + 1) * 128], key) * 128 ** (-0.5)
                scores = jnp.where(allowed, scores, NEG_LARGE)
                exponent = jnp.exp(scores - jnp.max(scores, -1, keepdims=True))
                prob = exponent * (1.0 / jnp.sum(exponent, -1, keepdims=True))
                prob = prob.astype(BF16)
                probs[n] = prob
                attended[rows, n * 128 : (n + 1) * 128] = dot_nn(prob, value).astype(BF16)
    total[...] = dot_nt(attended[:, :256], out_w[0][:, 512:])
    total[...] += dot_nt(attended[:, 256:], out_w[1][:, 512:])
    for s in range(4):
        pieces[s][...] = total[s * 128 : (s + 1) * 128, :].astype(pieces[s].dtype)


def attend_back_kernel(meta, *refs):
    grads, out_w, queries = refs[:4], refs[4:6], refs[6:8]
    keys, values, probs_low, probs_high = refs[8:12]
    grad_query, back_own, back_other = refs[12:15]
    grad_out, grad_keys, grad_values, joined = refs[15:]
    for s in range(4):
        joined[s * 128 : (s + 1) * 128, :] = grads[s][...]
    for j in range(2):
        grad_out[:, j * 256 : j * 256 + 256] = dot_nn(joined[...], out_w[j][:, 512:]).astype(BF16)
    grad_keys[...] = jnp.zeros_like(grad_keys)
    grad_values[...] = jnp.zeros_like(grad_values)
    for half, (count, probs) in enumerate(((512, probs_low), (768, probs_high))):
        rows = pl.ds(pl.multiple_of(meta[half], 256), 256)
        first = 0 if half == 0 else pl.multiple_of(meta[2], 256)
        span = pl.ds(first, count)
        for j in range(2):
            key = keys[j, span, :]
            value = values[j, span, :]
            for i in range(2):
                n = j * 2 + i
                cols = slice(n * 128, (n + 1) * 128)
                grad = grad_out[rows, cols]
                prob = probs[n]
                wide = prob.astype(F32)
                grad_prob = dot_nt(grad, value)
                inner = jnp.sum(wide * grad_prob, -1, keepdims=True)
                grad_scores = (wide * (grad_prob - inner)).astype(BF16)
                grad_query[rows, cols] = dot_nn(grad_scores, key) * 128 ** (-0.5)
                grad_keys[j, span, :] += dot_tn(
                    grad_scores, queries[j][rows, i * 128 : (i + 1) * 128]
                ) * 128 ** (-0.5)
                grad_values[j, span, :] += dot_tn(prob, grad)
    for t in range(8):
        rows = pl.ds(pl.multiple_of(meta[3 + t] * 128, 128), 128)
        target = back_own if t < 4 else back_other
        at = slice((t % 4) * 128, (t % 4 + 1) * 128)
        for j in range(2):
            jj = j if t < 4 else 1 - j
            target[at, jj * 128 : jj * 128 + 128] = grad_keys[j, rows, :].astype(target.dtype)
            target[at, 256 + jj * 128 : 384 + jj * 128] = grad_values[j, rows, :].astype(target.dtype)


def rolled(values, sine):
    return pltpu.roll(values, 64, 1) * sine


def tail_kernel(*refs):
    (grad_query, back_own, swapped, raw_own, raw_other, cosine, sine, gains, weight_own, weight_other) = refs[:10]
    normed, small, first_gain = refs[10:13]
    (low_own, low_other, mine, *pieces) = refs[13:19]
    partial = refs[19]
    sums = [0.0, 0.0]
    for j, (raw, low) in enumerate(((raw_own, low_own), (raw_other, low_other))):
        cols = slice(j * 128, (j + 1) * 128)
        grad_key = back_own[:, cols] + swapped[:, cols].astype(F32)
        cols = slice(256 + j * 128, 384 + j * 128)
        grad_value = back_own[:, cols] + swapped[:, cols].astype(F32)
        for i in range(3):
            cols = slice(i * 128, (i + 1) * 128)
            grad = grad_key if i == 2 else grad_query[:, (j * 2 + i) * 128 : (j * 2 + i + 1) * 128]
            grad = grad * cosine[...] - rolled(grad, sine[...])
            value = raw[:, cols]
            scale = lax.rsqrt(jnp.mean(value * value, -1, keepdims=True) + EPSILON)
            unit = value * scale
            sums[i // 2] = sums[i // 2] + jnp.sum(grad * unit, 0, keepdims=True)
            weighted = grad * gains[i // 2 : i // 2 + 1, :]
            back = scale * (weighted - unit * jnp.mean(unit * weighted, -1, keepdims=True))
            low[:, cols] = back.astype(BF16)
        low[:, 384:] = grad_value.astype(BF16)
    partial[...] = dot_nt(low_own[...], weight_own[:, :512])
    partial[...] += dot_nt(low_other[...], weight_other[:, :512])
    first = jnp.sum(partial[...] * normed[...].astype(F32), 0, keepdims=True)
    for s in range(4):
        rows = slice(s * 128, (s + 1) * 128)
        out = mine if s == 0 else pieces[s - 1]
        out[:128, :] = partial[rows, :].astype(out.dtype)
    gains_row = jnp.concatenate([sums[0], sums[1], jnp.zeros((1, 768), F32)], 1)
    block = jnp.concatenate(
        [first / first_gain[...], small[...], gains_row, jnp.zeros((13, 1024), F32)], 0
    ).astype(BF16)
    mine[128:, :] = block.astype(F32)
    for piece in pieces:
        piece[128:, :] = block


def pack_kernel(*refs):
    *shards, packed, done = refs
    copies, at = [], 0
    for n, ref in enumerate(shards):
        width = ref.shape[1]
        copies.append(pltpu.make_async_copy(ref, packed.at[:, at : at + width], done.at[n]))
        at += width
    for copy in copies:
        copy.start()
    for copy in copies:
        copy.wait()


def pick_with_kernel(where, own, swapped, extra, *outs):
    for s in range(4):
        for k in range(4):
            at = ((where[0] + s) % 4) * 4 + (where[1] ^ k)
            rows = pl.ds(pl.multiple_of(at * 64, 64), 64)
            total = own[rows, :].astype(F32) + swapped[rows, :].astype(F32)
            outs[s][k * 64 : (k + 1) * 64, :] = total.astype(BF16)
        outs[s][256:, :] = extra[...]


def vmem(n):
    return [pl.BlockSpec(memory_space=pltpu.VMEM)] * n


SMEM = pl.BlockSpec(memory_space=pltpu.SMEM)
PARAMS = pltpu.CompilerParams(vmem_limit_bytes=20 * 1024 * 1024)


def after(value, *others):
    return lax.optimization_barrier((value, *others))[0]


def gather_near(stage):
    return stage, ring(stage, "z", -1), ring(stage, "z", 1)


def gather_far(stage, ahead, behind):
    return [stage, ahead, (ring(ahead[:2], "z", -1), ring(behind[2:], "z", 1)), behind]


def place(parts, where):
    width = parts[0].shape[2]
    parts = jax.tree.leaves(parts)
    return pl.pallas_call(
        place_kernel,
        out_shape=jax.ShapeDtypeStruct((1024, width), BF16),
        in_specs=[SMEM] + vmem(len(parts)),
        out_specs=vmem(1)[0],
        compiler_params=PARAMS,
    )(where, *parts)


def pick(owns, swaps, where):
    width = sum(v.shape[1] for v in owns)
    return call(pick_kernel, [((4, 64, width), BF16)] * 4, where, *owns, *swaps, smem=1)


def pick_with(own, swapped, extra, where):
    shape = (272, own.shape[1])
    return call(pick_with_kernel, [(shape, BF16)] * 4, where, own, swapped, extra, smem=1)


def chain_first(parts):
    return ring(parts[2][:2], "z", 1), ring(parts[2][2:], "z", -1)


def chain_join(parts, up, down):
    add = lambda a, b: (a.astype(F32) + b.astype(F32)).astype(BF16)
    ahead = jnp.concatenate([add(parts[1][:2], up), parts[1][2:]])
    behind = jnp.concatenate([parts[3][:2], add(parts[3][2:], down)])
    return parts[0], ahead, behind


def chain_send(own, ahead, behind):
    return own, ring(ahead, "z", 1), ring(behind, "z", -1)


def chain_total(own, ahead, behind):
    return (own.astype(F32) + ahead.astype(F32) + behind.astype(F32)).astype(BF16)


def call(kernel, shapes, *args, smem=0, scratch=()):
    return pl.pallas_call(
        kernel,
        out_shape=[jax.ShapeDtypeStruct(shape, kind) for shape, kind in shapes],
        in_specs=[SMEM] * smem + vmem(len(args) - smem),
        out_specs=vmem(len(shapes)),
        scratch_shapes=[pltpu.VMEM(shape, kind) for shape, kind in scratch],
        compiler_params=PARAMS,
        cost_estimate=pl.CostEstimate(
            flops=10**9, bytes_accessed=3 * 10**6, transcendentals=0
        ),
    )(*args)


def pack(*shards):
    return pl.pallas_call(
        pack_kernel,
        out_shape=jax.ShapeDtypeStruct((64, sum(v.shape[1] for v in shards)), BF16),
        in_specs=[pl.BlockSpec(memory_space=pl.ANY)] * len(shards),
        out_specs=vmem(1)[0],
        scratch_shapes=[pltpu.SemaphoreType.DMA((len(shards),))],
    )(*shards)


def norm_forward(values):
    scale = lax.rsqrt(jnp.mean(values * values, -1, keepdims=True) + EPSILON)
    return values * scale, scale


def norm_backward(unit, scale, gain, grad):
    weighted = grad * gain
    return scale * (weighted - unit * jnp.mean(unit * weighted, -1, keepdims=True))


def per_device(
    tokens,
    segment_ids,
    first_gain,
    query_gain,
    key_gain,
    query_weight,
    key_weight,
    value_weight,
    out_weight,
    second_gain,
    gate_weight,
    up_weight,
    down_weight,
    cotangent,
):
    z, h, c = lax.axis_index("z"), lax.axis_index("h"), lax.axis_index("c")
    y, l = lax.axis_index("y"), lax.axis_index("l")
    where = jnp.stack([z, h * 2 + y // 2]).astype(jnp.int32)
    y_own = jnp.where(y % 2 == c, y, 3 - y)
    seg_rows = jnp.broadcast_to(segment_ids.astype(BF16), (16, 1024))
    both = remap(jnp.concatenate([tokens, cotangent, seg_rows], 0))
    tokens, cotangent, seg_row = both[:128], both[128:256], both[256:257].astype(F32)
    shards = pack(
        query_weight, key_weight, value_weight, out_weight.T, gate_weight, up_weight, down_weight.T
    )
    stages = [shard_out(shards, a, b) for a, b in SQUARE]
    attn_stage = jnp.stack([v[:, :768] for v in stages])
    mlp_stage = jnp.stack([v[:, 768:] for v in stages])
    attn_near = gather_near(attn_stage)
    attn_parts = gather_far(*attn_near)
    input_float = tokens.astype(F32)
    unit_one, scale_one = norm_forward(input_float)
    own_piece = (unit_one * first_gain).astype(BF16)
    pieces = [across(own_piece, i, j) for i, j in SQUARE]

    blocks = [(y_own ^ (2 * i)) * 2 + (l ^ j) for i, j in SQUARE]
    other_blocks = [((3 - y_own) ^ (2 * i)) * 2 + (l ^ j) for i, j in SQUARE]
    row = lax.broadcasted_iota(jnp.int32, (512, 1), 0)
    block = jnp.where(row < 256, jnp.where(row < 128, blocks[0], blocks[1]), jnp.where(row < 384, blocks[2], blocks[3]))
    index = block * 128 + row % 128
    begin = jnp.zeros((512, 1), jnp.int32)
    for v in range(1, 4):
        bound = jnp.sum((seg_row < v).astype(jnp.int32))
        begin = jnp.maximum(begin, jnp.where(bound <= index, bound, 0))
    places = (index - begin).astype(F32)
    inverse = ROPE_BASE ** (-jnp.arange(0, 128, 2, dtype=F32) / 128)
    phases = places * inverse[None, :]
    cosine, sine = jnp.cos(phases), jnp.sin(phases)
    cosine = jnp.concatenate([cosine, cosine], -1)
    sine = jnp.concatenate([-sine, sine], -1)
    upper = y_own // 2
    meta = jnp.stack([upper * 256, (1 - upper) * 256, (y_own % 2) * 256] + blocks + other_blocks)
    meta = meta.astype(jnp.int32)

    attn_parts = lax.optimization_barrier((attn_parts, pieces, cosine, sine, begin, index))[0]
    attn_own = place(attn_parts, where)
    attn_other = core_swap(attn_own)
    attn_w = [attn_own, attn_other]
    pair_gains = jnp.stack([query_gain, key_gain])
    shapes = [((512, 256), BF16)] * 2 + [((512, 384), F32)]
    query_0, kv_0, raw_0, normed_one = call(
        prep_kernel, shapes + [((512, 1024), BF16)], *pieces, attn_own, cosine, sine, pair_gains
    )
    query_1, kv_1, raw_1 = call(
        prep_kernel, shapes, normed_one, attn_other, cosine, sine, pair_gains
    )
    block = (128, 1024)
    keys, vals, probs_low, probs_high, attended, *parts = call(
        attend_kernel,
        [((2, 1024, 128), BF16)] * 2
        + [((4, 256, 512), BF16), ((4, 256, 768), BF16), ((512, 512), BF16), (block, F32)]
        + [(block, BF16)] * 3,
        meta,
        query_0,
        query_1,
        kv_0,
        kv_1,
        core_swap(kv_0),
        core_swap(kv_1),
        begin,
        index,
        *attn_w,
        smem=1,
        scratch=[((512, 1024), F32)],
    )
    mlp_near = gather_near(after(mlp_stage, attn_own))
    cotangent = after(cotangent, *pieces)
    cot_pieces = [across(cotangent, i, j) for i, j in SQUARE]
    mlp_parts = gather_far(*lax.optimization_barrier((mlp_near, attended))[0])
    parts, cot_pieces = lax.optimization_barrier((parts, cot_pieces))
    got = [across(parts[s], *SQUARE[s]) for s in (1, 2, 3)]
    mlp_parts = lax.optimization_barrier((mlp_parts, got))[0]
    cot_all = jnp.concatenate(cot_pieces, 0)
    mlp_own = place(mlp_parts, where)
    mlp_w = [mlp_own, core_swap(mlp_own)]
    gu_w = [w[:, :768] for w in mlp_w]
    down_w = [w[:, 768:] for w in mlp_w]
    hidden = input_float + parts[0]
    for value in got:
        hidden = hidden + value.astype(F32)

    unit_two, scale_two = norm_forward(hidden)
    normed_two = gather_tokens((unit_two * second_gain).astype(BF16))
    partial_two, acts, grad_gus = 0.0, [], []
    for j in range(2):
        gate_up = dot_nn(normed_two, gu_w[j])
        gate, up = gate_up[:, :384], gate_up[:, 384:]
        sig = jax.nn.sigmoid(gate)
        silu = gate * sig
        act = (silu * up).astype(BF16)
        grad_act = dot_nn(cot_all, down_w[j])
        grad_gate = (grad_act * up * (sig + silu * (1.0 - sig))).astype(BF16)
        grad_up = (grad_act * silu).astype(BF16)
        grad_gu = jnp.concatenate([grad_gate, grad_up], 1)
        partial_two = partial_two + dot_nt(grad_gu, gu_w[j])
        acts.append(act)
        grad_gus.append(grad_gu)
    low = partial_two.astype(BF16)
    got = [across(low[s * 128 : (s + 1) * 128], *SQUARE[s]) for s in (1, 2, 3)]
    grad_normed_two = partial_two[:128]
    for value in got:
        grad_normed_two = grad_normed_two + value.astype(F32)
    acts, grad_gus = lax.optimization_barrier((acts, grad_gus, got))[:2]
    mlp_grads = [
        jnp.concatenate([dot_tn(normed_two, grad_gus[j]), dot_tn(cot_all, acts[j])], 1).astype(BF16)
        for j in range(2)
    ]
    second_part = jnp.sum(partial_two * normed_two.astype(F32), 0) / second_gain

    grad_hidden = cotangent.astype(F32) + norm_backward(
        unit_two, scale_two, second_gain, grad_normed_two
    )
    grad_low = grad_hidden.astype(BF16)
    hidden_grads = [across(grad_low, i, j) for i, j in SQUARE]
    mlp_picked = pick(mlp_grads[:1], [core_swap(mlp_grads[1])], where)
    mlp_came = chain_first(mlp_picked)
    hidden_grads = lax.optimization_barrier((hidden_grads, mlp_picked))[0]
    grad_query, back_own, back_other = call(
        attend_back_kernel,
        [((512, 512), F32), ((512, 512), F32), ((512, 512), BF16)],
        meta,
        *hidden_grads,
        *attn_w,
        query_0,
        query_1,
        keys,
        vals,
        probs_low,
        probs_high,
        smem=1,
        scratch=[
            ((512, 512), BF16),
            ((2, 1024, 128), F32),
            ((2, 1024, 128), F32),
            ((512, 1024), BF16),
        ],
    )
    low = (dot_nt(acts[0], down_w[0]) + dot_nt(acts[1], down_w[1])).astype(BF16)
    *grad_raws, mine, piece_1, piece_2, piece_3 = call(
        tail_kernel,
        [((512, 512), BF16)] * 2 + [((144, 1024), F32)] + [((144, 1024), BF16)] * 3,
        grad_query,
        back_own,
        core_swap(back_other),
        raw_0,
        raw_1,
        cosine,
        sine,
        pair_gains,
        *attn_w,
        normed_one,
        second_part[None, :],
        first_gain[None, :],
        scratch=[((512, 1024), F32)],
    )
    hidden_grad = jnp.concatenate(lax.optimization_barrier((hidden_grads, piece_1))[0], 0)
    attn_grads = [
        jnp.concatenate(
            [
                dot_tn(normed_one, after(grad_raws[j], piece_1)).astype(BF16),
                dot_tn(hidden_grad, attended[:, j * 256 : (j + 1) * 256]).astype(BF16),
            ],
            1,
        )
        for j in range(2)
    ]
    got = [across(p, *SQUARE[s + 1]) for s, p in enumerate((piece_1, piece_2, piece_3))]
    mlp_came = lax.optimization_barrier((mlp_came, piece_1))[0]
    mlp_far = chain_send(*chain_join(mlp_picked, *mlp_came))
    attn_swapped = core_swap(attn_grads[1])
    got = [p.astype(F32) for p in got]
    total = (mine + got[0]) + (got[1] + got[2])
    sums = total[128:131]
    sums = sums + core_swap(sums)
    sums = jnp.concatenate([sums[:, :768], jnp.pad(sums[:, 768:], ((0, 0), (0, 512)))], 0)
    sums = jnp.pad(sums, ((0, 10), (0, 0))).astype(BF16)
    parts = pick_with(attn_grads[0], attn_swapped, sums, where)
    got = [ring(parts[s], "z", s) for s in (1, 2, 3)]
    near_done = got[0]
    low = after(low, near_done)
    branches = [across(low[s * 128 : (s + 1) * 128], *SQUARE[s]) for s in range(4)]
    mlp_low = chain_total(*lax.optimization_barrier((mlp_far, got[0]))[0])
    mlp_home = [shard_home(mlp_low[k], *SQUARE[k]) for k in range(4)]
    mlp_owned = sum(v.astype(F32) for v in mlp_home)
    got = lax.optimization_barrier((got, mlp_home))[0]
    grad_tokens = grad_hidden + norm_backward(unit_one, scale_one, first_gain, total[:128])
    layer_out = hidden
    for value in branches:
        layer_out = layer_out + value.astype(F32)
    results = jnp.concatenate([grad_tokens.astype(BF16), layer_out.astype(BF16)], 0)
    results = remap_back(after(results, near_done))
    got = [p.astype(F32) for p in got]
    low = ((parts[0].astype(F32) + got[1]) + (got[0] + got[2])).astype(BF16)
    attn_owned = [
        shard_home(
            jnp.concatenate([low[k * 64 : (k + 1) * 64], low[256:]], 0), *SQUARE[k]
        ).astype(F32)
        for k in range(4)
    ]
    attn_owned = (attn_owned[0] + attn_owned[1]) + (attn_owned[2] + attn_owned[3])
    sums = jnp.concatenate([attn_owned[64:67], attn_owned[67:70, :256]], 1)
    attn_owned, out_owned = attn_owned[:64, :512], attn_owned[:64, 512:]
    layer_out, grad_tokens = results[128:], results[:128]
    return (
        layer_out,
        grad_tokens,
        sums[0],
        sums[2, :128],
        sums[2, 128:256],
        attn_owned[:, :256],
        attn_owned[:, 256:384],
        attn_owned[:, 384:],
        out_owned.T,
        sums[1],
        mlp_owned[:, :384],
        mlp_owned[:, 384:768],
        mlp_owned[:, 768:].T,
    )


def solution(mesh):
    fine = Mesh(mesh.devices.reshape(4, 2, 2, 4, 2), ("z", "h", "c", "y", "l"))
    dp, tensor = ("z", "h", "c"), ("y", "l")
    rows, cols, trans = P(dp + tensor, None), P(dp, tensor), P(tensor, dp)
    in_specs = (
        rows, P(dp, None), P(), P(), P(), cols, cols, cols, trans, P(), cols, cols, trans, rows,
    )
    out_specs = (rows, rows, P(), P(), P(), cols, cols, cols, trans, P(), cols, cols, trans)
    return jax.shard_map(
        per_device, mesh=fine, in_specs=in_specs, out_specs=out_specs, check_vma=False
    )
```

```python
import jax
import jax.numpy as jnp
from jax import lax
from jax.experimental import pallas as pl
from jax.experimental.pallas import tpu as pltpu
from jax.sharding import Mesh
from jax.sharding import PartitionSpec as P

EPSILON = 1e-06
ROPE_BASE = 1000000.0
NEG_LARGE = -1e30
BF16 = jnp.bfloat16
F32 = jnp.float32
SQUARE = ((0, 0), (0, 1), (1, 0), (1, 1))


def place_of(y, pair):
    return y if y // 2 == pair else 3 - y


def remap_pairs():
    pairs = []
    for c in range(2):
        for y in range(4):
            for l in range(2):
                pairs.append(((c * 4 + y) * 2 + l, ((y % 2) * 4 + place_of(y, c)) * 2 + l))
    return pairs


def remap(value):
    return lax.ppermute(value, ("c", "y", "l"), remap_pairs())


def remap_back(value):
    return lax.ppermute(value, ("c", "y", "l"), [(b, a) for a, b in remap_pairs()])


def shard_pairs(a, b):
    pairs = []
    for h in range(2):
        for c in range(2):
            for y in range(4):
                for l in range(2):
                    source = ((h * 2 + c) * 4 + y) * 2 + l
                    pairs.append((source, (((h ^ a) * 2 + y % 2) * 4 + place_of(y, c ^ b)) * 2 + l))
    return pairs


def shard_out(value, a, b):
    return lax.ppermute(value, ("h", "c", "y", "l"), shard_pairs(a, b))


def shard_home(value, a, b):
    return lax.ppermute(value, ("h", "c", "y", "l"), [(t, s) for s, t in shard_pairs(a, b)])


def ring(value, axis, step):
    return lax.ppermute(value, (axis,), [(i, (i + step) % 4) for i in range(4)])


def core_swap(value):
    return lax.ppermute(value, ("c",), [(0, 1), (1, 0)])


def across(value, i, j):
    if (i, j) == (0, 0):
        return value
    pairs = [(y * 2 + l, (y ^ i) * 2 + (l ^ j)) for y in range(4) for l in range(2)]
    return lax.ppermute(value, ("y", "l"), pairs)


def dot_nn(a, b):
    return lax.dot_general(a, b, (((1,), (0,)), ((), ())), preferred_element_type=F32)


def dot_nt(a, b):
    return lax.dot_general(a, b, (((1,), (1,)), ((), ())), preferred_element_type=F32)


def dot_tn(a, b):
    return lax.dot_general(a, b, (((0,), (0,)), ((), ())), preferred_element_type=F32)


def gather_tokens(block):
    return jnp.concatenate([across(block, i, j) for i, j in SQUARE], 0)


def place_kernel(where, *refs):
    *parts, out = refs
    if len(parts) == 5:
        parts[2:4] = [(parts[2], parts[3])]
    for s in range(4):
        for k in range(4):
            at = ((where[0] + s) % 4) * 4 + (where[1] ^ k)
            block = parts[s][k // 2][k % 2] if isinstance(parts[s], tuple) else parts[s][k]
            out[pl.ds(pl.multiple_of(at * 64, 64), 64), :] = block


def pick_kernel(where, *refs):
    outs, pairs = refs[-4:], len(refs) // 2 - 2
    for s in range(4):
        for k in range(4):
            place = ((where[0] + s) % 4) * 4 + (where[1] ^ k)
            rows = pl.ds(pl.multiple_of(place * 64, 64), 64)
            at = 0
            for own, swapped in zip(refs[:pairs], refs[pairs : 2 * pairs]):
                total = own[rows, :].astype(F32) + swapped[rows, :].astype(F32)
                outs[s][k, :, at : at + own.shape[1]] = total.astype(BF16)
                at += own.shape[1]


def prep_kernel(*refs):
    if len(refs) == 12:
        weight, cosine, sine, gains = refs[4:8]
        query, kv, raw, joined = refs[8:]
        for s in range(4):
            joined[s * 128 : (s + 1) * 128, :] = refs[s][:128, :]
    else:
        joined, weight, cosine, sine, gains, query, kv, raw = refs
    value = dot_nn(joined[...], weight[:, :512])
    kv[:, 128:] = value[:, 384:].astype(BF16)
    raw[...] = value[:, :384]
    for i in range(3):
        cols = slice(i * 128, (i + 1) * 128)
        head = raw[:, cols]
        scale = lax.rsqrt(jnp.mean(head * head, -1, keepdims=True) + EPSILON)
        head = head * scale * gains[i // 2 : i // 2 + 1, :]
        head = (head * cosine[...] + rolled(head, sine[...])).astype(BF16)
        if i == 2:
            kv[:, :128] = head
        else:
            query[:, cols] = head


def attend_kernel(meta, *refs):
    queries, kv_own, kv_other, begin, index, out_w = refs[:2], refs[2:4], refs[4:6], refs[6], refs[7], refs[8:10]
    keys, values, probs_low, probs_high, attended = refs[10:15]
    pieces, total = refs[15:19], refs[19]
    for t in range(8):
        rows = pl.ds(pl.multiple_of(meta[3 + t] * 128, 128), 128)
        at = slice((t % 4) * 128, (t % 4 + 1) * 128)
        for j in range(2):
            source = kv_own[j] if t < 4 else kv_other[1 - j]
            keys[j, rows, :] = source[at, :128]
            values[j, rows, :] = source[at, 128:]
    for half, (count, probs) in enumerate(((512, probs_low), (768, probs_high))):
        rows = pl.ds(pl.multiple_of(meta[half], 256), 256)
        first = 0 if half == 0 else pl.multiple_of(meta[2], 256)
        place = first + lax.broadcasted_iota(jnp.int32, (256, count), 1)
        allowed = (place >= begin[rows, :]) & (place <= index[rows, :])
        for j in range(2):
            key = keys[j, pl.ds(first, count), :]
            value = values[j, pl.ds(first, count), :]
            for i in range(2):
                n = j * 2 + i
                scores = dot_nt(queries[j][rows, i * 128 : (i + 1) * 128], key) * 128 ** (-0.5)
                scores = jnp.where(allowed, scores, NEG_LARGE)
                exponent = jnp.exp(scores - jnp.max(scores, -1, keepdims=True))
                prob = exponent * (1.0 / jnp.sum(exponent, -1, keepdims=True))
                prob = prob.astype(BF16)
                probs[n] = prob
                attended[rows, n * 128 : (n + 1) * 128] = dot_nn(prob, value).astype(BF16)
    total[...] = dot_nt(attended[:, :256], out_w[0][:, 512:])
    total[...] += dot_nt(attended[:, 256:], out_w[1][:, 512:])
    for s in range(4):
        pieces[s][...] = total[s * 128 : (s + 1) * 128, :].astype(pieces[s].dtype)


def attend_back_kernel(meta, *refs):
    grads, out_w, queries = refs[:4], refs[4:6], refs[6:8]
    keys, values, probs_low, probs_high = refs[8:12]
    grad_query, back_own, back_other = refs[12:15]
    grad_out, grad_keys, grad_values, joined = refs[15:]
    for s in range(4):
        joined[s * 128 : (s + 1) * 128, :] = grads[s][...]
    for j in range(2):
        grad_out[:, j * 256 : j * 256 + 256] = dot_nn(joined[...], out_w[j][:, 512:]).astype(BF16)
    grad_keys[...] = jnp.zeros_like(grad_keys)
    grad_values[...] = jnp.zeros_like(grad_values)
    for half, (count, probs) in enumerate(((512, probs_low), (768, probs_high))):
        rows = pl.ds(pl.multiple_of(meta[half], 256), 256)
        first = 0 if half == 0 else pl.multiple_of(meta[2], 256)
        span = pl.ds(first, count)
        for j in range(2):
            key = keys[j, span, :]
            value = values[j, span, :]
            for i in range(2):
                n = j * 2 + i
                cols = slice(n * 128, (n + 1) * 128)
                grad = grad_out[rows, cols]
                prob = probs[n]
                wide = prob.astype(F32)
                grad_prob = dot_nt(grad, value)
                inner = jnp.sum(wide * grad_prob, -1, keepdims=True)
                grad_scores = (wide * (grad_prob - inner)).astype(BF16)
                grad_query[rows, cols] = dot_nn(grad_scores, key) * 128 ** (-0.5)
                grad_keys[j, span, :] += dot_tn(
                    grad_scores, queries[j][rows, i * 128 : (i + 1) * 128]
                ) * 128 ** (-0.5)
                grad_values[j, span, :] += dot_tn(prob, grad)
    for t in range(8):
        rows = pl.ds(pl.multiple_of(meta[3 + t] * 128, 128), 128)
        target = back_own if t < 4 else back_other
        at = slice((t % 4) * 128, (t % 4 + 1) * 128)
        for j in range(2):
            jj = j if t < 4 else 1 - j
            target[at, jj * 128 : jj * 128 + 128] = grad_keys[j, rows, :].astype(target.dtype)
            target[at, 256 + jj * 128 : 384 + jj * 128] = grad_values[j, rows, :].astype(target.dtype)


def rolled(values, sine):
    return pltpu.roll(values, 64, 1) * sine


def tail_kernel(*refs):
    (grad_query, back_own, swapped, raw_own, raw_other, cosine, sine, gains, weight_own, weight_other) = refs[:10]
    normed, small, first_gain = refs[10:13]
    (low_own, low_other, mine, *pieces) = refs[13:19]
    partial = refs[19]
    sums = [0.0, 0.0]
    for j, (raw, low) in enumerate(((raw_own, low_own), (raw_other, low_other))):
        cols = slice(j * 128, (j + 1) * 128)
        grad_key = back_own[:, cols] + swapped[:, cols].astype(F32)
        cols = slice(256 + j * 128, 384 + j * 128)
        grad_value = back_own[:, cols] + swapped[:, cols].astype(F32)
        for i in range(3):
            cols = slice(i * 128, (i + 1) * 128)
            grad = grad_key if i == 2 else grad_query[:, (j * 2 + i) * 128 : (j * 2 + i + 1) * 128]
            grad = grad * cosine[...] - rolled(grad, sine[...])
            value = raw[:, cols]
            scale = lax.rsqrt(jnp.mean(value * value, -1, keepdims=True) + EPSILON)
            unit = value * scale
            sums[i // 2] = sums[i // 2] + jnp.sum(grad * unit, 0, keepdims=True)
            weighted = grad * gains[i // 2 : i // 2 + 1, :]
            back = scale * (weighted - unit * jnp.mean(unit * weighted, -1, keepdims=True))
            low[:, cols] = back.astype(BF16)
        low[:, 384:] = grad_value.astype(BF16)
    partial[...] = dot_nt(low_own[...], weight_own[:, :512])
    partial[...] += dot_nt(low_other[...], weight_other[:, :512])
    first = jnp.sum(partial[...] * normed[...].astype(F32), 0, keepdims=True)
    for s in range(4):
        rows = slice(s * 128, (s + 1) * 128)
        out = mine if s == 0 else pieces[s - 1]
        out[:128, :] = partial[rows, :].astype(out.dtype)
    gains_row = jnp.concatenate([sums[0], sums[1], jnp.zeros((1, 768), F32)], 1)
    block = jnp.concatenate(
        [first / first_gain[...], small[...], gains_row, jnp.zeros((13, 1024), F32)], 0
    ).astype(BF16)
    mine[128:, :] = block.astype(F32)
    for piece in pieces:
        piece[128:, :] = block


def pack_kernel(*refs):
    *shards, packed, done = refs
    copies, at = [], 0
    for n, ref in enumerate(shards):
        width = ref.shape[1]
        copies.append(pltpu.make_async_copy(ref, packed.at[:, at : at + width], done.at[n]))
        at += width
    for copy in copies:
        copy.start()
    for copy in copies:
        copy.wait()


def pick_with_kernel(where, own, swapped, extra, *outs):
    for s in range(4):
        for k in range(4):
            at = ((where[0] + s) % 4) * 4 + (where[1] ^ k)
            rows = pl.ds(pl.multiple_of(at * 64, 64), 64)
            total = own[rows, :].astype(F32) + swapped[rows, :].astype(F32)
            outs[s][k * 64 : (k + 1) * 64, :] = total.astype(BF16)
        outs[s][256:, :] = extra[...]


def vmem(n):
    return [pl.BlockSpec(memory_space=pltpu.VMEM)] * n


SMEM = pl.BlockSpec(memory_space=pltpu.SMEM)
PARAMS = pltpu.CompilerParams(vmem_limit_bytes=16 * 1024 * 1024)


def after(value, *others):
    return lax.optimization_barrier((value, *others))[0]


def gather_near(stage):
    return stage, ring(stage, "z", -1), ring(stage, "z", 1)


def gather_far(stage, ahead, behind):
    return [stage, ahead, (ring(ahead[:2], "z", -1), ring(behind[2:], "z", 1)), behind]


def place(parts, where):
    width = parts[0].shape[2]
    parts = jax.tree.leaves(parts)
    return pl.pallas_call(
        place_kernel,
        out_shape=jax.ShapeDtypeStruct((1024, width), BF16),
        in_specs=[SMEM] + vmem(len(parts)),
        out_specs=vmem(1)[0],
        compiler_params=PARAMS,
    )(where, *parts)


def pick(owns, swaps, where):
    width = sum(v.shape[1] for v in owns)
    return call(pick_kernel, [((4, 64, width), BF16)] * 4, where, *owns, *swaps, smem=1)


def pick_with(own, swapped, extra, where):
    shape = (272, own.shape[1])
    return call(pick_with_kernel, [(shape, BF16)] * 4, where, own, swapped, extra, smem=1)


def chain_first(parts):
    return ring(parts[2][:2], "z", 1), ring(parts[2][2:], "z", -1)


def chain_join(parts, up, down):
    add = lambda a, b: (a.astype(F32) + b.astype(F32)).astype(BF16)
    ahead = jnp.concatenate([add(parts[1][:2], up), parts[1][2:]])
    behind = jnp.concatenate([parts[3][:2], add(parts[3][2:], down)])
    return parts[0], ahead, behind


def chain_send(own, ahead, behind):
    return own, ring(ahead, "z", 1), ring(behind, "z", -1)


def chain_total(own, ahead, behind):
    return (own.astype(F32) + ahead.astype(F32) + behind.astype(F32)).astype(BF16)


def call(kernel, shapes, *args, smem=0, scratch=()):
    return pl.pallas_call(
        kernel,
        out_shape=[jax.ShapeDtypeStruct(shape, kind) for shape, kind in shapes],
        in_specs=[SMEM] * smem + vmem(len(args) - smem),
        out_specs=vmem(len(shapes)),
        scratch_shapes=[pltpu.VMEM(shape, kind) for shape, kind in scratch],
        compiler_params=PARAMS,
        cost_estimate=pl.CostEstimate(
            flops=10**9, bytes_accessed=3 * 10**6, transcendentals=0
        ),
    )(*args)


def pack(*shards):
    return pl.pallas_call(
        pack_kernel,
        out_shape=jax.ShapeDtypeStruct((64, sum(v.shape[1] for v in shards)), BF16),
        in_specs=[pl.BlockSpec(memory_space=pl.ANY)] * len(shards),
        out_specs=vmem(1)[0],
        scratch_shapes=[pltpu.SemaphoreType.DMA((len(shards),))],
        compiler_params=PARAMS,
    )(*shards)


def norm_forward(values):
    scale = lax.rsqrt(jnp.mean(values * values, -1, keepdims=True) + EPSILON)
    return values * scale, scale


def norm_backward(unit, scale, gain, grad):
    weighted = grad * gain
    return scale * (weighted - unit * jnp.mean(unit * weighted, -1, keepdims=True))


def per_device(
    tokens,
    segment_ids,
    first_gain,
    query_gain,
    key_gain,
    query_weight,
    key_weight,
    value_weight,
    out_weight,
    second_gain,
    gate_weight,
    up_weight,
    down_weight,
    cotangent,
):
    z, h, c = lax.axis_index("z"), lax.axis_index("h"), lax.axis_index("c")
    y, l = lax.axis_index("y"), lax.axis_index("l")
    where = jnp.stack([z, h * 2 + y // 2]).astype(jnp.int32)
    y_own = jnp.where(y % 2 == c, y, 3 - y)
    seg_rows = jnp.broadcast_to(segment_ids.astype(BF16), (16, 1024))
    both = remap(jnp.concatenate([tokens, cotangent, seg_rows], 0))
    tokens, cotangent, seg_row = both[:128], both[128:256], both[256:257].astype(F32)
    shards = pack(
        query_weight, key_weight, value_weight, out_weight.T, gate_weight, up_weight, down_weight.T
    )
    stages = [shard_out(shards, a, b) for a, b in SQUARE]
    attn_stage = jnp.stack([v[:, :768] for v in stages])
    mlp_stage = jnp.stack([v[:, 768:] for v in stages])
    attn_near = gather_near(attn_stage)
    attn_parts = gather_far(*attn_near)
    input_float = tokens.astype(F32)
    unit_one, scale_one = norm_forward(input_float)
    own_piece = (unit_one * first_gain).astype(BF16)
    pieces = [across(own_piece, i, j) for i, j in SQUARE]

    blocks = [(y_own ^ (2 * i)) * 2 + (l ^ j) for i, j in SQUARE]
    other_blocks = [((3 - y_own) ^ (2 * i)) * 2 + (l ^ j) for i, j in SQUARE]
    row = lax.broadcasted_iota(jnp.int32, (512, 1), 0)
    block = jnp.where(row < 256, jnp.where(row < 128, blocks[0], blocks[1]), jnp.where(row < 384, blocks[2], blocks[3]))
    index = block * 128 + row % 128
    begin = jnp.zeros((512, 1), jnp.int32)
    for v in range(1, 4):
        bound = jnp.sum((seg_row < v).astype(jnp.int32))
        begin = jnp.maximum(begin, jnp.where(bound <= index, bound, 0))
    places = (index - begin).astype(F32)
    inverse = ROPE_BASE ** (-jnp.arange(0, 128, 2, dtype=F32) / 128)
    phases = places * inverse[None, :]
    cosine, sine = jnp.cos(phases), jnp.sin(phases)
    cosine = jnp.concatenate([cosine, cosine], -1)
    sine = jnp.concatenate([-sine, sine], -1)
    upper = y_own // 2
    meta = jnp.stack([upper * 256, (1 - upper) * 256, (y_own % 2) * 256] + blocks + other_blocks)
    meta = meta.astype(jnp.int32)

    attn_parts, meta = lax.optimization_barrier(
        (attn_parts, meta, pieces, cosine, sine, begin, index)
    )[:2]
    attn_own = place(attn_parts, where)
    attn_other = core_swap(attn_own)
    attn_w = [attn_own, attn_other]
    pair_gains = jnp.stack([query_gain, key_gain])
    shapes = [((512, 256), BF16)] * 2 + [((512, 384), F32)]
    query_0, kv_0, raw_0, normed_one = call(
        prep_kernel, shapes + [((512, 1024), BF16)], *pieces, attn_own, cosine, sine, pair_gains
    )
    query_1, kv_1, raw_1 = call(
        prep_kernel, shapes, normed_one, attn_other, cosine, sine, pair_gains
    )
    block = (128, 1024)
    keys, vals, probs_low, probs_high, attended, *parts = call(
        attend_kernel,
        [((2, 1024, 128), BF16)] * 2
        + [((4, 256, 512), BF16), ((4, 256, 768), BF16), ((512, 512), BF16), (block, F32)]
        + [(block, BF16)] * 3,
        meta,
        query_0,
        query_1,
        kv_0,
        kv_1,
        core_swap(kv_0),
        core_swap(kv_1),
        begin,
        index,
        *attn_w,
        smem=1,
        scratch=[((512, 1024), F32)],
    )
    mlp_near = gather_near(after(mlp_stage, attn_own))
    cotangent = after(cotangent, *pieces)
    cot_pieces = [across(cotangent, i, j) for i, j in SQUARE]
    mlp_parts = gather_far(*lax.optimization_barrier((mlp_near, attended))[0])
    parts, cot_pieces = lax.optimization_barrier((parts, cot_pieces))
    got = [across(parts[s], *SQUARE[s]) for s in (1, 2, 3)]
    mlp_parts = lax.optimization_barrier((mlp_parts, got))[0]
    cot_all = jnp.concatenate(cot_pieces, 0)
    mlp_own = place(mlp_parts, where)
    mlp_w = [mlp_own, core_swap(mlp_own)]
    gu_w = [w[:, :768] for w in mlp_w]
    down_w = [w[:, 768:] for w in mlp_w]
    hidden = input_float + parts[0]
    for value in got:
        hidden = hidden + value.astype(F32)

    unit_two, scale_two = norm_forward(hidden)
    normed_two = gather_tokens((unit_two * second_gain).astype(BF16))
    partial_two, acts, grad_gus = 0.0, [], []
    for j in range(2):
        gate_up = dot_nn(normed_two, gu_w[j])
        gate, up = gate_up[:, :384], gate_up[:, 384:]
        sig = jax.nn.sigmoid(gate)
        silu = gate * sig
        act = (silu * up).astype(BF16)
        grad_act = dot_nn(cot_all, down_w[j])
        grad_gate = (grad_act * up * (sig + silu * (1.0 - sig))).astype(BF16)
        grad_up = (grad_act * silu).astype(BF16)
        grad_gu = jnp.concatenate([grad_gate, grad_up], 1)
        partial_two = partial_two + dot_nt(grad_gu, gu_w[j])
        acts.append(act)
        grad_gus.append(grad_gu)
    low = partial_two.astype(BF16)
    got = [across(low[s * 128 : (s + 1) * 128], *SQUARE[s]) for s in (1, 2, 3)]
    grad_normed_two = partial_two[:128]
    for value in got:
        grad_normed_two = grad_normed_two + value.astype(F32)
    acts, grad_gus = lax.optimization_barrier((acts, grad_gus, got))[:2]
    mlp_grads = [
        jnp.concatenate([dot_tn(normed_two, grad_gus[j]), dot_tn(cot_all, acts[j])], 1).astype(BF16)
        for j in range(2)
    ]
    second_part = jnp.sum(partial_two * normed_two.astype(F32), 0) / second_gain

    grad_hidden = cotangent.astype(F32) + norm_backward(
        unit_two, scale_two, second_gain, grad_normed_two
    )
    grad_low = grad_hidden.astype(BF16)
    hidden_grads = [across(grad_low, i, j) for i, j in SQUARE]
    mlp_picked = pick(mlp_grads[:1], [core_swap(mlp_grads[1])], where)
    mlp_came = chain_first(mlp_picked)
    hidden_grads = lax.optimization_barrier((hidden_grads, mlp_picked))[0]
    grad_query, back_own, back_other = call(
        attend_back_kernel,
        [((512, 512), F32), ((512, 512), F32), ((512, 512), BF16)],
        meta,
        *hidden_grads,
        *attn_w,
        query_0,
        query_1,
        keys,
        vals,
        probs_low,
        probs_high,
        smem=1,
        scratch=[
            ((512, 512), BF16),
            ((2, 1024, 128), F32),
            ((2, 1024, 128), F32),
            ((512, 1024), BF16),
        ],
    )
    low = (dot_nt(acts[0], down_w[0]) + dot_nt(acts[1], down_w[1])).astype(BF16)
    *grad_raws, mine, piece_1, piece_2, piece_3 = call(
        tail_kernel,
        [((512, 512), BF16)] * 2 + [((144, 1024), F32)] + [((144, 1024), BF16)] * 3,
        grad_query,
        back_own,
        core_swap(back_other),
        raw_0,
        raw_1,
        cosine,
        sine,
        pair_gains,
        *attn_w,
        normed_one,
        second_part[None, :],
        first_gain[None, :],
        scratch=[((512, 1024), F32)],
    )
    hidden_grad = jnp.concatenate(lax.optimization_barrier((hidden_grads, piece_1))[0], 0)
    attn_grads = [
        jnp.concatenate(
            [
                dot_tn(normed_one, after(grad_raws[j], piece_1)).astype(BF16),
                dot_tn(hidden_grad, attended[:, j * 256 : (j + 1) * 256]).astype(BF16),
            ],
            1,
        )
        for j in range(2)
    ]
    got = [across(p, *SQUARE[s + 1]) for s, p in enumerate((piece_1, piece_2, piece_3))]
    mlp_came = lax.optimization_barrier((mlp_came, piece_1))[0]
    mlp_far = chain_send(*chain_join(mlp_picked, *mlp_came))
    attn_swapped = core_swap(attn_grads[1])
    got = [p.astype(F32) for p in got]
    total = (mine + got[0]) + (got[1] + got[2])
    sums = total[128:131]
    sums = sums + core_swap(sums)
    sums = jnp.concatenate([sums[:, :768], jnp.pad(sums[:, 768:], ((0, 0), (0, 512)))], 0)
    sums = jnp.pad(sums, ((0, 10), (0, 0))).astype(BF16)
    parts = pick_with(attn_grads[0], attn_swapped, sums, where)
    got = [ring(parts[s], "z", s) for s in (1, 2, 3)]
    near_done = got[0]
    low = after(low, near_done)
    branches = [across(low[s * 128 : (s + 1) * 128], *SQUARE[s]) for s in range(4)]
    mlp_low = chain_total(*lax.optimization_barrier((mlp_far, got[0]))[0])
    mlp_home = [shard_home(mlp_low[k], *SQUARE[k]) for k in range(4)]
    mlp_owned = sum(v.astype(F32) for v in mlp_home)
    got = lax.optimization_barrier((got, mlp_home))[0]
    grad_tokens = grad_hidden + norm_backward(unit_one, scale_one, first_gain, total[:128])
    layer_out = hidden
    for value in branches:
        layer_out = layer_out + value.astype(F32)
    results = jnp.concatenate([grad_tokens.astype(BF16), layer_out.astype(BF16)], 0)
    results = remap_back(after(results, near_done))
    got = [p.astype(F32) for p in got]
    low = ((parts[0].astype(F32) + got[1]) + (got[0] + got[2])).astype(BF16)
    attn_owned = [
        shard_home(
            jnp.concatenate([low[k * 64 : (k + 1) * 64], low[256:]], 0), *SQUARE[k]
        ).astype(F32)
        for k in range(4)
    ]
    attn_owned = (attn_owned[0] + attn_owned[1]) + (attn_owned[2] + attn_owned[3])
    sums = jnp.concatenate([attn_owned[64:67], attn_owned[67:70, :256]], 1)
    attn_owned, out_owned = attn_owned[:64, :512], attn_owned[:64, 512:]
    layer_out, grad_tokens = results[128:], results[:128]
    return (
        layer_out,
        grad_tokens,
        sums[0],
        sums[2, :128],
        sums[2, 128:256],
        attn_owned[:, :256],
        attn_owned[:, 256:384],
        attn_owned[:, 384:],
        out_owned.T,
        sums[1],
        mlp_owned[:, :384],
        mlp_owned[:, 384:768],
        mlp_owned[:, 768:].T,
    )


def solution(mesh):
    fine = Mesh(mesh.devices.reshape(4, 2, 2, 4, 2), ("z", "h", "c", "y", "l"))
    dp, tensor = ("z", "h", "c"), ("y", "l")
    rows, cols, trans = P(dp + tensor, None), P(dp, tensor), P(tensor, dp)
    in_specs = (
        rows, P(dp, None), P(), P(), P(), cols, cols, cols, trans, P(), cols, cols, trans, rows,
    )
    out_specs = (rows, rows, P(), P(), P(), cols, cols, cols, trans, P(), cols, cols, trans)
    return jax.shard_map(
        per_device, mesh=fine, in_specs=in_specs, out_specs=out_specs, check_vma=False
    )
```
